128 devices in a mesh: dp: 32 (over z, x, core), db: 4 (over y).
Axes of the slice: x: 4, y: 4, z: 4, core: 2. Of those that a mesh axis runs over, the one named last changes fastest.
Arguments:
- queries: bfloat16 [18432, 4096], P('dp', 'db'), may hold values from -100 to 100
- cotangent: bfloat16 [18432, 4096], P('dp', 'db'), may hold values from -6 to 6
- db_states: bfloat16 [1024, 128, 896], P('dp', 'db'), may hold values from -6 to 6
- key_weight: bfloat16 [896, 4096], P(None, 'db'), may hold values from -0.1875 to 0.1875
- value_weight: bfloat16 [896, 4096], P(None, 'db'), may hold values from -0.1875 to 0.1875
- conv_kernel: float32 [3, 896], replicated, may hold values from -2.5 to 2.5
- nbr_owner: int32 [288, 2], P('dp'), may hold values from 0 to 31, all different within a row; in each aligned block of 9 rows (0 to 8, 9 to 17, ...) at most 2 rows name the same one
- nbr_row: int32 [288, 2], P('dp'), may hold values from 0 to 31
Outputs:
- attended: bfloat16 [18432, 4096], P('dp', 'db')
- grad_queries: bfloat16 [18432, 4096], P('dp', 'db')
- grad_states: float32 [1024, 128, 896], P('dp', 'db')
- grad_key_weight: float32 [896, 4096], P(None, 'db')
- grad_value_weight: float32 [896, 4096], P(None, 'db')
- grad_kernel: float32 [3, 896], replicated
The draws below stay inside these ranges and needn't reach their ends.
Inputs may be any that keep to these rules, and one draw needn't show every extreme that they name: `nbr_owner`: in the 9 spans of one index of dp no owner is named more than 2 times, a bound that some block reaches; the 2 neighbours of a span have different owners.
All inputs are finite; a program needn't handle non-finite values.
Results may differ from the reference program's by a relative error of at most 0.035.
The reference program's roundings to bfloat16 on the way count: a program that leaves them out, or rounds other values in their place, can miss the bound.
Values may be sent and summed in bfloat16 or wider, within the bound.
A program may use at most 192 MiB of HBM per device.

```python
import math
import jax
import jax.numpy as jnp
import numpy as np
from jax import lax

D = 4096
HEADS = 32
HD = 128
ENC = 896
SPAN = 64
NBR = 2
NLEN = 128
KW = 3
CH_DEV = 9
BLK_DEV = 32
CAP = 2
SPANS = 288
TOKENS = 18432
BLOCKS = 1024
N_DP = 32


def draw_queries(key, part):
    key_main = jax.random.fold_in(key, 0)
    values = jnp.clip(jax.random.normal(key_main, (TOKENS, D), jnp.float32), -6.0, 6.0)
    return values.astype(jnp.bfloat16)


def plant(drawn, key, smallest, largest):
    extent = drawn.shape
    place = [jax.random.randint(jax.random.fold_in(key, axis), (), 0, extent[axis]) for axis in range(len(extent))]
    drawn = drawn.at[tuple(place)].set(smallest)
    longest = extent.index(max(extent))
    place[longest] = (place[longest] + 1) % extent[longest]
    return drawn.at[tuple(place)].set(largest)


def levels(stream_key, extent, shards, smallest, top_value):
    def one(axis_at, shards_of):
        heights = jax.random.uniform(jax.random.fold_in(jax.random.fold_in(stream_key, 6), axis_at), (shards_of,), jnp.float32, smallest / len(shards), top_value / len(shards))
        return jnp.repeat(jnp.exp(heights), extent[axis_at] // shards_of).reshape((-1,) + (1,) * (len(extent) - axis_at - 1))

    factor_of = one(*shards[0])
    for cut in shards[1:]:
        factor_of = factor_of * one(*cut)
    return factor_of


def assign_block(own_key, own, number, rows, count, top, bound, slope):
    sequence = jax.random.permutation(own_key, count)
    heavy_load, common = load_shares(count, rows * top, bound, slope, True), load_shares(count, rows * top, bound, slope, False)
    places = jnp.arange(count)

    def named(sizes, rotation):
        used = int((sizes > 0).sum())
        fixed = max(1, used // 4)
        shifted = fixed + (places - fixed + rotation * (used - fixed)) % max(1, count - fixed)
        return jnp.zeros((count,), jnp.int32).at[sequence[jnp.where(places < fixed, places, shifted)]].set(jnp.asarray(sizes, jnp.int32))

    sizes = jnp.where(number % 4 == 0, named(heavy_load, number // 4), named(common, number - number // 4 - 1))
    mixed = jax.random.permutation(jax.random.fold_in(own, 3), count)
    donor, sink = mixed[0:count // 2 * 2:2], mixed[1:count // 2 * 2:2]
    margin = jnp.minimum(sizes[donor] - 1, bound - sizes[sink]) // 2
    margin = jnp.where((donor == sequence[0]) | (sink == sequence[0]) | (sizes[sink] == 0), 0, jnp.maximum(margin, 0))
    shifted = jax.random.randint(jax.random.fold_in(own, 4), (count // 2,), 0, 1 << 20) % (margin + 1)
    sizes = sizes.at[donor].add(-shifted).at[sink].add(shifted)
    items = jnp.searchsorted(jnp.cumsum(sizes), jnp.arange(rows * top), side="right").astype(jnp.int32)
    table = items.reshape(top, rows).T
    table = table[jax.random.permutation(jax.random.fold_in(own, 1), rows)]
    rotation = jax.random.randint(jax.random.fold_in(own, 2), (rows, 1), 0, top)
    return jnp.take_along_axis(table, (jnp.arange(top)[None, :] + rotation) % top, axis=1)


def load_shares(amount, total, reach, skew, full):
    loads = [(1 << 20) // math.isqrt(grade ** skew) + 1 for grade in range(1, amount + 1)]
    largest = reach if full else min(reach, max(-(-total // amount), total * loads[0] // sum(loads)))
    least = 1 if total - largest >= amount - 1 else 0
    counts, rest = [largest] + [least] * (amount - 1), total - largest - least * (amount - 1)
    while rest > 0:
        candidates = [i for i in range(1, amount) if counts[i] < largest] or [i for i in range(1, amount) if counts[i] < reach]
        whole, remaining = sum([loads[i] for i in candidates]), rest
        for i in candidates:
            extra = min(reach - counts[i], max(1, remaining * loads[i] // whole), rest)
            counts[i] = counts[i] + extra
            rest = rest - extra
    return np.array(counts)


def scatter_about(key, extent, scale, limit, shards=(), kind=jnp.bfloat16):
    result = scale * jax.random.normal(key, extent, jnp.float32)
    if shards:
        result = result * levels(key, extent, shards, -0.22, 0.18)
    return jnp.clip(result, -limit, limit).astype(kind)


def setup_inputs(seed: int = 0) -> dict:
    arg_keys = jax.random.split(jax.random.key(seed), 9)
    queries = draw_queries(jax.random.fold_in(arg_keys[8], 71), 0)
    cotangent = scatter_about(arg_keys[1], (TOKENS, D), 1.0, 6.0, ((0, 32), (1, 4)))
    db_states = scatter_about(arg_keys[2], (BLOCKS, NLEN, ENC), 1.0, 6.0, ((0, 32), (1, 4)))
    key_weight = scatter_about(arg_keys[3], (ENC, D), ENC ** -0.5, 0.1875, ((1, 4),))
    value_weight = scatter_about(arg_keys[4], (ENC, D), ENC ** -0.5, 0.1875, ((1, 4),))
    conv_kernel = scatter_about(arg_keys[5], (KW, ENC), 0.6, 2.5, (), jnp.float32)
    nbr_owner_keys = jax.random.split(jax.random.fold_in(arg_keys[6], 1), SPANS // CH_DEV)
    nbr_owner_turns = jax.random.permutation(jax.random.fold_in(arg_keys[6], 3), SPANS // CH_DEV)
    nbr_owner = jax.vmap(lambda own, number: assign_block(jax.random.fold_in(arg_keys[6], 2), own, number, CH_DEV, N_DP, NBR, CAP, 2))(nbr_owner_keys, nbr_owner_turns).reshape((SPANS, NBR))
    nbr_row = plant(jax.random.randint(arg_keys[7], (SPANS, NBR), 0, BLK_DEV), jax.random.fold_in(arg_keys[7], 1), 0, BLK_DEV - 1).astype(jnp.int32)
    return dict(queries=queries, cotangent=cotangent, db_states=db_states, key_weight=key_weight, value_weight=value_weight, conv_kernel=conv_kernel, nbr_owner=nbr_owner, nbr_row=nbr_row)


def conv_apply(padded, kernel, length):
    summed = kernel[0] * padded[:, 0:length, :].astype(jnp.float32)
    for offset in range(1, KW):
        summed = summed + kernel[offset] * padded[:, offset:offset + length, :].astype(jnp.float32)
    return summed

def conv_adjoint(grad_padded, kernel, length):
    final_tap = KW - 1
    summed = kernel[0] * grad_padded[:, final_tap:final_tap + length, :]
    for offset in range(1, KW):
        begin = final_tap - offset
        summed = summed + kernel[offset] * grad_padded[:, begin:begin + length, :]
    return summed

def reference(queries, cotangent, db_states, key_weight, value_weight, conv_kernel, nbr_owner, nbr_row):
    half_taps = (KW - 1) // 2
    score_scale = 1.0 / math.sqrt(HD)
    block_ids = (nbr_owner * BLK_DEV + nbr_row).astype(jnp.int32)
    query_spans = queries.reshape(SPANS, SPAN, HEADS, HD)
    grad_spans = cotangent.reshape(SPANS, SPAN, HEADS, HD)

    def one_span(carry, inputs):
        grad_key, grad_value, grad_taps = carry
        span_ids, query_here, grad_here = inputs
        raw_blocks = db_states[span_ids]
        padded = jnp.pad(raw_blocks.astype(jnp.float32), ((0, 0), (half_taps, half_taps), (0, 0)))
        mixed = conv_apply(padded, conv_kernel, NLEN).astype(jnp.bfloat16)
        mixed_flat = mixed.reshape(NBR * NLEN, ENC)
        keys = jnp.dot(mixed_flat, key_weight, preferred_element_type=jnp.float32).astype(jnp.bfloat16)
        values = jnp.dot(mixed_flat, value_weight, preferred_element_type=jnp.float32).astype(jnp.bfloat16)
        key_heads = keys.reshape(NBR * NLEN, HEADS, HD).astype(jnp.float32)
        value_heads = values.reshape(NBR * NLEN, HEADS, HD).astype(jnp.float32)
        query_heads = query_here.astype(jnp.float32)
        scores = jnp.einsum('qhd,khd->hqk', query_heads, key_heads) * score_scale
        highest = lax.optimization_barrier(jnp.max(scores, axis=-1, keepdims=True))
        expo = jnp.exp(scores - highest)
        probs = expo / lax.optimization_barrier(jnp.sum(expo, axis=-1, keepdims=True))
        probs_b = probs.astype(jnp.bfloat16)
        probs_wide = probs_b.astype(jnp.float32)
        attended = jnp.einsum('hqk,khd->qhd', probs_wide, value_heads).astype(jnp.bfloat16)
        grad_heads = grad_here.astype(jnp.float32)
        grad_probs = jnp.einsum('qhd,khd->hqk', grad_heads, value_heads)
        grad_values = jnp.einsum('hqk,qhd->khd', probs_wide, grad_heads).astype(jnp.bfloat16)
        inner = lax.optimization_barrier(jnp.sum(grad_probs * probs, axis=-1, keepdims=True))
        grad_scores = (score_scale * probs * (grad_probs - inner)).astype(jnp.bfloat16).astype(jnp.float32)
        grad_query = jnp.einsum('hqk,khd->qhd', grad_scores, key_heads).astype(jnp.bfloat16)
        grad_keys = jnp.einsum('hqk,qhd->khd', grad_scores, query_heads).astype(jnp.bfloat16)
        keys_flat = grad_keys.reshape(NBR * NLEN, D)
        values_flat = grad_values.reshape(NBR * NLEN, D)
        grad_key = grad_key + jnp.dot(mixed_flat.T, keys_flat, preferred_element_type=jnp.float32)
        grad_value = grad_value + jnp.dot(mixed_flat.T, values_flat, preferred_element_type=jnp.float32)
        grad_mixed = jnp.dot(keys_flat, key_weight.T, preferred_element_type=jnp.float32)
        grad_mixed = grad_mixed + jnp.dot(values_flat, value_weight.T, preferred_element_type=jnp.float32)
        grad_mixed = grad_mixed.reshape(NBR, NLEN, ENC)
        grad_padded = jnp.pad(grad_mixed, ((0, 0), (half_taps, half_taps), (0, 0)))
        grad_raw = conv_adjoint(grad_padded, conv_kernel, NLEN).astype(jnp.bfloat16)
        tap_terms = jnp.stack([lax.optimization_barrier(jnp.sum(grad_mixed * padded[:, offset:offset + NLEN, :], axis=(0, 1))) for offset in range(KW)])
        grad_taps = grad_taps + tap_terms
        return ((grad_key, grad_value, grad_taps), (attended, grad_query, grad_raw))
    start = (jnp.zeros((ENC, D), jnp.float32), jnp.zeros((ENC, D), jnp.float32), jnp.zeros((KW, ENC), jnp.float32))
    totals, outputs = lax.scan(one_span, start, (block_ids, query_spans, grad_spans))
    grad_key, grad_value, grad_taps = totals
    attended, grad_query, grad_raw = outputs
    flat_ids = block_ids.reshape(SPANS * NBR)
    grad_states = jnp.zeros((BLOCKS, NLEN, ENC), jnp.float32).at[flat_ids].add(grad_raw.reshape(SPANS * NBR, NLEN, ENC).astype(jnp.float32))
    return (attended.reshape(TOKENS, D), grad_query.reshape(TOKENS, D), grad_states, grad_key, grad_value, grad_taps)
```

```python
import functools
import math

import jax
import jax.numpy as jnp
from jax import lax
from jax.experimental import pallas as pl
from jax.experimental.pallas import tpu as pltpu
from jax.sharding import PartitionSpec as P

HD = 128
ENC = 896
SPAN = 64
NBR = 2
NLEN = 128
KW = 3
LANES = 128
CHUNKS = ENC // LANES
F32 = jnp.float32
BF16 = jnp.bfloat16
NT = (((1,), (1,)), ((), ()))


def shifted(block):
    rows = block.shape[0]
    at = lax.broadcasted_iota(jnp.int32, block.shape, 0)
    down = jnp.where(at == 0, 0.0, pltpu.roll(block, 1, 0))
    up = jnp.where(at == rows - 1, 0.0, pltpu.roll(block, rows - 1, 0))
    return down, up


def core_kernel(
    heads,
    q_ref,
    g_ref,
    raw_ref,
    kw_ref,
    vw_ref,
    taps_ref,
    att_ref,
    gq_ref,
    part_ref,
    gkw_ref,
    gvw_ref,
    gt_ref,
    weights,
    mixed_s,
    mixed_t,
    grads,
    gm_s,
    taps_acc,
):
    span = pl.program_id(0)
    scale = 1.0 / math.sqrt(HD)
    keys_here = NBR * NLEN

    @pl.when(span == 0)
    def _():
        for h in range(heads):
            weights[:, 2 * h * HD : (2 * h + 1) * HD] = kw_ref[:, h * HD : (h + 1) * HD]
            weights[:, (2 * h + 1) * HD : (2 * h + 2) * HD] = vw_ref[:, h * HD : (h + 1) * HD]
        taps_acc[...] = jnp.zeros_like(taps_acc)

    for c in range(CHUNKS):
        cols = slice(c * LANES, (c + 1) * LANES)
        for n in range(NBR):
            raw = raw_ref[n, :, cols].astype(F32)
            down, up = shifted(raw)
            mixed = taps_ref[0:1, cols] * down
            mixed = mixed + taps_ref[1:2, cols] * raw
            mixed = mixed + taps_ref[2:3, cols] * up
            mixed_s[n * NLEN : (n + 1) * NLEN, cols] = mixed.astype(BF16)
    mixed = mixed_s[...]
    rows = pl.ds(pl.multiple_of(span * keys_here, keys_here), keys_here)
    mixed_t[:, rows] = mixed.T

    zeros = jnp.zeros((SPAN, HD), BF16)
    for h in range(heads):
        wide = slice(2 * h * HD, (2 * h + 2) * HD)
        cols = slice(h * HD, (h + 1) * HD)
        kv = jnp.dot(mixed, weights[:, wide], preferred_element_type=F32).astype(BF16)
        q = q_ref[:, cols]
        g = g_ref[:, cols]
        block_diag = jnp.concatenate(
            [jnp.concatenate([q, zeros], axis=1), jnp.concatenate([zeros, g], axis=1)], axis=0
        )
        both = lax.dot_general(block_diag, kv, NT, preferred_element_type=F32)
        scores = both[:SPAN] * scale
        grad_probs = both[SPAN:]
        expo = jnp.exp(scores - jnp.max(scores, axis=-1, keepdims=True))
        probs = expo / jnp.sum(expo, axis=-1, keepdims=True)
        inner = jnp.sum(grad_probs * probs, axis=-1, keepdims=True)
        grad_scores = scale * probs * (grad_probs - inner)
        stacked = jnp.concatenate([grad_scores, probs], axis=0).astype(BF16)
        out = jnp.dot(stacked, kv, preferred_element_type=F32)
        gq_ref[:, cols] = out[:SPAN, :HD].astype(BF16)
        att_ref[:, cols] = out[SPAN:, HD:].astype(BF16)
        grads[rows, wide] = jnp.dot(
            stacked.T, block_diag, preferred_element_type=F32
        ).astype(BF16)

    gm_s[...] = lax.dot_general(grads[rows, :], weights[...], NT, preferred_element_type=F32)
    for c in range(CHUNKS):
        cols = slice(c * LANES, (c + 1) * LANES)
        for n in range(NBR):
            gm = gm_s[n * NLEN : (n + 1) * NLEN, cols]
            gm_down, gm_up = shifted(gm)
            back = taps_ref[0:1, cols] * gm_up
            back = back + taps_ref[1:2, cols] * gm
            back = back + taps_ref[2:3, cols] * gm_down
            part_ref[n, :, cols] = back.astype(BF16)
            raw = raw_ref[n, :, cols].astype(F32)
            down, up = shifted(raw)
            for w, other in enumerate((down, raw, up)):
                taps_acc[w, :, cols] += jnp.sum(
                    (gm * other).reshape(NLEN // 8, 8, LANES), axis=0
                )

    @pl.when(span == pl.num_programs(0) - 1)
    def _():
        gt_ref[...] = jnp.sum(taps_acc[...], axis=1)

        def one_head(h, carry):
            wide = pl.ds(pl.multiple_of(h * 2 * HD, 2 * HD), 2 * HD)
            cols = pl.ds(pl.multiple_of(h * HD, HD), HD)
            term = jnp.dot(mixed_t[...], grads[:, wide], preferred_element_type=F32)
            gkw_ref[:, cols] = term[:, :HD].astype(BF16)
            gvw_ref[:, cols] = term[:, HD:].astype(BF16)
            return carry

        lax.fori_loop(0, heads, one_head, 0)


def core(queries, cotangent, raw, key_weight, value_weight, conv_kernel):
    tokens, width = queries.shape
    heads = width // HD
    spans = tokens // SPAN
    keys_all = spans * NBR * NLEN
    whole = lambda shape: pl.BlockSpec(
        shape, lambda i: (0,) * len(shape), pipeline_mode=pl.Buffered(1)
    )
    span_rows = pl.BlockSpec((SPAN, width), lambda i: (i, 0))
    blocks = pl.BlockSpec((NBR, NLEN, ENC), lambda i: (i, 0, 0))
    return pl.pallas_call(
        functools.partial(core_kernel, heads),
        grid=(spans,),
        in_specs=[
            span_rows,
            span_rows,
            blocks,
            whole((ENC, width)),
            whole((ENC, width)),
            whole((KW, ENC)),
        ],
        out_specs=[
            span_rows,
            span_rows,
            blocks,
            whole((ENC, width)),
            whole((ENC, width)),
            whole((KW, ENC)),
        ],
        out_shape=[
            jax.ShapeDtypeStruct((tokens, width), BF16),
            jax.ShapeDtypeStruct((tokens, width), BF16),
            jax.ShapeDtypeStruct((spans * NBR, NLEN, ENC), BF16),
            jax.ShapeDtypeStruct((ENC, width), BF16),
            jax.ShapeDtypeStruct((ENC, width), BF16),
            jax.ShapeDtypeStruct((KW, ENC), F32),
        ],
        scratch_shapes=[
            pltpu.VMEM((ENC, 2 * width), BF16),
            pltpu.VMEM((NBR * NLEN, ENC), BF16),
            pltpu.VMEM((ENC, keys_all), BF16),
            pltpu.VMEM((keys_all, 2 * width), BF16),
            pltpu.VMEM((NBR * NLEN, ENC), F32),
            pltpu.VMEM((KW, 8, ENC), F32),
        ],
        compiler_params=pltpu.CompilerParams(
            dimension_semantics=("arbitrary",), vmem_limit_bytes=56 * 1024 * 1024
        ),
        cost_estimate=pl.CostEstimate(
            flops=27_000_000_000, bytes_accessed=30_000_000, transcendentals=1_200_000
        ),
    )(queries, cotangent, raw, key_weight, value_weight, conv_kernel)


def shards(
    queries, cotangent, db_states, key_weight, value_weight, conv_kernel, nbr_owner, nbr_row
):
    owners = lax.axis_size("dp")
    span_count = nbr_owner.shape[0]
    request_count = span_count * NBR
    capacity = max(2, (request_count + owners - 1) // owners)
    quarter = db_states.shape[1]
    local_blocks = db_states.shape[0]
    slots_total = owners * capacity
    owner_flat = nbr_owner.reshape(request_count)
    row_flat = nbr_row.reshape(request_count)
    positions = jnp.arange(request_count, dtype=jnp.int32)
    same_owner = owner_flat[:, None] == owner_flat[None, :]
    earlier = positions[:, None] > positions[None, :]
    slot_index = jnp.sum(jnp.logical_and(same_owner, earlier).astype(jnp.int32), axis=1)
    target = owner_flat * capacity + slot_index
    slot_hits = target[:, None] == jnp.arange(slots_total, dtype=jnp.int32)[None, :]
    used_slot = jnp.any(slot_hits, axis=0)
    row_sent = jnp.sum(jnp.where(slot_hits, row_flat[:, None], 0), axis=0)
    row_table = jnp.where(used_slot, row_sent, -1).reshape(owners, capacity)
    slot_matrix = slot_hits.astype(jnp.bfloat16)
    states_flat = db_states.reshape(local_blocks, quarter * ENC)
    asked = lax.all_to_all(row_table, "dp", split_axis=0, concat_axis=0, tiled=True)
    asked_flat = asked.reshape(slots_total)
    picker = (asked_flat[:, None] == jnp.arange(local_blocks, dtype=jnp.int32)[None, :]).astype(
        jnp.bfloat16
    )
    fetched = jnp.dot(picker, states_flat, preferred_element_type=jnp.float32).astype(jnp.bfloat16)
    fetched = fetched.reshape(owners, capacity, quarter, ENC)
    replied = lax.all_to_all(fetched, "dp", split_axis=0, concat_axis=0, tiled=True)
    received = jnp.dot(
        slot_matrix, replied.reshape(slots_total, quarter * ENC), preferred_element_type=jnp.float32
    )
    received = received.astype(jnp.bfloat16).reshape(request_count, quarter, ENC)
    raw = lax.all_gather(received, "db", axis=1, tiled=True)
    attended, grad_query, part, key_term, value_term, taps_term = core(
        queries, cotangent, raw, key_weight, value_weight, conv_kernel
    )
    grad_raw = lax.psum_scatter(part, "db", scatter_dimension=1, tiled=True)
    grad_raw_b = grad_raw.reshape(request_count, quarter * ENC)
    grad_send = jnp.einsum(
        "ns,nf->sf", slot_matrix, grad_raw_b, preferred_element_type=jnp.float32
    ).astype(jnp.bfloat16)
    grad_send = grad_send.reshape(owners, capacity, quarter, ENC)
    grad_back = lax.all_to_all(grad_send, "dp", split_axis=0, concat_axis=0, tiled=True)
    picker_back = (
        jnp.arange(local_blocks, dtype=jnp.int32)[:, None] == asked_flat[None, :]
    ).astype(jnp.bfloat16)
    grad_states = jnp.dot(
        picker_back,
        grad_back.reshape(slots_total, quarter * ENC),
        preferred_element_type=jnp.float32,
    )
    grad_states = grad_states.reshape(local_blocks, quarter, ENC)
    grad_key_weight, grad_value_weight = lax.psum((key_term, value_term), "dp")
    grad_kernel = lax.psum(taps_term, ("dp", "db"))
    return (
        attended,
        grad_query,
        grad_states,
        grad_key_weight.astype(F32),
        grad_value_weight.astype(F32),
        grad_kernel,
    )


def solution(mesh):
    return jax.shard_map(
        shards,
        mesh=mesh,
        in_specs=(
            P("dp", "db"),
            P("dp", "db"),
            P("dp", "db", None),
            P(None, "db"),
            P(None, "db"),
            P(),
            P("dp", None),
            P("dp", None),
        ),
        out_specs=(
            P("dp", "db"),
            P("dp", "db"),
            P("dp", "db", None),
            P(None, "db"),
            P(None, "db"),
            P(),
        ),
        check_vma=False,
    )
```

```python
import functools
import math

import jax
import jax.numpy as jnp
from jax import lax
from jax.experimental import pallas as pl
from jax.experimental.pallas import tpu as pltpu
from jax.sharding import PartitionSpec as P

HD = 128
ENC = 896
SPAN = 64
NBR = 2
NLEN = 128
KW = 3
LANES = 128
CHUNKS = ENC // LANES
F32 = jnp.float32
BF16 = jnp.bfloat16
NT = (((1,), (1,)), ((), ()))


def shifted(block):
    rows = block.shape[0]
    at = lax.broadcasted_iota(jnp.int32, block.shape, 0)
    down = jnp.where(at == 0, 0.0, pltpu.roll(block, 1, 0))
    up = jnp.where(at == rows - 1, 0.0, pltpu.roll(block, rows - 1, 0))
    return down, up


def core_kernel(
    heads,
    q_ref,
    g_ref,
    raw_ref,
    kw_ref,
    vw_ref,
    taps_ref,
    att_ref,
    gq_ref,
    part_ref,
    gkw_ref,
    gvw_ref,
    gt_ref,
    weights,
    mixed_s,
    mixed_t,
    grads,
    gm_s,
    taps_acc,
    kv_s,
    both_s,
    stacked_s,
):
    span = pl.program_id(0)
    scale = 1.0 / math.sqrt(HD)
    keys_here = NBR * NLEN

    @pl.when(span == 0)
    def _():
        for h in range(heads):
            weights[:, 2 * h * HD : (2 * h + 1) * HD] = kw_ref[:, h * HD : (h + 1) * HD]
            weights[:, (2 * h + 1) * HD : (2 * h + 2) * HD] = vw_ref[:, h * HD : (h + 1) * HD]
        taps_acc[...] = jnp.zeros_like(taps_acc)

    for c in range(CHUNKS):
        cols = slice(c * LANES, (c + 1) * LANES)
        for n in range(NBR):
            raw = raw_ref[c, :, n].reshape(NLEN, LANES).astype(F32)
            down, up = shifted(raw)
            mixed = taps_ref[0:1, cols] * down
            mixed = mixed + taps_ref[1:2, cols] * raw
            mixed = mixed + taps_ref[2:3, cols] * up
            mixed_s[n * NLEN : (n + 1) * NLEN, cols] = mixed.astype(BF16)
    mixed = mixed_s[...]
    rows = pl.ds(pl.multiple_of(span * keys_here, keys_here), keys_here)
    mixed_t[:, rows] = mixed.T

    zeros = jnp.zeros((SPAN, HD), BF16)
    kv_s[...] = jnp.dot(mixed, weights[...], preferred_element_type=F32).astype(BF16)

    def diag(h):
        q = q_ref[:, h * HD : (h + 1) * HD]
        g = g_ref[:, h * HD : (h + 1) * HD]
        return jnp.concatenate(
            [jnp.concatenate([q, zeros], axis=1), jnp.concatenate([zeros, g], axis=1)], axis=0
        )

    for h in range(heads):
        wide = slice(2 * h * HD, (2 * h + 2) * HD)
        both_s[h] = lax.dot_general(diag(h), kv_s[:, wide], NT, preferred_element_type=F32)
    for h in range(heads):
        scores = both_s[h, :SPAN] * scale
        grad_probs = both_s[h, SPAN:]
        expo = jnp.exp(scores - jnp.max(scores, axis=-1, keepdims=True))
        probs = expo / jnp.sum(expo, axis=-1, keepdims=True)
        inner = jnp.sum(grad_probs * probs, axis=-1, keepdims=True)
        grad_scores = scale * probs * (grad_probs - inner)
        stacked_s[h, :SPAN] = grad_scores.astype(BF16)
        stacked_s[h, SPAN:] = probs.astype(BF16)
    for h in range(heads):
        wide = slice(2 * h * HD, (2 * h + 2) * HD)
        cols = slice(h * HD, (h + 1) * HD)
        out = jnp.dot(stacked_s[h], kv_s[:, wide], preferred_element_type=F32)
        gq_ref[:, cols] = out[:SPAN, :HD].astype(BF16)
        att_ref[:, cols] = out[SPAN:, HD:].astype(BF16)
    for h in range(heads):
        wide = slice(2 * h * HD, (2 * h + 2) * HD)
        grads[rows, wide] = lax.dot_general(
            stacked_s[h], diag(h), (((0,), (0,)), ((), ())), preferred_element_type=F32
        ).astype(BF16)

    gm_s[...] = lax.dot_general(grads[rows, :], weights[...], NT, preferred_element_type=F32)
    for c in range(CHUNKS):
        cols = slice(c * LANES, (c + 1) * LANES)
        for n in range(NBR):
            gm = gm_s[n * NLEN : (n + 1) * NLEN, cols]
            gm_down, gm_up = shifted(gm)
            back = taps_ref[0:1, cols] * gm_up
            back = back + taps_ref[1:2, cols] * gm
            back = back + taps_ref[2:3, cols] * gm_down
            part_ref[c, :, n] = back.astype(BF16).reshape(part_ref.shape[1], -1, LANES)
            raw = raw_ref[c, :, n].reshape(NLEN, LANES).astype(F32)
            down, up = shifted(raw)
            for w, other in enumerate((down, raw, up)):
                taps_acc[w, :, cols] += jnp.sum(
                    (gm * other).reshape(NLEN // 8, 8, LANES), axis=0
                )

    @pl.when(span == pl.num_programs(0) - 1)
    def _():
        gt_ref[...] = jnp.sum(taps_acc[...], axis=1)

        def one_head(h, carry):
            wide = pl.ds(pl.multiple_of(h * 2 * HD, 2 * HD), 2 * HD)
            cols = pl.ds(pl.multiple_of(h * HD, HD), HD)
            term = jnp.dot(mixed_t[...], grads[:, wide], preferred_element_type=F32)
            gkw_ref[:, cols] = term[:, :HD].astype(BF16)
            gvw_ref[:, cols] = term[:, HD:].astype(BF16)
            return carry

        lax.fori_loop(0, heads, one_head, 0)


def core(queries, cotangent, raw, key_weight, value_weight, conv_kernel):
    tokens, width = queries.shape
    heads = width // HD
    spans = tokens // SPAN
    keys_all = spans * NBR * NLEN
    whole = lambda shape: pl.BlockSpec(
        shape, lambda i: (0,) * len(shape), pipeline_mode=pl.Buffered(1)
    )
    span_rows = pl.BlockSpec((SPAN, width), lambda i: (i, 0))
    parts, quarter = raw.shape[1], raw.shape[3]
    blocks = pl.BlockSpec((CHUNKS, parts, NBR, quarter, LANES), lambda i: (0, 0, i, 0, 0))
    return pl.pallas_call(
        functools.partial(core_kernel, heads),
        grid=(spans,),
        in_specs=[
            span_rows,
            span_rows,
            blocks,
            whole((ENC, width)),
            whole((ENC, width)),
            whole((KW, ENC)),
        ],
        out_specs=[
            span_rows,
            span_rows,
            blocks,
            whole((ENC, width)),
            whole((ENC, width)),
            whole((KW, ENC)),
        ],
        out_shape=[
            jax.ShapeDtypeStruct((tokens, width), BF16),
            jax.ShapeDtypeStruct((tokens, width), BF16),
            jax.ShapeDtypeStruct(raw.shape, BF16),
            jax.ShapeDtypeStruct((ENC, width), BF16),
            jax.ShapeDtypeStruct((ENC, width), BF16),
            jax.ShapeDtypeStruct((KW, ENC), F32),
        ],
        scratch_shapes=[
            pltpu.VMEM((ENC, 2 * width), BF16),
            pltpu.VMEM((NBR * NLEN, ENC), BF16),
            pltpu.VMEM((ENC, keys_all), BF16),
            pltpu.VMEM((keys_all, 2 * width), BF16),
            pltpu.VMEM((NBR * NLEN, ENC), F32),
            pltpu.VMEM((KW, 8, ENC), F32),
            pltpu.VMEM((NBR * NLEN, 2 * width), BF16),
            pltpu.VMEM((heads, 2 * SPAN, NBR * NLEN), F32),
            pltpu.VMEM((heads, 2 * SPAN, NBR * NLEN), BF16),
        ],
        compiler_params=pltpu.CompilerParams(
            dimension_semantics=("arbitrary",), vmem_limit_bytes=56 * 1024 * 1024
        ),
        cost_estimate=pl.CostEstimate(
            flops=27_000_000_000, bytes_accessed=30_000_000, transcendentals=1_200_000
        ),
    )(queries, cotangent, raw, key_weight, value_weight, conv_kernel)


def dp_peer(step):
    me = lax.axis_index("dp")
    z = lax.rem(me // 8 + step // 8, 4)
    x = lax.rem(lax.rem(me // 2, 4) + lax.rem(step // 2, 4), 4)
    return z * 8 + x * 2 + lax.rem(me + step, 2)


def fetch_kernel(
    owners,
    parts,
    slot_ref,
    table_ref,
    states_ref,
    raw_ref,
    asked_ref,
    asked_s,
    send,
    ask_sem,
    local_sem,
    send_sem,
    recv_sem,
    y_send,
    y_recv,
    *recv,
):
    me = lax.axis_index("dp")
    y = lax.axis_index("db")
    right = lax.rem(y + 1, parts)
    left = lax.rem(y + parts - 1, parts)
    requests = raw_ref.shape[2]
    half = requests // 2
    capacity = 2
    others = owners - 1

    barrier = pltpu.get_barrier_semaphore()

    def greet(step, carry):
        pl.semaphore_signal(barrier, inc=1, device_id={"dp": dp_peer(step)})
        return carry

    lax.fori_loop(1, owners, greet, 0)
    for side in (left, right):
        pl.semaphore_signal(barrier, inc=1, device_id={"db": side})
    pl.semaphore_wait(barrier, others + 2)

    def ask(step, carry):
        peer = dp_peer(step)
        pltpu.make_async_remote_copy(
            src_ref=table_ref.at[peer],
            dst_ref=asked_ref.at[me],
            send_sem=ask_sem.at[0],
            recv_sem=ask_sem.at[1],
            device_id={"dp": peer},
        ).start()
        return carry

    lax.fori_loop(1, owners, ask, 0)
    asked_ref[me] = table_ref[me]
    most = asked_ref.at[pl.ds(0, others)]
    pltpu.make_async_copy(most, most, ask_sem.at[1]).wait()
    pltpu.make_async_copy(asked_ref, asked_s, local_sem).start()
    pltpu.make_async_copy(asked_ref, asked_s, local_sem).wait()

    for c in range(CHUNKS):
        cols = slice(c * LANES, (c + 1) * LANES)

        def reply(step, carry):
            peer = dp_peer(step)
            for k in range(capacity):
                row = jnp.maximum(asked_s[peer, 0, k], 0)
                send[c, capacity * peer + k] = states_ref[row, :, cols]
            pltpu.make_async_remote_copy(
                src_ref=send.at[c, pl.ds(capacity * peer, capacity)],
                dst_ref=recv[c].at[pl.ds(capacity * me, capacity)],
                send_sem=send_sem.at[c],
                recv_sem=recv_sem.at[c],
                device_id={"dp": peer},
            ).start()
            return carry

        lax.fori_loop(1, owners, reply, 0)
        for k in range(capacity):
            row = jnp.maximum(asked_s[me, 0, k], 0)
            recv[c][capacity * me + k] = states_ref[row, :, cols]

    def along_y(kind, c, part, rows, side):
        block = raw_ref.at[c, part, rows]
        return pltpu.make_async_remote_copy(
            src_ref=block,
            dst_ref=block,
            send_sem=y_send.at[kind, c],
            recv_sem=y_recv.at[kind, c],
            device_id={"db": side},
        )

    everything, low, high = pl.ds(0, requests), pl.ds(0, half), pl.ds(half, requests - half)

    def arrivals(kind, c):
        far = lax.rem(y + 2, parts)
        part, rows = ((left, everything), (right, everything), (far, low), (far, high))[kind]
        return along_y(kind, c, part, rows, right)

    for c in range(CHUNKS + 1):
        if c < CHUNKS:
            most = recv[c].at[pl.ds(0, capacity * others)]
            pltpu.make_async_copy(most, most, recv_sem.at[c]).wait()
            for p in range(requests):
                raw_ref[c, y, p] = recv[c][slot_ref[p]]
            along_y(0, c, y, everything, right).start()
            along_y(1, c, y, everything, left).start()
        if c >= 1:
            arrivals(0, c - 1).wait_recv()
            along_y(2, c - 1, left, low, right).start()
            arrivals(1, c - 1).wait_recv()
            along_y(3, c - 1, right, high, left).start()
    for c in range(CHUNKS):
        arrivals(2, c).wait_recv()
        arrivals(3, c).wait_recv()
        along_y(0, c, y, everything, right).wait_send()
        along_y(1, c, y, everything, left).wait_send()
        along_y(2, c, left, low, right).wait_send()
        along_y(3, c, right, high, left).wait_send()
        most = send.at[c, pl.ds(0, capacity * others)]
        pltpu.make_async_copy(most, most, send_sem.at[c]).wait()
    most = table_ref.at[pl.ds(0, others)]
    pltpu.make_async_copy(most, most, ask_sem.at[0]).wait()


def fetch(slots, table, states):
    owners = table.shape[0]
    parts = lax.axis_size("db")
    requests = slots.shape[0]
    quarter = states.shape[1]
    vmem = pl.BlockSpec(memory_space=pltpu.VMEM)
    dma = pltpu.SemaphoreType.DMA
    return pl.pallas_call(
        functools.partial(fetch_kernel, owners, parts),
        in_specs=[pl.BlockSpec(memory_space=pltpu.SMEM), vmem, vmem],
        out_specs=[vmem, vmem],
        out_shape=[
            jax.ShapeDtypeStruct((CHUNKS, parts, requests, quarter, LANES), BF16),
            jax.ShapeDtypeStruct(table.shape, jnp.int32),
        ],
        scratch_shapes=[
            pltpu.SMEM(table.shape, jnp.int32),
            pltpu.VMEM((CHUNKS, 2 * owners, quarter, LANES), BF16),
            dma((2,)),
            dma,
            dma((CHUNKS,)),
            dma((CHUNKS,)),
            dma((4, CHUNKS)),
            dma((4, CHUNKS)),
        ]
        + [pltpu.VMEM((2 * owners, quarter, LANES), BF16)] * CHUNKS,
        compiler_params=pltpu.CompilerParams(
            collective_id=0, has_side_effects=True, vmem_limit_bytes=40 * 1024 * 1024
        ),
        cost_estimate=pl.CostEstimate(flops=0, bytes_accessed=16_000_000, transcendentals=0),
    )(slots, table, states)


def shards(
    queries, cotangent, db_states, key_weight, value_weight, conv_kernel, nbr_owner, nbr_row
):
    owners = lax.axis_size("dp")
    span_count = nbr_owner.shape[0]
    request_count = span_count * NBR
    capacity = max(2, (request_count + owners - 1) // owners)
    quarter = db_states.shape[1]
    local_blocks = db_states.shape[0]
    slots_total = owners * capacity
    owner_flat = nbr_owner.reshape(request_count)
    row_flat = nbr_row.reshape(request_count)
    positions = jnp.arange(request_count, dtype=jnp.int32)
    same_owner = owner_flat[:, None] == owner_flat[None, :]
    earlier = positions[:, None] > positions[None, :]
    slot_index = jnp.sum(jnp.logical_and(same_owner, earlier).astype(jnp.int32), axis=1)
    target = owner_flat * capacity + slot_index
    slot_hits = target[:, None] == jnp.arange(slots_total, dtype=jnp.int32)[None, :]
    used_slot = jnp.any(slot_hits, axis=0)
    row_sent = jnp.sum(jnp.where(slot_hits, row_flat[:, None], 0), axis=0)
    row_table = jnp.where(used_slot, row_sent, -1).reshape(owners, capacity)
    slot_matrix = slot_hits.astype(jnp.bfloat16)
    table = jnp.pad(row_table[:, None, :], ((0, 0), (0, 0), (0, LANES - capacity)))
    raw, asked = fetch(target, table, db_states)
    asked_flat = asked[:, 0, :capacity].reshape(slots_total)
    attended, grad_query, part, key_term, value_term, taps_term = core(
        queries, cotangent, raw, key_weight, value_weight, conv_kernel
    )
    grad_raw = lax.psum_scatter(part, "db", scatter_dimension=1, tiled=True)
    grad_raw = jnp.transpose(grad_raw.reshape(CHUNKS, request_count, quarter, LANES), (1, 2, 0, 3))
    grad_raw_b = grad_raw.reshape(request_count, quarter * ENC)
    grad_send = jnp.einsum(
        "ns,nf->sf", slot_matrix, grad_raw_b, preferred_element_type=jnp.float32
    ).astype(jnp.bfloat16)
    grad_send = grad_send.reshape(owners, capacity, quarter, ENC)
    grad_back = lax.all_to_all(grad_send, "dp", split_axis=0, concat_axis=0, tiled=True)
    picker_back = (
        jnp.arange(local_blocks, dtype=jnp.int32)[:, None] == asked_flat[None, :]
    ).astype(jnp.bfloat16)
    grad_states = jnp.dot(
        picker_back,
        grad_back.reshape(slots_total, quarter * ENC),
        preferred_element_type=jnp.float32,
    )
    grad_states = grad_states.reshape(local_blocks, quarter, ENC)
    grad_key_weight, grad_value_weight = lax.psum((key_term, value_term), "dp")
    grad_kernel = lax.psum(taps_term, ("dp", "db"))
    return (
        attended,
        grad_query,
        grad_states,
        grad_key_weight.astype(F32),
        grad_value_weight.astype(F32),
        grad_kernel,
    )


def solution(mesh):
    return jax.shard_map(
        shards,
        mesh=mesh,
        in_specs=(
            P("dp", "db"),
            P("dp", "db"),
            P("dp", "db", None),
            P(None, "db"),
            P(None, "db"),
            P(),
            P("dp", None),
            P("dp", None),
        ),
        out_specs=(
            P("dp", "db"),
            P("dp", "db"),
            P("dp", "db", None),
            P(None, "db"),
            P(None, "db"),
            P(),
        ),
        check_vma=False,
    )
```

```python
import functools
import math

import jax
import jax.numpy as jnp
from jax import lax
from jax.experimental import pallas as pl
from jax.experimental.pallas import tpu as pltpu
from jax.sharding import PartitionSpec as P

HD = 128
ENC = 896
SPAN = 64
NBR = 2
NLEN = 128
KW = 3
LANES = 128
CHUNKS = ENC // LANES
F32 = jnp.float32
BF16 = jnp.bfloat16
NT = (((1,), (1,)), ((), ()))


def shifted(block):
    rows = block.shape[0]
    at = lax.broadcasted_iota(jnp.int32, block.shape, 0)
    down = jnp.where(at == 0, 0.0, pltpu.roll(block, 1, 0))
    up = jnp.where(at == rows - 1, 0.0, pltpu.roll(block, rows - 1, 0))
    return down, up


def core_kernel(
    heads,
    q_ref,
    g_ref,
    raw_ref,
    kw_ref,
    vw_ref,
    taps_ref,
    att_ref,
    gq_ref,
    part_ref,
    gw_ref,
    gt_ref,
    weights,
    mixed_s,
    mixed_t,
    grads,
    gm_s,
    taps_acc,
    kv_s,
    both_s,
    stacked_s,
):
    span = pl.program_id(0)
    scale = 1.0 / math.sqrt(HD)
    keys_here = NBR * NLEN

    @pl.when(span == 0)
    def _():
        for h in range(heads):
            weights[:, 2 * h * HD : (2 * h + 1) * HD] = kw_ref[:, h * HD : (h + 1) * HD]
            weights[:, (2 * h + 1) * HD : (2 * h + 2) * HD] = vw_ref[:, h * HD : (h + 1) * HD]
        taps_acc[...] = jnp.zeros_like(taps_acc)

    for c in range(CHUNKS):
        cols = slice(c * LANES, (c + 1) * LANES)
        for n in range(NBR):
            raw = raw_ref[c, :, n].reshape(NLEN, LANES).astype(F32)
            down, up = shifted(raw)
            mixed = taps_ref[0:1, cols] * down
            mixed = mixed + taps_ref[1:2, cols] * raw
            mixed = mixed + taps_ref[2:3, cols] * up
            mixed_s[n * NLEN : (n + 1) * NLEN, cols] = mixed.astype(BF16)
    mixed = mixed_s[...]
    rows = pl.ds(pl.multiple_of(span * keys_here, keys_here), keys_here)
    mixed_t[:, rows] = mixed.T

    zeros = jnp.zeros((SPAN, HD), BF16)
    kv_s[...] = jnp.dot(mixed, weights[...], preferred_element_type=F32).astype(BF16)

    def diag(h):
        q = q_ref[:, h * HD : (h + 1) * HD]
        g = g_ref[:, h * HD : (h + 1) * HD]
        return jnp.concatenate(
            [jnp.concatenate([q, zeros], axis=1), jnp.concatenate([zeros, g], axis=1)], axis=0
        )

    for h in range(heads):
        wide = slice(2 * h * HD, (2 * h + 2) * HD)
        both_s[h] = lax.dot_general(diag(h), kv_s[:, wide], NT, preferred_element_type=F32)
    for h in range(heads):
        scores = both_s[h, :SPAN] * scale
        grad_probs = both_s[h, SPAN:]
        expo = jnp.exp(scores - jnp.max(scores, axis=-1, keepdims=True))
        probs = expo / jnp.sum(expo, axis=-1, keepdims=True)
        inner = jnp.sum(grad_probs * probs, axis=-1, keepdims=True)
        grad_scores = scale * probs * (grad_probs - inner)
        stacked_s[h, :SPAN] = grad_scores.astype(BF16)
        stacked_s[h, SPAN:] = probs.astype(BF16)
    for h in range(heads):
        wide = slice(2 * h * HD, (2 * h + 2) * HD)
        cols = slice(h * HD, (h + 1) * HD)
        out = jnp.dot(stacked_s[h], kv_s[:, wide], preferred_element_type=F32)
        gq_ref[:, cols] = out[:SPAN, :HD].astype(BF16)
        att_ref[:, cols] = out[SPAN:, HD:].astype(BF16)
    for h in range(heads):
        wide = slice(2 * h * HD, (2 * h + 2) * HD)
        grads[rows, wide] = lax.dot_general(
            stacked_s[h], diag(h), (((0,), (0,)), ((), ())), preferred_element_type=F32
        ).astype(BF16)

    gm_s[...] = lax.dot_general(grads[rows, :], weights[...], NT, preferred_element_type=F32)
    for c in range(CHUNKS):
        cols = slice(c * LANES, (c + 1) * LANES)
        for n in range(NBR):
            gm = gm_s[n * NLEN : (n + 1) * NLEN, cols]
            gm_down, gm_up = shifted(gm)
            back = taps_ref[0:1, cols] * gm_up
            back = back + taps_ref[1:2, cols] * gm
            back = back + taps_ref[2:3, cols] * gm_down
            part_ref[c, :, n] = back.astype(BF16).reshape(part_ref.shape[1], -1, LANES)
            raw = raw_ref[c, :, n].reshape(NLEN, LANES).astype(F32)
            down, up = shifted(raw)
            for w, other in enumerate((down, raw, up)):
                taps_acc[w, :, cols] += jnp.sum(
                    (gm * other).reshape(NLEN // 8, 8, LANES), axis=0
                )

    @pl.when(span == pl.num_programs(0) - 1)
    def _():
        gt_ref[...] = jnp.sum(taps_acc[...], axis=1)

        def one_head(h, carry):
            wide = pl.ds(pl.multiple_of(h * 2 * HD, 2 * HD), 2 * HD)
            term = jnp.dot(mixed_t[...], grads[:, wide], preferred_element_type=F32)
            gw_ref[0, h] = term[:, :HD].astype(BF16)
            gw_ref[1, h] = term[:, HD:].astype(BF16)
            return carry

        lax.fori_loop(0, heads, one_head, 0)


def core(queries, cotangent, raw, key_weight, value_weight, conv_kernel):
    tokens, width = queries.shape
    heads = width // HD
    spans = tokens // SPAN
    keys_all = spans * NBR * NLEN
    whole = lambda shape: pl.BlockSpec(
        shape, lambda i: (0,) * len(shape), pipeline_mode=pl.Buffered(1)
    )
    span_rows = pl.BlockSpec((SPAN, width), lambda i: (i, 0))
    parts, quarter = raw.shape[1], raw.shape[3]
    blocks = pl.BlockSpec((CHUNKS, parts, NBR, quarter, LANES), lambda i: (0, 0, i, 0, 0))
    return pl.pallas_call(
        functools.partial(core_kernel, heads),
        grid=(spans,),
        in_specs=[
            span_rows,
            span_rows,
            blocks,
            whole((ENC, width)),
            whole((ENC, width)),
            whole((KW, ENC)),
        ],
        out_specs=[
            span_rows,
            span_rows,
            blocks,
            whole((2, heads, ENC, HD)),
            whole((KW, ENC)),
        ],
        out_shape=[
            jax.ShapeDtypeStruct((tokens, width), BF16),
            jax.ShapeDtypeStruct((tokens, width), BF16),
            jax.ShapeDtypeStruct(raw.shape, BF16),
            jax.ShapeDtypeStruct((2, heads, ENC, HD), BF16),
            jax.ShapeDtypeStruct((KW, ENC), F32),
        ],
        scratch_shapes=[
            pltpu.VMEM((ENC, 2 * width), BF16),
            pltpu.VMEM((NBR * NLEN, ENC), BF16),
            pltpu.VMEM((ENC, keys_all), BF16),
            pltpu.VMEM((keys_all, 2 * width), BF16),
            pltpu.VMEM((NBR * NLEN, ENC), F32),
            pltpu.VMEM((KW, 8, ENC), F32),
            pltpu.VMEM((NBR * NLEN, 2 * width), BF16),
            pltpu.VMEM((heads, 2 * SPAN, NBR * NLEN), F32),
            pltpu.VMEM((heads, 2 * SPAN, NBR * NLEN), BF16),
        ],
        compiler_params=pltpu.CompilerParams(
            dimension_semantics=("arbitrary",), vmem_limit_bytes=56 * 1024 * 1024
        ),
        cost_estimate=pl.CostEstimate(
            flops=27_000_000_000, bytes_accessed=30_000_000, transcendentals=1_200_000
        ),
    )(queries, cotangent, raw, key_weight, value_weight, conv_kernel)


def dp_peer(step):
    me = lax.axis_index("dp")
    z = lax.rem(me // 8 + step // 8, 4)
    x = lax.rem(lax.rem(me // 2, 4) + lax.rem(step // 2, 4), 4)
    return z * 8 + x * 2 + lax.rem(me + step, 2)


def fetch_kernel(
    owners,
    parts,
    slot_ref,
    table_ref,
    states_ref,
    raw_ref,
    asked_ref,
    asked_s,
    send,
    ask_sem,
    local_sem,
    send_sem,
    recv_sem,
    y_send,
    y_recv,
    *recv,
):
    me = lax.axis_index("dp")
    y = lax.axis_index("db")
    right = lax.rem(y + 1, parts)
    left = lax.rem(y + parts - 1, parts)
    requests = raw_ref.shape[2]
    half = requests // 2
    capacity = 2
    others = owners - 1

    barrier = pltpu.get_barrier_semaphore()

    def greet(step, carry):
        pl.semaphore_signal(barrier, inc=1, device_id={"dp": dp_peer(step)})
        return carry

    lax.fori_loop(1, owners, greet, 0)
    for side in (left, right):
        pl.semaphore_signal(barrier, inc=1, device_id={"db": side})
    pl.semaphore_wait(barrier, others + 2)

    def ask(step, carry):
        peer = dp_peer(step)
        pltpu.make_async_remote_copy(
            src_ref=table_ref.at[peer],
            dst_ref=asked_ref.at[me],
            send_sem=ask_sem.at[0],
            recv_sem=ask_sem.at[1],
            device_id={"dp": peer},
        ).start()
        return carry

    lax.fori_loop(1, owners, ask, 0)
    asked_ref[me] = table_ref[me]
    most = asked_ref.at[pl.ds(0, others)]
    pltpu.make_async_copy(most, most, ask_sem.at[1]).wait()
    pltpu.make_async_copy(asked_ref, asked_s, local_sem).start()
    pltpu.make_async_copy(asked_ref, asked_s, local_sem).wait()

    for c in range(CHUNKS):
        cols = slice(c * LANES, (c + 1) * LANES)

        def reply(step, carry):
            peer = dp_peer(step)
            for k in range(capacity):
                row = jnp.maximum(asked_s[peer, 0, k], 0)
                send[c, capacity * peer + k] = states_ref[row, :, cols]
            pltpu.make_async_remote_copy(
                src_ref=send.at[c, pl.ds(capacity * peer, capacity)],
                dst_ref=recv[c].at[pl.ds(capacity * me, capacity)],
                send_sem=send_sem.at[c],
                recv_sem=recv_sem.at[c],
                device_id={"dp": peer},
            ).start()
            return carry

        lax.fori_loop(1, owners, reply, 0)
        for k in range(capacity):
            row = jnp.maximum(asked_s[me, 0, k], 0)
            recv[c][capacity * me + k] = states_ref[row, :, cols]

    def along_y(kind, c, part, rows, side):
        block = raw_ref.at[c, part, rows]
        return pltpu.make_async_remote_copy(
            src_ref=block,
            dst_ref=block,
            send_sem=y_send.at[kind, c],
            recv_sem=y_recv.at[kind, c],
            device_id={"db": side},
        )

    everything, low, high = pl.ds(0, requests), pl.ds(0, half), pl.ds(half, requests - half)

    def arrivals(kind, c):
        far = lax.rem(y + 2, parts)
        part, rows = ((left, everything), (right, everything), (far, low), (far, high))[kind]
        return along_y(kind, c, part, rows, right)

    for c in range(CHUNKS + 1):
        if c < CHUNKS:
            most = recv[c].at[pl.ds(0, capacity * others)]
            pltpu.make_async_copy(most, most, recv_sem.at[c]).wait()
            for p in range(requests):
                raw_ref[c, y, p] = recv[c][slot_ref[p]]
            along_y(0, c, y, everything, right).start()
            along_y(1, c, y, everything, left).start()
        if c >= 1:
            arrivals(0, c - 1).wait_recv()
            along_y(2, c - 1, left, low, right).start()
            arrivals(1, c - 1).wait_recv()
            along_y(3, c - 1, right, high, left).start()
    for c in range(CHUNKS):
        arrivals(2, c).wait_recv()
        arrivals(3, c).wait_recv()
        along_y(0, c, y, everything, right).wait_send()
        along_y(1, c, y, everything, left).wait_send()
        along_y(2, c, left, low, right).wait_send()
        along_y(3, c, right, high, left).wait_send()
        most = send.at[c, pl.ds(0, capacity * others)]
        pltpu.make_async_copy(most, most, send_sem.at[c]).wait()
    most = table_ref.at[pl.ds(0, others)]
    pltpu.make_async_copy(most, most, ask_sem.at[0]).wait()


def fetch(slots, table, states):
    owners = table.shape[0]
    parts = lax.axis_size("db")
    requests = slots.shape[0]
    quarter = states.shape[1]
    vmem = pl.BlockSpec(memory_space=pltpu.VMEM)
    dma = pltpu.SemaphoreType.DMA
    return pl.pallas_call(
        functools.partial(fetch_kernel, owners, parts),
        in_specs=[pl.BlockSpec(memory_space=pltpu.SMEM), vmem, vmem],
        out_specs=[vmem, vmem],
        out_shape=[
            jax.ShapeDtypeStruct((CHUNKS, parts, requests, quarter, LANES), BF16),
            jax.ShapeDtypeStruct(table.shape, jnp.int32),
        ],
        scratch_shapes=[
            pltpu.SMEM(table.shape, jnp.int32),
            pltpu.VMEM((CHUNKS, 2 * owners, quarter, LANES), BF16),
            dma((2,)),
            dma,
            dma((CHUNKS,)),
            dma((CHUNKS,)),
            dma((4, CHUNKS)),
            dma((4, CHUNKS)),
        ]
        + [pltpu.VMEM((2 * owners, quarter, LANES), BF16)] * CHUNKS,
        compiler_params=pltpu.CompilerParams(
            collective_id=0, has_side_effects=True, vmem_limit_bytes=40 * 1024 * 1024
        ),
        cost_estimate=pl.CostEstimate(flops=0, bytes_accessed=16_000_000, transcendentals=0),
    )(slots, table, states)


def tail_kernel(
    owners,
    parts,
    req_ref,
    part_ref,
    w_ref,
    taps_ref,
    back_ref,
    wsum_ref,
    tsum_ref,
    from_far,
    onward,
    from_near,
    send,
    sibling_w,
    pair_w,
    first_in,
    first_sum,
    second_in,
    taps_in,
    taps_now,
    far_send,
    far_recv,
    near_send,
    near_recv,
    back_send,
    back_recv,
    pair_send,
    pair_recv,
    axis_send,
    axis_recv,
    taps_send,
    taps_recv,
    *mine,
):
    me = lax.axis_index("dp")
    y = lax.axis_index("db")
    z, x, core = me // 8, lax.rem(me // 2, 4), lax.rem(me, 2)
    sibling = me + 1 - 2 * core
    right = lax.rem(y + 1, parts)
    left = lax.rem(y + parts - 1, parts)
    far = lax.rem(y + 2, parts)
    requests = part_ref.shape[2]
    half = requests // 2
    capacity = 2
    others = owners - 1
    low, high = pl.ds(0, half), pl.ds(half, requests - half)

    def x_peer(step):
        return z * 8 + lax.rem(x + step, 4) * 2 + core

    def z_peer(step):
        return lax.rem(z + step, 4) * 8 + x * 2 + core

    barrier = pltpu.get_barrier_semaphore()

    def greet(step, carry):
        pl.semaphore_signal(barrier, inc=1, device_id={"dp": dp_peer(step)})
        return carry

    lax.fori_loop(1, owners, greet, 0)
    for other in range(1, parts):
        pl.semaphore_signal(barrier, inc=1, device_id={"db": lax.rem(y + other, parts)})
    pl.semaphore_wait(barrier, others + parts - 1)

    def remote(src, dst, send_sem, recv_sem, where):
        return pltpu.make_async_remote_copy(
            src_ref=src, dst_ref=dst, send_sem=send_sem, recv_sem=recv_sem, device_id=where
        )

    def far_copy(side, c):
        rows, to = ((low, right), (high, left))[side]
        return remote(
            part_ref.at[c, far, rows],
            from_far.at[side, c],
            far_send.at[side, c],
            far_recv.at[side, c],
            {"db": to},
        )

    def near_copy(side, c):
        return remote(
            onward.at[side, c],
            from_near.at[side, c],
            near_send.at[side, c],
            near_recv.at[side, c],
            {"db": (right, left)[side]},
        )

    def forward(c):
        far_copy(0, c).wait_recv()
        added = part_ref[c, right, 0:half].astype(F32) + from_far[0, c].astype(F32)
        onward[0, c, 0:half] = added.astype(BF16)
        onward[0, c, half:requests] = part_ref[c, right, half:requests]
        near_copy(0, c).start()
        far_copy(1, c).wait_recv()
        added = part_ref[c, left, half:requests].astype(F32) + from_far[1, c].astype(F32)
        onward[1, c, half:requests] = added.astype(BF16)
        onward[1, c, 0:half] = part_ref[c, left, 0:half]
        near_copy(1, c).start()

    def give_back(c):
        near_copy(0, c).wait_recv()
        near_copy(1, c).wait_recv()
        total = part_ref[c, y].astype(F32) + from_near[0, c].astype(F32)
        mine[c][...] = (total + from_near[1, c].astype(F32)).astype(BF16)

        def one(step, carry):
            peer = dp_peer(step)
            for k in range(capacity):
                send[c, capacity * peer + k] = mine[c][req_ref[capacity * peer + k]]
            remote(
                send.at[c, pl.ds(capacity * peer, capacity)],
                back_ref.at[c, pl.ds(capacity * me, capacity)],
                back_send.at[c],
                back_recv.at[c],
                {"dp": peer},
            ).start()
            return carry

        lax.fori_loop(1, owners, one, 0)
        for k in range(capacity):
            back_ref[c, capacity * me + k] = mine[c][req_ref[capacity * me + k]]

    first_at, second_at = (x, z), (z, x)
    first_peer, second_peer = (x_peer, z_peer), (z_peer, x_peer)
    order = [(d, h) for d in (1, 2, 3, 0) for h in (0, 1)]

    def group(h, step):
        return h * 4 + lax.rem(first_at[h] + step, 4)

    def pair_copy(d, h):
        g = group(h, d)
        return remote(
            w_ref.at[1 - core, g],
            sibling_w.at[g],
            pair_send.at[0, h * 4 + d],
            pair_recv.at[0, h * 4 + d],
            {"dp": sibling},
        )

    def first_copy(d, h):
        return remote(
            pair_w.at[group(h, d)],
            first_in.at[h, d - 1],
            axis_send.at[0, h * 3 + d - 1],
            axis_recv.at[0, h * 3 + d - 1],
            {"dp": first_peer[h](d)},
        )

    def second_copy(d, h):
        return remote(
            first_sum.at[h, lax.rem(second_at[h] + d, 4)],
            second_in.at[h, d - 1],
            axis_send.at[1, h * 3 + d - 1],
            axis_recv.at[1, h * 3 + d - 1],
            {"dp": second_peer[h](d)},
        )

    def second_gather(d, h, back):
        block = wsum_ref.at[core, group(h, 0), lax.rem(second_at[h] + back, 4)]
        return remote(
            block,
            block,
            axis_send.at[2, h * 3 + d - 1],
            axis_recv.at[2, h * 3 + d - 1],
            {"dp": second_peer[h](d)},
        )

    def first_gather(d, h, back):
        block = wsum_ref.at[core, group(h, back)]
        return remote(
            block,
            block,
            axis_send.at[3, h * 3 + d - 1],
            axis_recv.at[3, h * 3 + d - 1],
            {"dp": first_peer[h](d)},
        )

    def pair_gather(d, h, which):
        block = wsum_ref.at[which, group(h, 4 - d)]
        return remote(
            block,
            block,
            pair_send.at[1, h * 4 + d],
            pair_recv.at[1, h * 4 + d],
            {"dp": sibling},
        )

    def pair_sum(d, h):
        pair_copy(d, h).wait_recv()
        g = group(h, d)
        pair_w[g] = (w_ref[core, g].astype(F32) + sibling_w[g].astype(F32)).astype(BF16)
        if d:
            first_copy(d, h).start()

    def sum_first(h):
        for d in (1, 2, 3):
            first_copy(d, h).wait_recv()
        total = pair_w[group(h, 0)].astype(F32)
        for d in (1, 2, 3):
            total = total + first_in[h, d - 1].astype(F32)
        first_sum[h] = total.astype(BF16)
        for d in (1, 2, 3):
            second_copy(d, h).start()

    def sum_second(h):
        for d in (1, 2, 3):
            second_copy(d, h).wait_recv()
        total = first_sum[h, second_at[h]].astype(F32)
        for d in (1, 2, 3):
            total = total + second_in[h, d - 1].astype(F32)
        wsum_ref[core, group(h, 0), second_at[h]] = total.astype(BF16)
        for d in (1, 2, 3):
            second_gather(d, h, 0).start()

    def gather_first(h):
        for d in (1, 2, 3):
            second_gather(d, h, 4 - d).wait_recv()
        for d in (1, 2, 3):
            first_gather(d, h, 0).start()
        pair_gather(0, h, core).start()

    def gather_pair(h):
        for d in (1, 2, 3):
            first_gather(d, h, 4 - d).wait_recv()
            pair_gather(d, h, core).start()

    stages = (
        (2, core, lambda step: {"dp": sibling}),
        (4, x, lambda step: {"dp": x_peer(step)}),
        (4, z, lambda step: {"dp": z_peer(step)}),
        (parts, y, lambda step: {"db": lax.rem(y + step, parts)}),
    )

    def taps_copy(stage, d):
        count, at, peer = stages[stage]
        return remote(
            taps_now.at[stage],
            taps_in.at[stage, at],
            taps_send.at[stage, d - 1],
            taps_recv.at[stage, d - 1],
            peer(d),
        )

    def taps_start(stage, value):
        count, at, peer = stages[stage]
        taps_now[stage] = value
        taps_in[stage, at] = value
        for d in range(1, count):
            taps_copy(stage, d).start()

    def taps_end(stage):
        count = stages[stage][0]
        for d in range(1, count):
            taps_copy(stage, d).wait_recv()
        total = taps_in[stage, 0]
        for other in range(1, count):
            total = total + taps_in[stage, other]
        return total

    for d, h in order[:2]:
        pair_copy(d, h).start()
    for c in range(CHUNKS):
        far_copy(0, c).start()
        far_copy(1, c).start()
    for d, h in order[2:]:
        pair_copy(d, h).start()
    taps_start(0, taps_ref[...])
    for i in range(8):
        pair_sum(*order[i])
        if i < CHUNKS:
            forward(i)
    taps_start(1, taps_end(0))
    for c in range(CHUNKS):
        give_back(c)
        if c == 1:
            sum_first(0)
            sum_first(1)
            taps_start(2, taps_end(1))
        if c == 3:
            sum_second(0)
            sum_second(1)
            taps_start(3, taps_end(2))
        if c == 4:
            gather_first(0)
            gather_first(1)
    gather_pair(0)
    gather_pair(1)
    tsum_ref[...] = taps_end(3)

    for d, h in order:
        pair_gather(d, h, 1 - core).wait_recv()
        pair_gather(d, h, core).wait_send()
        pair_copy(d, h).wait_send()
        if d:
            first_copy(d, h).wait_send()
            second_copy(d, h).wait_send()
            second_gather(d, h, 0).wait_send()
            first_gather(d, h, 0).wait_send()
    for stage in range(4):
        for d in range(1, stages[stage][0]):
            taps_copy(stage, d).wait_send()
    for c in range(CHUNKS):
        for side in (0, 1):
            far_copy(side, c).wait_send()
            near_copy(side, c).wait_send()
        most = send.at[c, pl.ds(0, capacity * others)]
        pltpu.make_async_copy(most, most, back_send.at[c]).wait()
        most = back_ref.at[c, pl.ds(0, capacity * others)]
        pltpu.make_async_copy(most, most, back_recv.at[c]).wait()


def tail(wanted, part, weights, taps):
    owners = lax.axis_size("dp")
    parts = lax.axis_size("db")
    requests, quarter = part.shape[2], part.shape[3]
    slots = wanted.shape[0]
    vmem = pl.BlockSpec(memory_space=pltpu.VMEM)
    dma = pltpu.SemaphoreType.DMA
    heads = weights.shape[1]
    rows = ENC // 4
    weights = weights.reshape(2, heads, 4, rows, HD)
    both = (2, CHUNKS, requests, quarter, LANES)
    return pl.pallas_call(
        functools.partial(tail_kernel, owners, parts),
        in_specs=[pl.BlockSpec(memory_space=pltpu.SMEM), vmem, vmem, vmem],
        out_specs=[vmem, vmem, vmem],
        out_shape=[
            jax.ShapeDtypeStruct((CHUNKS, slots, quarter, LANES), BF16),
            jax.ShapeDtypeStruct(weights.shape, BF16),
            jax.ShapeDtypeStruct(taps.shape, F32),
        ],
        scratch_shapes=[
            pltpu.VMEM((2, CHUNKS, requests // 2, quarter, LANES), BF16),
            pltpu.VMEM(both, BF16),
            pltpu.VMEM(both, BF16),
            pltpu.VMEM((CHUNKS, slots, quarter, LANES), BF16),
            pltpu.VMEM((heads, 4, rows, HD), BF16),
            pltpu.VMEM((heads, 4, rows, HD), BF16),
            pltpu.VMEM((2, 3, 4, rows, HD), BF16),
            pltpu.VMEM((2, 4, rows, HD), BF16),
            pltpu.VMEM((2, 3, rows, HD), BF16),
            pltpu.VMEM((4, 4) + taps.shape, F32),
            pltpu.VMEM((4,) + taps.shape, F32),
            dma((2, CHUNKS)),
            dma((2, CHUNKS)),
            dma((2, CHUNKS)),
            dma((2, CHUNKS)),
            dma((CHUNKS,)),
            dma((CHUNKS,)),
            dma((2, 8)),
            dma((2, 8)),
            dma((4, 6)),
            dma((4, 6)),
            dma((4, 3)),
            dma((4, 3)),
        ]
        + [pltpu.VMEM((requests, quarter, LANES), BF16)] * CHUNKS,
        compiler_params=pltpu.CompilerParams(
            collective_id=1, has_side_effects=True, vmem_limit_bytes=48 * 1024 * 1024
        ),
        cost_estimate=pl.CostEstimate(flops=0, bytes_accessed=30_000_000, transcendentals=0),
    )(wanted, part, weights, taps)


def spread_kernel(rows_ref, back_ref, w_ref, states_ref, gkw_ref, gvw_ref):
    gkw_ref[...] = w_ref[0, 0].astype(F32)
    gvw_ref[...] = w_ref[1, 0].astype(F32)

    @pl.when(pl.program_id(0) < CHUNKS)
    def _():
        states_ref[...] = jnp.zeros_like(states_ref)

        def add(slot, carry):
            row = rows_ref[slot]

            @pl.when(row >= 0)
            def _():
                states_ref[row] += back_ref[0, slot].astype(F32)

            return carry

        lax.fori_loop(0, rows_ref.shape[0], add, 0)


def spread(rows, back, weights, blocks):
    heads = weights.shape[1]
    slots, quarter = back.shape[1], back.shape[2]
    last = CHUNKS - 1
    head_cols = pl.BlockSpec((ENC, HD), lambda i: (0, i))
    return pl.pallas_call(
        spread_kernel,
        grid=(max(heads, CHUNKS),),
        in_specs=[
            pl.BlockSpec(memory_space=pltpu.SMEM),
            pl.BlockSpec((1, slots, quarter, LANES), lambda i: (jnp.minimum(i, last), 0, 0, 0)),
            pl.BlockSpec((2, 1, ENC, HD), lambda i: (0, i, 0, 0)),
        ],
        out_specs=[
            pl.BlockSpec((blocks, quarter, LANES), lambda i: (0, 0, jnp.minimum(i, last))),
            head_cols,
            head_cols,
        ],
        out_shape=[
            jax.ShapeDtypeStruct((blocks, quarter, ENC), F32),
            jax.ShapeDtypeStruct((ENC, heads * HD), F32),
            jax.ShapeDtypeStruct((ENC, heads * HD), F32),
        ],
        compiler_params=pltpu.CompilerParams(
            dimension_semantics=("arbitrary",), vmem_limit_bytes=32 * 1024 * 1024
        ),
        cost_estimate=pl.CostEstimate(flops=0, bytes_accessed=19_000_000, transcendentals=0),
    )(rows, back, weights.reshape(2, heads, ENC, HD))


def shards(
    queries, cotangent, db_states, key_weight, value_weight, conv_kernel, nbr_owner, nbr_row
):
    owners = lax.axis_size("dp")
    span_count = nbr_owner.shape[0]
    request_count = span_count * NBR
    capacity = max(2, (request_count + owners - 1) // owners)
    quarter = db_states.shape[1]
    local_blocks = db_states.shape[0]
    slots_total = owners * capacity
    owner_flat = nbr_owner.reshape(request_count)
    row_flat = nbr_row.reshape(request_count)
    positions = jnp.arange(request_count, dtype=jnp.int32)
    same_owner = owner_flat[:, None] == owner_flat[None, :]
    earlier = positions[:, None] > positions[None, :]
    slot_index = jnp.sum(jnp.logical_and(same_owner, earlier).astype(jnp.int32), axis=1)
    target = owner_flat * capacity + slot_index
    slot_hits = target[:, None] == jnp.arange(slots_total, dtype=jnp.int32)[None, :]
    used_slot = jnp.any(slot_hits, axis=0)
    row_sent = jnp.sum(jnp.where(slot_hits, row_flat[:, None], 0), axis=0)
    row_table = jnp.where(used_slot, row_sent, -1).reshape(owners, capacity)
    wanted = jnp.sum(jnp.where(slot_hits, positions[:, None], 0), axis=0)
    table = jnp.pad(row_table[:, None, :], ((0, 0), (0, 0), (0, LANES - capacity)))
    raw, asked = fetch(target, table, db_states)
    asked_flat = asked[:, 0, :capacity].reshape(slots_total)
    attended, grad_query, part, weight_terms, taps_term = core(
        queries, cotangent, raw, key_weight, value_weight, conv_kernel
    )
    taps_term = jnp.pad(taps_term, ((0, 8 - KW), (0, 0)))
    back, weight_sums, taps_sum = tail(wanted, part, weight_terms, taps_term)
    grad_states, grad_key_weight, grad_value_weight = spread(
        asked_flat, back, weight_sums, local_blocks
    )
    return (
        attended,
        grad_query,
        grad_states,
        grad_key_weight,
        grad_value_weight,
        taps_sum[:KW],
    )


def solution(mesh):
    return jax.shard_map(
        shards,
        mesh=mesh,
        in_specs=(
            P("dp", "db"),
            P("dp", "db"),
            P("dp", "db", None),
            P(None, "db"),
            P(None, "db"),
            P(),
            P("dp", None),
            P("dp", None),
        ),
        out_specs=(
            P("dp", "db"),
            P("dp", "db"),
            P("dp", "db", None),
            P(None, "db"),
            P(None, "db"),
            P(),
        ),
        check_vma=False,
    )
```

```python
import functools
import math

import jax
import jax.numpy as jnp
from jax import lax
from jax.experimental import pallas as pl
from jax.experimental.pallas import tpu as pltpu
from jax.sharding import PartitionSpec as P

HD = 128
ENC = 896
SPAN = 64
NBR = 2
NLEN = 128
KW = 3
LANES = 128
CHUNKS = ENC // LANES
F32 = jnp.float32
BF16 = jnp.bfloat16
NT = (((1,), (1,)), ((), ()))


def shifted(block):
    rows = block.shape[0]
    at = lax.broadcasted_iota(jnp.int32, block.shape, 0)
    down = jnp.where(at == 0, 0.0, pltpu.roll(block, 1, 0))
    up = jnp.where(at == rows - 1, 0.0, pltpu.roll(block, rows - 1, 0))
    return down, up


def core_kernel(
    heads,
    q_ref,
    g_ref,
    raw_ref,
    kw_ref,
    vw_ref,
    taps_ref,
    att_ref,
    gq_ref,
    grads_ref,
    mixed_ref,
    mixed_s,
    kv_s,
    both_s,
    stacked_s,
):
    scale = 1.0 / math.sqrt(HD)
    for c in range(CHUNKS):
        cols = slice(c * LANES, (c + 1) * LANES)
        for n in range(NBR):
            raw = raw_ref[c, :, n].reshape(NLEN, LANES).astype(F32)
            down, up = shifted(raw)
            mixed = taps_ref[0:1, cols] * down
            mixed = mixed + taps_ref[1:2, cols] * raw
            mixed = mixed + taps_ref[2:3, cols] * up
            mixed_s[n * NLEN : (n + 1) * NLEN, cols] = mixed.astype(BF16)
    mixed = mixed_s[...]
    mixed_ref[...] = mixed.T

    zeros = jnp.zeros((SPAN, HD), BF16)
    for place, weight in enumerate((kw_ref, vw_ref)):
        states = jnp.dot(mixed, weight[...], preferred_element_type=F32).astype(BF16)
        for h in range(heads):
            at = (2 * h + place) * HD
            kv_s[:, at : at + HD] = states[:, h * HD : (h + 1) * HD]

    def diag(h):
        q = q_ref[:, h * HD : (h + 1) * HD]
        g = g_ref[:, h * HD : (h + 1) * HD]
        return jnp.concatenate(
            [jnp.concatenate([q, zeros], axis=1), jnp.concatenate([zeros, g], axis=1)], axis=0
        )

    for h in range(heads):
        wide = slice(2 * h * HD, (2 * h + 2) * HD)
        both_s[h] = lax.dot_general(diag(h), kv_s[:, wide], NT, preferred_element_type=F32)
    for h in range(heads):
        scores = both_s[h, :SPAN] * scale
        grad_probs = both_s[h, SPAN:]
        expo = jnp.exp(scores - jnp.max(scores, axis=-1, keepdims=True))
        probs = expo / jnp.sum(expo, axis=-1, keepdims=True)
        inner = jnp.sum(grad_probs * probs, axis=-1, keepdims=True)
        grad_scores = scale * probs * (grad_probs - inner)
        stacked_s[h, :SPAN] = grad_scores.astype(BF16)
        stacked_s[h, SPAN:] = probs.astype(BF16)
    for h in range(heads):
        wide = slice(2 * h * HD, (2 * h + 2) * HD)
        cols = slice(h * HD, (h + 1) * HD)
        out = jnp.dot(stacked_s[h], kv_s[:, wide], preferred_element_type=F32)
        gq_ref[:, cols] = out[:SPAN, :HD].astype(BF16)
        att_ref[:, cols] = out[SPAN:, HD:].astype(BF16)
    for h in range(heads):
        cols = slice(h * HD, (h + 1) * HD)
        pair = lax.dot_general(
            stacked_s[h], diag(h), (((0,), (0,)), ((), ())), preferred_element_type=F32
        ).astype(BF16)
        grads_ref[0, :, cols] = pair[:, :HD]
        grads_ref[1, :, cols] = pair[:, HD:]


def core(queries, cotangent, raw, key_weight, value_weight, conv_kernel):
    tokens, width = queries.shape
    heads = width // HD
    spans = tokens // SPAN
    keys_here = NBR * NLEN
    keys_all = spans * keys_here
    whole = lambda shape: pl.BlockSpec(
        shape, lambda i: (0,) * len(shape), pipeline_mode=pl.Buffered(1)
    )
    span_rows = pl.BlockSpec((SPAN, width), lambda i: (i, 0))
    parts, quarter = raw.shape[1], raw.shape[3]
    blocks = pl.BlockSpec((CHUNKS, parts, NBR, quarter, LANES), lambda i: (0, 0, i, 0, 0))
    return pl.pallas_call(
        functools.partial(core_kernel, heads),
        grid=(spans,),
        in_specs=[
            span_rows,
            span_rows,
            blocks,
            whole((ENC, width)),
            whole((ENC, width)),
            whole((KW, ENC)),
        ],
        out_specs=[
            span_rows,
            span_rows,
            pl.BlockSpec((2, keys_here, width), lambda i: (0, i, 0)),
            pl.BlockSpec((ENC, keys_here), lambda i: (0, i)),
        ],
        out_shape=[
            jax.ShapeDtypeStruct((tokens, width), BF16),
            jax.ShapeDtypeStruct((tokens, width), BF16),
            jax.ShapeDtypeStruct((2, keys_all, width), BF16),
            jax.ShapeDtypeStruct((ENC, keys_all), BF16),
        ],
        scratch_shapes=[
            pltpu.VMEM((keys_here, ENC), BF16),
            pltpu.VMEM((keys_here, 2 * width), BF16),
            pltpu.VMEM((heads, 2 * SPAN, keys_here), F32),
            pltpu.VMEM((heads, 2 * SPAN, keys_here), BF16),
        ],
        compiler_params=pltpu.CompilerParams(
            dimension_semantics=("arbitrary",), vmem_limit_bytes=40 * 1024 * 1024
        ),
        cost_estimate=pl.CostEstimate(
            flops=10_000_000_000, bytes_accessed=30_000_000, transcendentals=1_200_000
        ),
    )(queries, cotangent, raw, key_weight, value_weight, conv_kernel)


def dp_peer(step):
    me = lax.axis_index("dp")
    z = lax.rem(me // 8 + step // 8, 4)
    x = lax.rem(lax.rem(me // 2, 4) + lax.rem(step // 2, 4), 4)
    return z * 8 + x * 2 + lax.rem(me + step, 2)


def fetch_kernel(
    owners,
    parts,
    slot_ref,
    table_ref,
    states_ref,
    raw_ref,
    asked_ref,
    asked_s,
    send,
    ask_sem,
    local_sem,
    send_sem,
    recv_sem,
    y_send,
    y_recv,
    *recv,
):
    me = lax.axis_index("dp")
    y = lax.axis_index("db")
    right = lax.rem(y + 1, parts)
    left = lax.rem(y + parts - 1, parts)
    requests = raw_ref.shape[2]
    half = requests // 2
    capacity = 2
    others = owners - 1

    barrier = pltpu.get_barrier_semaphore()

    def greet(step, carry):
        pl.semaphore_signal(barrier, inc=1, device_id={"dp": dp_peer(step)})
        return carry

    lax.fori_loop(1, owners, greet, 0)
    for side in (left, right):
        pl.semaphore_signal(barrier, inc=1, device_id={"db": side})
    pl.semaphore_wait(barrier, others + 2)

    def ask(step, carry):
        peer = dp_peer(step)
        pltpu.make_async_remote_copy(
            src_ref=table_ref.at[peer],
            dst_ref=asked_ref.at[me],
            send_sem=ask_sem.at[0],
            recv_sem=ask_sem.at[1],
            device_id={"dp": peer},
        ).start()
        return carry

    lax.fori_loop(1, owners, ask, 0)
    asked_ref[me] = table_ref[me]
    most = asked_ref.at[pl.ds(0, others)]
    pltpu.make_async_copy(most, most, ask_sem.at[1]).wait()
    pltpu.make_async_copy(asked_ref, asked_s, local_sem).start()
    pltpu.make_async_copy(asked_ref, asked_s, local_sem).wait()

    for c in range(CHUNKS):
        cols = slice(c * LANES, (c + 1) * LANES)

        def reply(step, carry):
            peer = dp_peer(step)
            for k in range(capacity):
                row = jnp.maximum(asked_s[peer, 0, k], 0)
                send[c, capacity * peer + k] = states_ref[row, :, cols]
            pltpu.make_async_remote_copy(
                src_ref=send.at[c, pl.ds(capacity * peer, capacity)],
                dst_ref=recv[c].at[pl.ds(capacity * me, capacity)],
                send_sem=send_sem.at[c],
                recv_sem=recv_sem.at[c],
                device_id={"dp": peer},
            ).start()
            return carry

        lax.fori_loop(1, owners, reply, 0)
        for k in range(capacity):
            row = jnp.maximum(asked_s[me, 0, k], 0)
            recv[c][capacity * me + k] = states_ref[row, :, cols]

    def along_y(kind, c, part, rows, side):
        block = raw_ref.at[c, part, rows]
        return pltpu.make_async_remote_copy(
            src_ref=block,
            dst_ref=block,
            send_sem=y_send.at[kind, c],
            recv_sem=y_recv.at[kind, c],
            device_id={"db": side},
        )

    everything, low, high = pl.ds(0, requests), pl.ds(0, half), pl.ds(half, requests - half)

    def arrivals(kind, c):
        far = lax.rem(y + 2, parts)
        part, rows = ((left, everything), (right, everything), (far, low), (far, high))[kind]
        return along_y(kind, c, part, rows, right)

    for c in range(CHUNKS + 1):
        if c < CHUNKS:
            most = recv[c].at[pl.ds(0, capacity * others)]
            pltpu.make_async_copy(most, most, recv_sem.at[c]).wait()
            for p in range(requests):
                raw_ref[c, y, p] = recv[c][slot_ref[p]]
            along_y(0, c, y, everything, right).start()
            along_y(1, c, y, everything, left).start()
        if c >= 1:
            arrivals(0, c - 1).wait_recv()
            along_y(2, c - 1, left, low, right).start()
            arrivals(1, c - 1).wait_recv()
            along_y(3, c - 1, right, high, left).start()
    for c in range(CHUNKS):
        arrivals(2, c).wait_recv()
        arrivals(3, c).wait_recv()
        along_y(0, c, y, everything, right).wait_send()
        along_y(1, c, y, everything, left).wait_send()
        along_y(2, c, left, low, right).wait_send()
        along_y(3, c, right, high, left).wait_send()
        most = send.at[c, pl.ds(0, capacity * others)]
        pltpu.make_async_copy(most, most, send_sem.at[c]).wait()
    most = table_ref.at[pl.ds(0, others)]
    pltpu.make_async_copy(most, most, ask_sem.at[0]).wait()


def fetch(slots, table, states):
    owners = table.shape[0]
    parts = lax.axis_size("db")
    requests = slots.shape[0]
    quarter = states.shape[1]
    vmem = pl.BlockSpec(memory_space=pltpu.VMEM)
    dma = pltpu.SemaphoreType.DMA
    return pl.pallas_call(
        functools.partial(fetch_kernel, owners, parts),
        in_specs=[pl.BlockSpec(memory_space=pltpu.SMEM), vmem, vmem],
        out_specs=[vmem, vmem],
        out_shape=[
            jax.ShapeDtypeStruct((CHUNKS, parts, requests, quarter, LANES), BF16),
            jax.ShapeDtypeStruct(table.shape, jnp.int32),
        ],
        scratch_shapes=[
            pltpu.SMEM(table.shape, jnp.int32),
            pltpu.VMEM((CHUNKS, 2 * owners, quarter, LANES), BF16),
            dma((2,)),
            dma,
            dma((CHUNKS,)),
            dma((CHUNKS,)),
            dma((4, CHUNKS)),
            dma((4, CHUNKS)),
        ]
        + [pltpu.VMEM((2 * owners, quarter, LANES), BF16)] * CHUNKS,
        compiler_params=pltpu.CompilerParams(
            collective_id=0, has_side_effects=True, vmem_limit_bytes=40 * 1024 * 1024
        ),
        cost_estimate=pl.CostEstimate(flops=0, bytes_accessed=16_000_000, transcendentals=0),
    )(slots, table, states)


def tail_kernel(
    owners,
    parts,
    req_ref,
    conv_ref,
    grads_hbm,
    mixed_hbm,
    raw_hbm,
    kw_hbm,
    vw_hbm,
    back_ref,
    wsum_ref,
    tsum_ref,
    grads,
    mixed_t,
    raw_ref,
    kw_ref,
    vw_ref,
    part_ref,
    w_ref,
    taps_acc,
    load_sem,
    grads_sem,
    from_far,
    onward,
    from_near,
    send,
    sibling_w,
    pair_w,
    first_in,
    first_sum,
    second_in,
    taps_in,
    taps_now,
    far_send,
    far_recv,
    near_send,
    near_recv,
    back_send,
    back_recv,
    pair_send,
    pair_recv,
    axis_send,
    axis_recv,
    taps_send,
    taps_recv,
    *mine,
):
    me = lax.axis_index("dp")
    y = lax.axis_index("db")
    z, x, core = me // 8, lax.rem(me // 2, 4), lax.rem(me, 2)
    sibling = me + 1 - 2 * core
    right = lax.rem(y + 1, parts)
    left = lax.rem(y + parts - 1, parts)
    far = lax.rem(y + 2, parts)
    requests = part_ref.shape[2]
    keys_here = NBR * NLEN
    spans = requests // NBR

    def load(index):
        pair = ((kw_hbm, kw_ref), (vw_hbm, vw_ref), (raw_hbm, raw_ref), (mixed_hbm, mixed_t))[index]
        return pltpu.make_async_copy(*pair, load_sem.at[index])

    def load_grads(span):
        rows = pl.ds(pl.multiple_of(span * keys_here, keys_here), keys_here)
        return pltpu.make_async_copy(
            grads_hbm.at[:, rows], grads.at[:, rows], grads_sem.at[span]
        )

    load(0).start()
    load(1).start()
    load_grads(0).start()
    load(2).start()
    for span in range(1, spans):
        load_grads(span).start()
    load(3).start()
    taps_acc[...] = jnp.zeros_like(taps_acc)
    half = requests // 2
    capacity = 2
    others = owners - 1
    low, high = pl.ds(0, half), pl.ds(half, requests - half)

    def x_peer(step):
        return z * 8 + lax.rem(x + step, 4) * 2 + core

    def z_peer(step):
        return lax.rem(z + step, 4) * 8 + x * 2 + core

    barrier = pltpu.get_barrier_semaphore()

    def greet(step, carry):
        pl.semaphore_signal(barrier, inc=1, device_id={"dp": dp_peer(step)})
        return carry

    lax.fori_loop(1, owners, greet, 0)
    for other in range(1, parts):
        pl.semaphore_signal(barrier, inc=1, device_id={"db": lax.rem(y + other, parts)})
    pl.semaphore_wait(barrier, others + parts - 1)

    def remote(src, dst, send_sem, recv_sem, where):
        return pltpu.make_async_remote_copy(
            src_ref=src, dst_ref=dst, send_sem=send_sem, recv_sem=recv_sem, device_id=where
        )

    def grad_columns(chunks, first):
        cols = slice(chunks[0] * LANES, (chunks[-1] + 1) * LANES)

        def one(span, carry):
            if first:
                load_grads(span).wait()
            rows = pl.ds(pl.multiple_of(span * keys_here, keys_here), keys_here)
            whole = lax.dot_general(
                grads[0, rows], kw_ref[cols], NT, preferred_element_type=F32
            ) + lax.dot_general(grads[1, rows], vw_ref[cols], NT, preferred_element_type=F32)
            for i, c in enumerate(chunks):
                lanes = slice(c * LANES, (c + 1) * LANES)
                for n in range(NBR):
                    gm = whole[n * NLEN : (n + 1) * NLEN, i * LANES : (i + 1) * LANES]
                    gm_down, gm_up = shifted(gm)
                    grad = conv_ref[0:1, lanes] * gm_up
                    grad = grad + conv_ref[1:2, lanes] * gm
                    grad = grad + conv_ref[2:3, lanes] * gm_down
                    part_ref[c, :, span * NBR + n] = grad.astype(BF16).reshape(parts, -1, LANES)
                    raw = raw_ref[c, :, span * NBR + n].reshape(NLEN, LANES).astype(F32)
                    for w, other in enumerate((gm_up, gm, gm_down)):
                        taps_acc[w, :, lanes] += jnp.sum(
                            (raw * other).reshape(NLEN // 8, 8, LANES), axis=0
                        )
            return carry

        lax.fori_loop(0, spans, one, 0)

    def weight_terms(which, pair):
        wide = pl.ds(pair * 2 * HD, 2 * HD)
        term = jnp.dot(mixed_t[...], grads[which, :, wide], preferred_element_type=F32)
        for i in (0, 1):
            block = term[:, i * HD : (i + 1) * HD].astype(BF16)
            w_ref[which, 2 * pair + i] = block.reshape(4, -1, HD)

    def far_copy(side, c):
        rows, to = ((low, right), (high, left))[side]
        return remote(
            part_ref.at[c, far, rows],
            from_far.at[side, c],
            far_send.at[side, c],
            far_recv.at[side, c],
            {"db": to},
        )

    def near_copy(side, c):
        return remote(
            onward.at[side, c],
            from_near.at[side, c],
            near_send.at[side, c],
            near_recv.at[side, c],
            {"db": (right, left)[side]},
        )

    def forward(c):
        far_copy(0, c).wait_recv()
        added = part_ref[c, right, 0:half].astype(F32) + from_far[0, c].astype(F32)
        onward[0, c, 0:half] = added.astype(BF16)
        onward[0, c, half:requests] = part_ref[c, right, half:requests]
        near_copy(0, c).start()
        far_copy(1, c).wait_recv()
        added = part_ref[c, left, half:requests].astype(F32) + from_far[1, c].astype(F32)
        onward[1, c, half:requests] = added.astype(BF16)
        onward[1, c, 0:half] = part_ref[c, left, 0:half]
        near_copy(1, c).start()

    def give_back(c):
        near_copy(0, c).wait_recv()
        near_copy(1, c).wait_recv()
        total = part_ref[c, y].astype(F32) + from_near[0, c].astype(F32)
        mine[c][...] = (total + from_near[1, c].astype(F32)).astype(BF16)

        def one(step, carry):
            peer = dp_peer(step)
            for k in range(capacity):
                send[c, capacity * peer + k] = mine[c][req_ref[capacity * peer + k]]
            remote(
                send.at[c, pl.ds(capacity * peer, capacity)],
                back_ref.at[c, pl.ds(capacity * me, capacity)],
                back_send.at[c],
                back_recv.at[c],
                {"dp": peer},
            ).start()
            return carry

        lax.fori_loop(1, owners, one, 0)
        for k in range(capacity):
            back_ref[c, capacity * me + k] = mine[c][req_ref[capacity * me + k]]

    first_at, second_at = (x, z), (z, x)
    first_peer, second_peer = (x_peer, z_peer), (z_peer, x_peer)
    order = [(d, h) for d in (1, 2, 3, 0) for h in (0, 1)]

    def group(h, step):
        return h * 4 + lax.rem(first_at[h] + step, 4)

    def pair_copy(g):
        return remote(
            w_ref.at[1 - core, g],
            sibling_w.at[g],
            pair_send.at[0, g],
            pair_recv.at[0, g],
            {"dp": sibling},
        )

    def first_copy(d, h):
        return remote(
            pair_w.at[group(h, d)],
            first_in.at[h, d - 1],
            axis_send.at[0, h * 3 + d - 1],
            axis_recv.at[0, h * 3 + d - 1],
            {"dp": first_peer[h](d)},
        )

    def second_copy(d, h):
        return remote(
            first_sum.at[h, lax.rem(second_at[h] + d, 4)],
            second_in.at[h, d - 1],
            axis_send.at[1, h * 3 + d - 1],
            axis_recv.at[1, h * 3 + d - 1],
            {"dp": second_peer[h](d)},
        )

    def second_gather(d, h, back):
        block = wsum_ref.at[core, group(h, 0), lax.rem(second_at[h] + back, 4)]
        return remote(
            block,
            block,
            axis_send.at[2, h * 3 + d - 1],
            axis_recv.at[2, h * 3 + d - 1],
            {"dp": second_peer[h](d)},
        )

    def first_gather(d, h, back):
        block = wsum_ref.at[core, group(h, back)]
        return remote(
            block,
            block,
            axis_send.at[3, h * 3 + d - 1],
            axis_recv.at[3, h * 3 + d - 1],
            {"dp": first_peer[h](d)},
        )

    def pair_gather(d, h, which):
        block = wsum_ref.at[which, group(h, 4 - d)]
        return remote(
            block,
            block,
            pair_send.at[1, h * 4 + d],
            pair_recv.at[1, h * 4 + d],
            {"dp": sibling},
        )

    def pair_sum(d, h):
        g = group(h, d)
        pair_w[g] = (w_ref[core, g].astype(F32) + sibling_w[g].astype(F32)).astype(BF16)
        if d:
            first_copy(d, h).start()

    def sum_first(h):
        for d in (1, 2, 3):
            first_copy(d, h).wait_recv()
        total = pair_w[group(h, 0)].astype(F32)
        for d in (1, 2, 3):
            total = total + first_in[h, d - 1].astype(F32)
        first_sum[h] = total.astype(BF16)
        for d in (1, 2, 3):
            second_copy(d, h).start()

    def sum_second(h):
        for d in (1, 2, 3):
            second_copy(d, h).wait_recv()
        total = first_sum[h, second_at[h]].astype(F32)
        for d in (1, 2, 3):
            total = total + second_in[h, d - 1].astype(F32)
        wsum_ref[core, group(h, 0), second_at[h]] = total.astype(BF16)
        for d in (1, 2, 3):
            second_gather(d, h, 0).start()

    def gather_first(h):
        for d in (1, 2, 3):
            second_gather(d, h, 4 - d).wait_recv()
        for d in (1, 2, 3):
            first_gather(d, h, 0).start()
        pair_gather(0, h, core).start()

    def gather_pair(h):
        for d in (1, 2, 3):
            first_gather(d, h, 4 - d).wait_recv()
            pair_gather(d, h, core).start()

    stages = (
        (2, core, lambda step: {"dp": sibling}),
        (4, x, lambda step: {"dp": x_peer(step)}),
        (4, z, lambda step: {"dp": z_peer(step)}),
        (parts, y, lambda step: {"db": lax.rem(y + step, parts)}),
    )

    def taps_copy(stage, d):
        count, at, peer = stages[stage]
        return remote(
            taps_now.at[stage],
            taps_in.at[stage, at],
            taps_send.at[stage, d - 1],
            taps_recv.at[stage, d - 1],
            peer(d),
        )

    def taps_start(stage, value):
        count, at, peer = stages[stage]
        taps_now[stage] = value
        taps_in[stage, at] = value
        for d in range(1, count):
            taps_copy(stage, d).start()

    def taps_end(stage):
        count = stages[stage][0]
        for d in range(1, count):
            taps_copy(stage, d).wait_recv()
        total = taps_in[stage, 0]
        for other in range(1, count):
            total = total + taps_in[stage, other]
        return total

    load(0).wait()
    load(1).wait()
    load(2).wait()
    grad_columns((0, 1), True)
    for c in (0, 1):
        far_copy(0, c).start()
        far_copy(1, c).start()
    load(3).wait()
    for pair in range(4):
        weight_terms(1 - core, pair)
        pair_copy(2 * pair).start()
        pair_copy(2 * pair + 1).start()
        if pair in (1, 2):
            forward(pair - 1)
    for pair in range(4):
        weight_terms(core, pair)
        if pair in (1, 3):
            give_back(pair // 2)
    for g in range(8):
        pair_copy(g).wait_recv()
    for d, h in order:
        pair_sum(d, h)
    grad_columns((2, 3), False)
    for c in (2, 3):
        far_copy(0, c).start()
        far_copy(1, c).start()
    grad_columns((4, 5), False)
    for c in (4, 5):
        far_copy(0, c).start()
        far_copy(1, c).start()
    forward(2)
    forward(3)
    sum_first(0)
    sum_first(1)
    grad_columns((6,), False)
    far_copy(0, 6).start()
    far_copy(1, 6).start()
    taps_start(0, jnp.sum(taps_acc[...], axis=1))
    give_back(2)
    forward(4)
    forward(5)
    sum_second(0)
    sum_second(1)
    give_back(3)
    forward(6)
    taps_start(1, taps_end(0))
    gather_first(0)
    gather_first(1)
    give_back(4)
    taps_start(2, taps_end(1))
    give_back(5)
    taps_start(3, taps_end(2))
    give_back(6)
    gather_pair(0)
    gather_pair(1)
    tsum_ref[...] = taps_end(3)

    for d, h in order:
        pair_gather(d, h, 1 - core).wait_recv()
        pair_gather(d, h, core).wait_send()
        pair_copy(h * 4 + d).wait_send()
        if d:
            first_copy(d, h).wait_send()
            second_copy(d, h).wait_send()
            second_gather(d, h, 0).wait_send()
            first_gather(d, h, 0).wait_send()
    for stage in range(4):
        for d in range(1, stages[stage][0]):
            taps_copy(stage, d).wait_send()
    for c in range(CHUNKS):
        for side in (0, 1):
            far_copy(side, c).wait_send()
            near_copy(side, c).wait_send()
        most = send.at[c, pl.ds(0, capacity * others)]
        pltpu.make_async_copy(most, most, back_send.at[c]).wait()
        most = back_ref.at[c, pl.ds(0, capacity * others)]
        pltpu.make_async_copy(most, most, back_recv.at[c]).wait()


def tail(wanted, conv_kernel, grads, mixed, raw, key_weight, value_weight):
    owners = lax.axis_size("dp")
    parts = lax.axis_size("db")
    requests, quarter = raw.shape[2], raw.shape[3]
    slots = wanted.shape[0]
    vmem = pl.BlockSpec(memory_space=pltpu.VMEM)
    anywhere = pl.BlockSpec(memory_space=pl.ANY)
    dma = pltpu.SemaphoreType.DMA
    heads = key_weight.shape[1] // HD
    rows = ENC // 4
    weights = (2, heads, 4, rows, HD)
    taps = (8, ENC)
    both = (2, CHUNKS, requests, quarter, LANES)
    return pl.pallas_call(
        functools.partial(tail_kernel, owners, parts),
        in_specs=[pl.BlockSpec(memory_space=pltpu.SMEM), vmem] + [anywhere] * 5,
        out_specs=[vmem, vmem, vmem],
        out_shape=[
            jax.ShapeDtypeStruct((CHUNKS, slots, quarter, LANES), BF16),
            jax.ShapeDtypeStruct(weights, BF16),
            jax.ShapeDtypeStruct(taps, F32),
        ],
        scratch_shapes=[
            pltpu.VMEM(grads.shape, BF16),
            pltpu.VMEM(mixed.shape, BF16),
            pltpu.VMEM(raw.shape, BF16),
            pltpu.VMEM(key_weight.shape, BF16),
            pltpu.VMEM(value_weight.shape, BF16),
            pltpu.VMEM(raw.shape, BF16),
            pltpu.VMEM(weights, BF16),
            pltpu.VMEM((8, 8, ENC), F32),
            dma((4,)),
            dma((requests // NBR,)),
            pltpu.VMEM((2, CHUNKS, requests // 2, quarter, LANES), BF16),
            pltpu.VMEM(both, BF16),
            pltpu.VMEM(both, BF16),
            pltpu.VMEM((CHUNKS, slots, quarter, LANES), BF16),
            pltpu.VMEM((heads, 4, rows, HD), BF16),
            pltpu.VMEM((heads, 4, rows, HD), BF16),
            pltpu.VMEM((2, 3, 4, rows, HD), BF16),
            pltpu.VMEM((2, 4, rows, HD), BF16),
            pltpu.VMEM((2, 3, rows, HD), BF16),
            pltpu.VMEM((4, 4) + taps, F32),
            pltpu.VMEM((4,) + taps, F32),
            dma((2, CHUNKS)),
            dma((2, CHUNKS)),
            dma((2, CHUNKS)),
            dma((2, CHUNKS)),
            dma((CHUNKS,)),
            dma((CHUNKS,)),
            dma((2, 8)),
            dma((2, 8)),
            dma((4, 6)),
            dma((4, 6)),
            dma((4, 3)),
            dma((4, 3)),
        ]
        + [pltpu.VMEM((requests, quarter, LANES), BF16)] * CHUNKS,
        compiler_params=pltpu.CompilerParams(
            collective_id=1, has_side_effects=True, vmem_limit_bytes=60 * 1024 * 1024
        ),
        cost_estimate=pl.CostEstimate(
            flops=17_000_000_000, bytes_accessed=30_000_000, transcendentals=0
        ),
    )(wanted, conv_kernel, grads, mixed, raw, key_weight, value_weight)


def spread_kernel(rows_ref, back_ref, w_ref, states_ref, gkw_ref, gvw_ref):
    gkw_ref[...] = w_ref[0, 0].astype(F32)
    gvw_ref[...] = w_ref[1, 0].astype(F32)

    @pl.when(pl.program_id(0) < CHUNKS)
    def _():
        states_ref[...] = jnp.zeros_like(states_ref)

        def add(slot, carry):
            row = rows_ref[slot]

            @pl.when(row >= 0)
            def _():
                states_ref[row] += back_ref[0, slot].astype(F32)

            return carry

        lax.fori_loop(0, rows_ref.shape[0], add, 0)


def spread(rows, back, weights, blocks):
    heads = weights.shape[1]
    slots, quarter = back.shape[1], back.shape[2]
    last = CHUNKS - 1
    head_cols = pl.BlockSpec((ENC, HD), lambda i: (0, i))
    return pl.pallas_call(
        spread_kernel,
        grid=(max(heads, CHUNKS),),
        in_specs=[
            pl.BlockSpec(memory_space=pltpu.SMEM),
            pl.BlockSpec((1, slots, quarter, LANES), lambda i: (jnp.minimum(i, last), 0, 0, 0)),
            pl.BlockSpec((2, 1, ENC, HD), lambda i: (0, i, 0, 0)),
        ],
        out_specs=[
            pl.BlockSpec((blocks, quarter, LANES), lambda i: (0, 0, jnp.minimum(i, last))),
            head_cols,
            head_cols,
        ],
        out_shape=[
            jax.ShapeDtypeStruct((blocks, quarter, ENC), F32),
            jax.ShapeDtypeStruct((ENC, heads * HD), F32),
            jax.ShapeDtypeStruct((ENC, heads * HD), F32),
        ],
        compiler_params=pltpu.CompilerParams(
            dimension_semantics=("arbitrary",), vmem_limit_bytes=32 * 1024 * 1024
        ),
        cost_estimate=pl.CostEstimate(flops=0, bytes_accessed=19_000_000, transcendentals=0),
    )(rows, back, weights.reshape(2, heads, ENC, HD))


def shards(
    queries, cotangent, db_states, key_weight, value_weight, conv_kernel, nbr_owner, nbr_row
):
    owners = lax.axis_size("dp")
    span_count = nbr_owner.shape[0]
    request_count = span_count * NBR
    capacity = max(2, (request_count + owners - 1) // owners)
    quarter = db_states.shape[1]
    local_blocks = db_states.shape[0]
    slots_total = owners * capacity
    owner_flat = nbr_owner.reshape(request_count)
    row_flat = nbr_row.reshape(request_count)
    positions = jnp.arange(request_count, dtype=jnp.int32)
    same_owner = owner_flat[:, None] == owner_flat[None, :]
    earlier = positions[:, None] > positions[None, :]
    slot_index = jnp.sum(jnp.logical_and(same_owner, earlier).astype(jnp.int32), axis=1)
    target = owner_flat * capacity + slot_index
    slot_hits = target[:, None] == jnp.arange(slots_total, dtype=jnp.int32)[None, :]
    used_slot = jnp.any(slot_hits, axis=0)
    row_sent = jnp.sum(jnp.where(slot_hits, row_flat[:, None], 0), axis=0)
    row_table = jnp.where(used_slot, row_sent, -1).reshape(owners, capacity)
    wanted = jnp.sum(jnp.where(slot_hits, positions[:, None], 0), axis=0)
    table = jnp.pad(row_table[:, None, :], ((0, 0), (0, 0), (0, LANES - capacity)))
    raw, asked = fetch(target, table, db_states)
    asked_flat = asked[:, 0, :capacity].reshape(slots_total)
    attended, grad_query, grads, mixed = core(
        queries, cotangent, raw, key_weight, value_weight, conv_kernel
    )
    back, weight_sums, taps_sum = tail(
        wanted, conv_kernel, grads, mixed, raw, key_weight, value_weight
    )
    grad_states, grad_key_weight, grad_value_weight = spread(
        asked_flat, back, weight_sums, local_blocks
    )
    return (
        attended,
        grad_query,
        grad_states,
        grad_key_weight,
        grad_value_weight,
        taps_sum[:KW],
    )


def solution(mesh):
    return jax.shard_map(
        shards,
        mesh=mesh,
        in_specs=(
            P("dp", "db"),
            P("dp", "db"),
            P("dp", "db", None),
            P(None, "db"),
            P(None, "db"),
            P(),
            P("dp", None),
            P("dp", None),
        ),
        out_specs=(
            P("dp", "db"),
            P("dp", "db"),
            P("dp", "db", None),
            P(None, "db"),
            P(None, "db"),
            P(),
        ),
        check_vma=False,
    )
```

```python
import functools
import math

import jax
import jax.numpy as jnp
from jax import lax
from jax.experimental import pallas as pl
from jax.experimental.pallas import tpu as pltpu
from jax.sharding import PartitionSpec as P

HD = 128
ENC = 896
SPAN = 64
NBR = 2
NLEN = 128
KW = 3
LANES = 128
CHUNKS = ENC // LANES
F32 = jnp.float32
BF16 = jnp.bfloat16
NT = (((1,), (1,)), ((), ()))


def shifted(block):
    rows = block.shape[0]
    at = lax.broadcasted_iota(jnp.int32, block.shape, 0)
    down = jnp.where(at == 0, 0.0, pltpu.roll(block, 1, 0))
    up = jnp.where(at == rows - 1, 0.0, pltpu.roll(block, rows - 1, 0))
    return down, up


def core_kernel(
    heads,
    q_ref,
    g_ref,
    raw_ref,
    kw_ref,
    vw_ref,
    taps_ref,
    att_ref,
    gq_ref,
    grads_ref,
    mixed_ref,
    mixed_s,
    kv_s,
    both_s,
    stacked_s,
):
    scale = 1.0 / math.sqrt(HD)
    for c in range(CHUNKS):
        cols = slice(c * LANES, (c + 1) * LANES)
        for n in range(NBR):
            raw = raw_ref[c, :, n].reshape(NLEN, LANES).astype(F32)
            down, up = shifted(raw)
            mixed = taps_ref[0:1, cols] * down
            mixed = mixed + taps_ref[1:2, cols] * raw
            mixed = mixed + taps_ref[2:3, cols] * up
            mixed_s[n * NLEN : (n + 1) * NLEN, cols] = mixed.astype(BF16)
    mixed = mixed_s[...]
    mixed_ref[...] = mixed.T

    zeros = jnp.zeros((SPAN, HD), BF16)
    for place, weight in enumerate((kw_ref, vw_ref)):
        states = jnp.dot(mixed, weight[...], preferred_element_type=F32).astype(BF16)
        for h in range(heads):
            at = (2 * h + place) * HD
            kv_s[:, at : at + HD] = states[:, h * HD : (h + 1) * HD]

    def diag(h):
        q = q_ref[:, h * HD : (h + 1) * HD]
        g = g_ref[:, h * HD : (h + 1) * HD]
        return jnp.concatenate(
            [jnp.concatenate([q, zeros], axis=1), jnp.concatenate([zeros, g], axis=1)], axis=0
        )

    for h in range(heads):
        wide = slice(2 * h * HD, (2 * h + 2) * HD)
        both_s[h] = lax.dot_general(diag(h), kv_s[:, wide], NT, preferred_element_type=F32)
    for h in range(heads):
        scores = both_s[h, :SPAN] * scale
        grad_probs = both_s[h, SPAN:]
        expo = jnp.exp(scores - jnp.max(scores, axis=-1, keepdims=True))
        probs = expo / jnp.sum(expo, axis=-1, keepdims=True)
        inner = jnp.sum(grad_probs * probs, axis=-1, keepdims=True)
        grad_scores = scale * probs * (grad_probs - inner)
        stacked_s[h, :SPAN] = grad_scores.astype(BF16)
        stacked_s[h, SPAN:] = probs.astype(BF16)
    for h in range(heads):
        wide = slice(2 * h * HD, (2 * h + 2) * HD)
        cols = slice(h * HD, (h + 1) * HD)
        out = jnp.dot(stacked_s[h], kv_s[:, wide], preferred_element_type=F32)
        gq_ref[:, cols] = out[:SPAN, :HD].astype(BF16)
        att_ref[:, cols] = out[SPAN:, HD:].astype(BF16)
    for h in range(heads):
        cols = slice(h * HD, (h + 1) * HD)
        pair = lax.dot_general(
            stacked_s[h], diag(h), (((0,), (0,)), ((), ())), preferred_element_type=F32
        ).astype(BF16)
        grads_ref[0, :, cols] = pair[:, :HD]
        grads_ref[1, :, cols] = pair[:, HD:]


def core(queries, cotangent, raw, key_weight, value_weight, conv_kernel):
    tokens, width = queries.shape
    heads = width // HD
    spans = tokens // SPAN
    keys_here = NBR * NLEN
    keys_all = spans * keys_here
    whole = lambda shape: pl.BlockSpec(
        shape, lambda i: (0,) * len(shape), pipeline_mode=pl.Buffered(1)
    )
    span_rows = pl.BlockSpec((SPAN, width), lambda i: (i, 0))
    parts, quarter = raw.shape[1], raw.shape[3]
    blocks = pl.BlockSpec((CHUNKS, parts, NBR, quarter, LANES), lambda i: (0, 0, i, 0, 0))
    return pl.pallas_call(
        functools.partial(core_kernel, heads),
        grid=(spans,),
        in_specs=[
            span_rows,
            span_rows,
            blocks,
            whole((ENC, width)),
            whole((ENC, width)),
            whole((KW, ENC)),
        ],
        out_specs=[
            span_rows,
            span_rows,
            pl.BlockSpec((2, keys_here, width), lambda i: (0, i, 0)),
            pl.BlockSpec((ENC, keys_here), lambda i: (0, i)),
        ],
        out_shape=[
            jax.ShapeDtypeStruct((tokens, width), BF16),
            jax.ShapeDtypeStruct((tokens, width), BF16),
            jax.ShapeDtypeStruct((2, keys_all, width), BF16),
            jax.ShapeDtypeStruct((ENC, keys_all), BF16),
        ],
        scratch_shapes=[
            pltpu.VMEM((keys_here, ENC), BF16),
            pltpu.VMEM((keys_here, 2 * width), BF16),
            pltpu.VMEM((heads, 2 * SPAN, keys_here), F32),
            pltpu.VMEM((heads, 2 * SPAN, keys_here), BF16),
        ],
        compiler_params=pltpu.CompilerParams(
            dimension_semantics=("arbitrary",), vmem_limit_bytes=60 * 1024 * 1024
        ),
        cost_estimate=pl.CostEstimate(
            flops=10_000_000_000, bytes_accessed=30_000_000, transcendentals=1_200_000
        ),
    )(queries, cotangent, raw, key_weight, value_weight, conv_kernel)


def dp_peer(step):
    me = lax.axis_index("dp")
    z = lax.rem(me // 8 + step // 8, 4)
    x = lax.rem(lax.rem(me // 2, 4) + lax.rem(step // 2, 4), 4)
    return z * 8 + x * 2 + lax.rem(me + step, 2)


def fetch_kernel(
    owners,
    parts,
    slot_ref,
    table_ref,
    states_ref,
    raw_ref,
    asked_ref,
    asked_s,
    send,
    ask_sem,
    local_sem,
    send_sem,
    recv_sem,
    y_send,
    y_recv,
    *recv,
):
    me = lax.axis_index("dp")
    y = lax.axis_index("db")
    right = lax.rem(y + 1, parts)
    left = lax.rem(y + parts - 1, parts)
    requests = raw_ref.shape[2]
    half = requests // 2
    capacity = 2
    others = owners - 1

    barrier = pltpu.get_barrier_semaphore()

    def greet(step, carry):
        pl.semaphore_signal(barrier, inc=1, device_id={"dp": dp_peer(step)})
        return carry

    lax.fori_loop(1, owners, greet, 0)
    for side in (left, right):
        pl.semaphore_signal(barrier, inc=1, device_id={"db": side})
    pl.semaphore_wait(barrier, others + 2)

    def ask(step, carry):
        peer = dp_peer(step)
        pltpu.make_async_remote_copy(
            src_ref=table_ref.at[peer],
            dst_ref=asked_ref.at[me],
            send_sem=ask_sem.at[0],
            recv_sem=ask_sem.at[1],
            device_id={"dp": peer},
        ).start()
        return carry

    lax.fori_loop(1, owners, ask, 0)
    asked_ref[me] = table_ref[me]
    most = asked_ref.at[pl.ds(0, others)]
    pltpu.make_async_copy(most, most, ask_sem.at[1]).wait()
    pltpu.make_async_copy(asked_ref, asked_s, local_sem).start()
    pltpu.make_async_copy(asked_ref, asked_s, local_sem).wait()

    def replies(c):
        cols = slice(c * LANES, (c + 1) * LANES)

        def reply(step, carry):
            peer = dp_peer(step)
            for k in range(capacity):
                row = jnp.maximum(asked_s[peer, 0, k], 0)
                send[c, capacity * peer + k] = states_ref[row, :, cols]
            pltpu.make_async_remote_copy(
                src_ref=send.at[c, pl.ds(capacity * peer, capacity)],
                dst_ref=recv[c].at[pl.ds(capacity * me, capacity)],
                send_sem=send_sem.at[c],
                recv_sem=recv_sem.at[c],
                device_id={"dp": peer},
            ).start()
            return carry

        lax.fori_loop(1, owners, reply, 0)
        for k in range(capacity):
            row = jnp.maximum(asked_s[me, 0, k], 0)
            recv[c][capacity * me + k] = states_ref[row, :, cols]

    ahead = 2
    for c in range(ahead):
        replies(c)

    def along_y(kind, c, part, rows, side):
        block = raw_ref.at[c, part, rows]
        return pltpu.make_async_remote_copy(
            src_ref=block,
            dst_ref=block,
            send_sem=y_send.at[kind, c],
            recv_sem=y_recv.at[kind, c],
            device_id={"db": side},
        )

    everything, low, high = pl.ds(0, requests), pl.ds(0, half), pl.ds(half, requests - half)

    def arrivals(kind, c):
        far = lax.rem(y + 2, parts)
        part, rows = ((left, everything), (right, everything), (far, low), (far, high))[kind]
        return along_y(kind, c, part, rows, right)

    for c in range(CHUNKS + 1):
        if c + ahead < CHUNKS:
            replies(c + ahead)
        if c < CHUNKS:
            most = recv[c].at[pl.ds(0, capacity * others)]
            pltpu.make_async_copy(most, most, recv_sem.at[c]).wait()
            for p in range(requests):
                raw_ref[c, y, p] = recv[c][slot_ref[p]]
            along_y(0, c, y, everything, right).start()
            along_y(1, c, y, everything, left).start()
        if c >= 1:
            arrivals(0, c - 1).wait_recv()
            along_y(2, c - 1, left, low, right).start()
            arrivals(1, c - 1).wait_recv()
            along_y(3, c - 1, right, high, left).start()
    for c in range(CHUNKS):
        arrivals(2, c).wait_recv()
        arrivals(3, c).wait_recv()
        along_y(0, c, y, everything, right).wait_send()
        along_y(1, c, y, everything, left).wait_send()
        along_y(2, c, left, low, right).wait_send()
        along_y(3, c, right, high, left).wait_send()
        most = send.at[c, pl.ds(0, capacity * others)]
        pltpu.make_async_copy(most, most, send_sem.at[c]).wait()
    most = table_ref.at[pl.ds(0, others)]
    pltpu.make_async_copy(most, most, ask_sem.at[0]).wait()


def fetch(slots, table, states):
    owners = table.shape[0]
    parts = lax.axis_size("db")
    requests = slots.shape[0]
    quarter = states.shape[1]
    vmem = pl.BlockSpec(memory_space=pltpu.VMEM)
    dma = pltpu.SemaphoreType.DMA
    return pl.pallas_call(
        functools.partial(fetch_kernel, owners, parts),
        in_specs=[pl.BlockSpec(memory_space=pltpu.SMEM), vmem, vmem],
        out_specs=[vmem, vmem],
        out_shape=[
            jax.ShapeDtypeStruct((CHUNKS, parts, requests, quarter, LANES), BF16),
            jax.ShapeDtypeStruct(table.shape, jnp.int32),
        ],
        scratch_shapes=[
            pltpu.SMEM(table.shape, jnp.int32),
            pltpu.VMEM((CHUNKS, 2 * owners, quarter, LANES), BF16),
            dma((2,)),
            dma,
            dma((CHUNKS,)),
            dma((CHUNKS,)),
            dma((4, CHUNKS)),
            dma((4, CHUNKS)),
        ]
        + [pltpu.VMEM((2 * owners, quarter, LANES), BF16)] * CHUNKS,
        compiler_params=pltpu.CompilerParams(
            collective_id=0, has_side_effects=True, vmem_limit_bytes=60 * 1024 * 1024
        ),
        cost_estimate=pl.CostEstimate(flops=0, bytes_accessed=16_000_000, transcendentals=0),
    )(slots, table, states)


def tail_kernel(
    owners,
    parts,
    req_ref,
    conv_ref,
    grads_hbm,
    mixed_hbm,
    raw_hbm,
    kw_hbm,
    vw_hbm,
    back_ref,
    wsum_ref,
    tsum_ref,
    grads,
    mixed_t,
    raw_ref,
    kw_ref,
    vw_ref,
    part_ref,
    w_ref,
    taps_acc,
    load_sem,
    grads_sem,
    from_far,
    onward,
    from_near,
    send,
    sibling_w,
    pair_w,
    first_in,
    first_sum,
    second_in,
    taps_in,
    taps_now,
    far_send,
    far_recv,
    near_send,
    near_recv,
    back_send,
    back_recv,
    pair_send,
    pair_recv,
    axis_send,
    axis_recv,
    taps_send,
    taps_recv,
    *mine,
):
    me = lax.axis_index("dp")
    y = lax.axis_index("db")
    z, x, core = me // 8, lax.rem(me // 2, 4), lax.rem(me, 2)
    sibling = me + 1 - 2 * core
    right = lax.rem(y + 1, parts)
    left = lax.rem(y + parts - 1, parts)
    far = lax.rem(y + 2, parts)
    requests = part_ref.shape[2]
    keys_here = NBR * NLEN
    spans = requests // NBR

    def load(index):
        pair = ((kw_hbm, kw_ref), (vw_hbm, vw_ref), (raw_hbm, raw_ref), (mixed_hbm, mixed_t))[index]
        return pltpu.make_async_copy(*pair, load_sem.at[index])

    def load_grads(span):
        rows = pl.ds(pl.multiple_of(span * keys_here, keys_here), keys_here)
        return pltpu.make_async_copy(
            grads_hbm.at[:, rows], grads.at[:, rows], grads_sem.at[span]
        )

    for span in range(spans):
        load_grads(span).start()
    for index in (3, 0, 1, 2):
        load(index).start()
    taps_acc[...] = jnp.zeros_like(taps_acc)
    half = requests // 2
    capacity = 2
    others = owners - 1
    low, high = pl.ds(0, half), pl.ds(half, requests - half)

    def x_peer(step):
        return z * 8 + lax.rem(x + step, 4) * 2 + core

    def z_peer(step):
        return lax.rem(z + step, 4) * 8 + x * 2 + core

    barrier = pltpu.get_barrier_semaphore()

    def greet(step, carry):
        pl.semaphore_signal(barrier, inc=1, device_id={"dp": dp_peer(step)})
        return carry

    lax.fori_loop(1, owners, greet, 0)
    for other in range(1, parts):
        pl.semaphore_signal(barrier, inc=1, device_id={"db": lax.rem(y + other, parts)})
    pl.semaphore_wait(barrier, others + parts - 1)

    def remote(src, dst, send_sem, recv_sem, where):
        return pltpu.make_async_remote_copy(
            src_ref=src, dst_ref=dst, send_sem=send_sem, recv_sem=recv_sem, device_id=where
        )

    def grad_columns(chunks):
        cols = slice(chunks[0] * LANES, (chunks[-1] + 1) * LANES)

        def one(span, carry):
            rows = pl.ds(pl.multiple_of(span * keys_here, keys_here), keys_here)
            whole = lax.dot_general(
                grads[0, rows], kw_ref[cols], NT, preferred_element_type=F32
            ) + lax.dot_general(grads[1, rows], vw_ref[cols], NT, preferred_element_type=F32)
            for i, c in enumerate(chunks):
                lanes = slice(c * LANES, (c + 1) * LANES)
                for n in range(NBR):
                    gm = whole[n * NLEN : (n + 1) * NLEN, i * LANES : (i + 1) * LANES]
                    gm_down, gm_up = shifted(gm)
                    grad = conv_ref[0:1, lanes] * gm_up
                    grad = grad + conv_ref[1:2, lanes] * gm
                    grad = grad + conv_ref[2:3, lanes] * gm_down
                    part_ref[c, :, span * NBR + n] = grad.astype(BF16).reshape(parts, -1, LANES)
                    raw = raw_ref[c, :, span * NBR + n].reshape(NLEN, LANES).astype(F32)
                    for w, other in enumerate((gm_up, gm, gm_down)):
                        taps_acc[w, :, lanes] += jnp.sum(
                            (raw * other).reshape(NLEN // 8, 8, LANES), axis=0
                        )
            return carry

        lax.fori_loop(0, spans, one, 0)

    def far_copy(side, c):
        rows, to = ((low, right), (high, left))[side]
        return remote(
            part_ref.at[c, far, rows],
            from_far.at[side, c],
            far_send.at[side, c],
            far_recv.at[side, c],
            {"db": to},
        )

    def near_copy(side, c):
        return remote(
            onward.at[side, c],
            from_near.at[side, c],
            near_send.at[side, c],
            near_recv.at[side, c],
            {"db": (right, left)[side]},
        )

    def forward(c):
        far_copy(0, c).wait_recv()
        added = part_ref[c, right, 0:half].astype(F32) + from_far[0, c].astype(F32)
        onward[0, c, 0:half] = added.astype(BF16)
        onward[0, c, half:requests] = part_ref[c, right, half:requests]
        near_copy(0, c).start()
        far_copy(1, c).wait_recv()
        added = part_ref[c, left, half:requests].astype(F32) + from_far[1, c].astype(F32)
        onward[1, c, half:requests] = added.astype(BF16)
        onward[1, c, 0:half] = part_ref[c, left, 0:half]
        near_copy(1, c).start()

    def give_back(c):
        near_copy(0, c).wait_recv()
        near_copy(1, c).wait_recv()
        total = part_ref[c, y].astype(F32) + from_near[0, c].astype(F32)
        mine[c][...] = (total + from_near[1, c].astype(F32)).astype(BF16)

        def one(step, carry):
            peer = dp_peer(step)
            for k in range(capacity):
                send[c, capacity * peer + k] = mine[c][req_ref[capacity * peer + k]]
            remote(
                send.at[c, pl.ds(capacity * peer, capacity)],
                back_ref.at[c, pl.ds(capacity * me, capacity)],
                back_send.at[c],
                back_recv.at[c],
                {"dp": peer},
            ).start()
            return carry

        lax.fori_loop(1, owners, one, 0)
        for k in range(capacity):
            back_ref[c, capacity * me + k] = mine[c][req_ref[capacity * me + k]]

    first_at, second_at = (x, z), (z, x)
    first_peer, second_peer = (x_peer, z_peer), (z_peer, x_peer)
    order = [(d, h) for d in (1, 2, 3, 0) for h in (0, 1)]

    def group(h, step):
        return h * 4 + lax.rem(first_at[h] + step, 4)

    def pair_copy(d, h):
        g = group(h, d)
        return remote(
            w_ref.at[1 - core, g],
            sibling_w.at[g],
            pair_send.at[0, h * 4 + d],
            pair_recv.at[0, h * 4 + d],
            {"dp": sibling},
        )

    def weight_terms(which, d):
        def columns(h):
            return grads[which, :, pl.ds(pl.multiple_of(group(h, d) * HD, HD), HD)]

        both = jnp.concatenate([columns(0), columns(1)], axis=1)
        term = jnp.dot(mixed_t[...], both, preferred_element_type=F32)
        for h in (0, 1):
            block = term[:, h * HD : (h + 1) * HD].astype(BF16)
            w_ref[which, group(h, d)] = block.reshape(4, -1, HD)

    def first_copy(d, h):
        return remote(
            pair_w.at[group(h, d)],
            first_in.at[h, d - 1],
            axis_send.at[0, h * 3 + d - 1],
            axis_recv.at[0, h * 3 + d - 1],
            {"dp": first_peer[h](d)},
        )

    def second_copy(d, h):
        return remote(
            first_sum.at[h, lax.rem(second_at[h] + d, 4)],
            second_in.at[h, d - 1],
            axis_send.at[1, h * 3 + d - 1],
            axis_recv.at[1, h * 3 + d - 1],
            {"dp": second_peer[h](d)},
        )

    def second_gather(d, h, back):
        block = wsum_ref.at[core, group(h, 0), lax.rem(second_at[h] + back, 4)]
        return remote(
            block,
            block,
            axis_send.at[2, h * 3 + d - 1],
            axis_recv.at[2, h * 3 + d - 1],
            {"dp": second_peer[h](d)},
        )

    def first_gather(d, h, back):
        block = wsum_ref.at[core, group(h, back)]
        return remote(
            block,
            block,
            axis_send.at[3, h * 3 + d - 1],
            axis_recv.at[3, h * 3 + d - 1],
            {"dp": first_peer[h](d)},
        )

    def pair_gather(d, h, which):
        block = wsum_ref.at[which, group(h, 4 - d)]
        return remote(
            block,
            block,
            pair_send.at[1, h * 4 + d],
            pair_recv.at[1, h * 4 + d],
            {"dp": sibling},
        )

    def pair_sum(d, h):
        pair_copy(d, h).wait_recv()
        g = group(h, d)
        pair_w[g] = (w_ref[core, g].astype(F32) + sibling_w[g].astype(F32)).astype(BF16)
        if d:
            first_copy(d, h).start()

    def sum_first(h):
        for d in (1, 2, 3):
            first_copy(d, h).wait_recv()
        total = pair_w[group(h, 0)].astype(F32)
        for d in (1, 2, 3):
            total = total + first_in[h, d - 1].astype(F32)
        first_sum[h] = total.astype(BF16)
        for d in (1, 2, 3):
            second_copy(d, h).start()

    def sum_second(h):
        for d in (1, 2, 3):
            second_copy(d, h).wait_recv()
        total = first_sum[h, second_at[h]].astype(F32)
        for d in (1, 2, 3):
            total = total + second_in[h, d - 1].astype(F32)
        wsum_ref[core, group(h, 0), second_at[h]] = total.astype(BF16)
        for d in (1, 2, 3):
            second_gather(d, h, 0).start()

    def gather_first(h):
        for d in (1, 2, 3):
            second_gather(d, h, 4 - d).wait_recv()
        for d in (1, 2, 3):
            first_gather(d, h, 0).start()
        pair_gather(0, h, core).start()

    def gather_pair(h):
        for d in (1, 2, 3):
            first_gather(d, h, 4 - d).wait_recv()
            pair_gather(d, h, core).start()

    stages = (
        (2, core, lambda step: {"dp": sibling}),
        (4, x, lambda step: {"dp": x_peer(step)}),
        (4, z, lambda step: {"dp": z_peer(step)}),
        (parts, y, lambda step: {"db": lax.rem(y + step, parts)}),
    )

    def taps_copy(stage, d):
        count, at, peer = stages[stage]
        return remote(
            taps_now.at[stage],
            taps_in.at[stage, at],
            taps_send.at[stage, d - 1],
            taps_recv.at[stage, d - 1],
            peer(d),
        )

    def taps_start(stage, value):
        count, at, peer = stages[stage]
        taps_now[stage] = value
        taps_in[stage, at] = value
        for d in range(1, count):
            taps_copy(stage, d).start()

    def taps_end(stage):
        count = stages[stage][0]
        for d in range(1, count):
            taps_copy(stage, d).wait_recv()
        total = taps_in[stage, 0]
        for other in range(1, count):
            total = total + taps_in[stage, other]
        return total

    def start_far(chunks):
        for c in chunks:
            far_copy(0, c).start()
            far_copy(1, c).start()

    for span in range(spans):
        load_grads(span).wait()
    load(3).wait()
    steps = (1, 2, 3, 0)
    for i, d in enumerate(steps):
        weight_terms(1 - core, d)
        pair_copy(d, 0).start()
        pair_copy(d, 1).start()
        weight_terms(core, d)
        if i:
            pair_sum(steps[i - 1], 0)
            pair_sum(steps[i - 1], 1)
    pair_sum(steps[-1], 0)
    pair_sum(steps[-1], 1)
    for index in (0, 1, 2):
        load(index).wait()
    grad_columns((0, 1))
    start_far((0, 1))
    sum_first(0)
    sum_first(1)
    grad_columns((2, 3))
    start_far((2, 3))
    forward(0)
    forward(1)
    sum_second(0)
    sum_second(1)
    grad_columns((4, 5))
    start_far((4, 5))
    give_back(0)
    gather_first(0)
    gather_first(1)
    forward(2)
    forward(3)
    grad_columns((6,))
    start_far((6,))
    taps_start(0, jnp.sum(taps_acc[...], axis=1))
    give_back(1)
    forward(4)
    forward(5)
    give_back(2)
    forward(6)
    taps_start(1, taps_end(0))
    give_back(3)
    taps_start(2, taps_end(1))
    give_back(4)
    taps_start(3, taps_end(2))
    give_back(5)
    gather_pair(0)
    gather_pair(1)
    give_back(6)
    tsum_ref[...] = taps_end(3)

    for d, h in order:
        pair_gather(d, h, 1 - core).wait_recv()
        pair_gather(d, h, core).wait_send()
        pair_copy(d, h).wait_send()
        if d:
            first_copy(d, h).wait_send()
            second_copy(d, h).wait_send()
            second_gather(d, h, 0).wait_send()
            first_gather(d, h, 0).wait_send()
    for stage in range(4):
        for d in range(1, stages[stage][0]):
            taps_copy(stage, d).wait_send()
    for c in range(CHUNKS):
        for side in (0, 1):
            far_copy(side, c).wait_send()
            near_copy(side, c).wait_send()
        most = send.at[c, pl.ds(0, capacity * others)]
        pltpu.make_async_copy(most, most, back_send.at[c]).wait()
        most = back_ref.at[c, pl.ds(0, capacity * others)]
        pltpu.make_async_copy(most, most, back_recv.at[c]).wait()


def tail(wanted, conv_kernel, grads, mixed, raw, key_weight, value_weight):
    owners = lax.axis_size("dp")
    parts = lax.axis_size("db")
    requests, quarter = raw.shape[2], raw.shape[3]
    slots = wanted.shape[0]
    vmem = pl.BlockSpec(memory_space=pltpu.VMEM)
    anywhere = pl.BlockSpec(memory_space=pl.ANY)
    dma = pltpu.SemaphoreType.DMA
    heads = key_weight.shape[1] // HD
    rows = ENC // 4
    weights = (2, heads, 4, rows, HD)
    taps = (8, ENC)
    both = (2, CHUNKS, requests, quarter, LANES)
    return pl.pallas_call(
        functools.partial(tail_kernel, owners, parts),
        in_specs=[pl.BlockSpec(memory_space=pltpu.SMEM), vmem] + [anywhere] * 5,
        out_specs=[vmem, vmem, vmem],
        out_shape=[
            jax.ShapeDtypeStruct((CHUNKS, slots, quarter, LANES), BF16),
            jax.ShapeDtypeStruct(weights, BF16),
            jax.ShapeDtypeStruct(taps, F32),
        ],
        scratch_shapes=[
            pltpu.VMEM(grads.shape, BF16),
            pltpu.VMEM(mixed.shape, BF16),
            pltpu.VMEM(raw.shape, BF16),
            pltpu.VMEM(key_weight.shape, BF16),
            pltpu.VMEM(value_weight.shape, BF16),
            pltpu.VMEM(raw.shape, BF16),
            pltpu.VMEM(weights, BF16),
            pltpu.VMEM((8, 8, ENC), F32),
            dma((4,)),
            dma((requests // NBR,)),
            pltpu.VMEM((2, CHUNKS, requests // 2, quarter, LANES), BF16),
            pltpu.VMEM(both, BF16),
            pltpu.VMEM(both, BF16),
            pltpu.VMEM((CHUNKS, slots, quarter, LANES), BF16),
            pltpu.VMEM((heads, 4, rows, HD), BF16),
            pltpu.VMEM((heads, 4, rows, HD), BF16),
            pltpu.VMEM((2, 3, 4, rows, HD), BF16),
            pltpu.VMEM((2, 4, rows, HD), BF16),
            pltpu.VMEM((2, 3, rows, HD), BF16),
            pltpu.VMEM((4, 4) + taps, F32),
            pltpu.VMEM((4,) + taps, F32),
            dma((2, CHUNKS)),
            dma((2, CHUNKS)),
            dma((2, CHUNKS)),
            dma((2, CHUNKS)),
            dma((CHUNKS,)),
            dma((CHUNKS,)),
            dma((2, 8)),
            dma((2, 8)),
            dma((4, 6)),
            dma((4, 6)),
            dma((4, 3)),
            dma((4, 3)),
        ]
        + [pltpu.VMEM((requests, quarter, LANES), BF16)] * CHUNKS,
        compiler_params=pltpu.CompilerParams(
            collective_id=1, has_side_effects=True, vmem_limit_bytes=60 * 1024 * 1024
        ),
        cost_estimate=pl.CostEstimate(
            flops=17_000_000_000, bytes_accessed=30_000_000, transcendentals=0
        ),
    )(wanted, conv_kernel, grads, mixed, raw, key_weight, value_weight)


def spread_kernel(rows_ref, back_ref, w_ref, states_ref, gkw_ref, gvw_ref):
    gkw_ref[...] = w_ref[0, 0].astype(F32)
    gvw_ref[...] = w_ref[1, 0].astype(F32)

    @pl.when(pl.program_id(0) < CHUNKS)
    def _():
        states_ref[...] = jnp.zeros_like(states_ref)

        def add(index, carry):
            for k in range(8):
                slot = index * 8 + k
                row = rows_ref[slot]

                @pl.when(row >= 0)
                def _():
                    states_ref[row] += back_ref[0, slot].astype(F32)

            return carry

        lax.fori_loop(0, rows_ref.shape[0] // 8, add, 0)


def spread(rows, back, weights, blocks):
    heads = weights.shape[1]
    slots, quarter = back.shape[1], back.shape[2]
    last = CHUNKS - 1
    head_cols = pl.BlockSpec((ENC, HD), lambda i: (0, i))
    return pl.pallas_call(
        spread_kernel,
        grid=(max(heads, CHUNKS),),
        in_specs=[
            pl.BlockSpec(memory_space=pltpu.SMEM),
            pl.BlockSpec((1, slots, quarter, LANES), lambda i: (jnp.minimum(i, last), 0, 0, 0)),
            pl.BlockSpec((2, 1, ENC, HD), lambda i: (0, i, 0, 0)),
        ],
        out_specs=[
            pl.BlockSpec((blocks, quarter, LANES), lambda i: (0, 0, jnp.minimum(i, last))),
            head_cols,
            head_cols,
        ],
        out_shape=[
            jax.ShapeDtypeStruct((blocks, quarter, ENC), F32),
            jax.ShapeDtypeStruct((ENC, heads * HD), F32),
            jax.ShapeDtypeStruct((ENC, heads * HD), F32),
        ],
        compiler_params=pltpu.CompilerParams(
            dimension_semantics=("arbitrary",), vmem_limit_bytes=60 * 1024 * 1024
        ),
        cost_estimate=pl.CostEstimate(flops=0, bytes_accessed=19_000_000, transcendentals=0),
    )(rows, back, weights.reshape(2, heads, ENC, HD))


def shards(
    queries, cotangent, db_states, key_weight, value_weight, conv_kernel, nbr_owner, nbr_row
):
    owners = lax.axis_size("dp")
    span_count = nbr_owner.shape[0]
    request_count = span_count * NBR
    capacity = max(2, (request_count + owners - 1) // owners)
    quarter = db_states.shape[1]
    local_blocks = db_states.shape[0]
    slots_total = owners * capacity
    owner_flat = nbr_owner.reshape(request_count)
    row_flat = nbr_row.reshape(request_count)
    positions = jnp.arange(request_count, dtype=jnp.int32)
    same_owner = owner_flat[:, None] == owner_flat[None, :]
    earlier = positions[:, None] > positions[None, :]
    slot_index = jnp.sum(jnp.logical_and(same_owner, earlier).astype(jnp.int32), axis=1)
    target = owner_flat * capacity + slot_index
    slot_hits = target[:, None] == jnp.arange(slots_total, dtype=jnp.int32)[None, :]
    used_slot = jnp.any(slot_hits, axis=0)
    row_sent = jnp.sum(jnp.where(slot_hits, row_flat[:, None], 0), axis=0)
    row_table = jnp.where(used_slot, row_sent, -1).reshape(owners, capacity)
    wanted = jnp.sum(jnp.where(slot_hits, positions[:, None], 0), axis=0)
    table = jnp.pad(row_table[:, None, :], ((0, 0), (0, 0), (0, LANES - capacity)))
    raw, asked = fetch(target, table, db_states)
    asked_flat = asked[:, 0, :capacity].reshape(slots_total)
    attended, grad_query, grads, mixed = core(
        queries, cotangent, raw, key_weight, value_weight, conv_kernel
    )
    back, weight_sums, taps_sum = tail(
        wanted, conv_kernel, grads, mixed, raw, key_weight, value_weight
    )
    grad_states, grad_key_weight, grad_value_weight = spread(
        asked_flat, back, weight_sums, local_blocks
    )
    return (
        attended,
        grad_query,
        grad_states,
        grad_key_weight,
        grad_value_weight,
        taps_sum[:KW],
    )


def solution(mesh):
    return jax.shard_map(
        shards,
        mesh=mesh,
        in_specs=(
            P("dp", "db"),
            P("dp", "db"),
            P("dp", "db", None),
            P(None, "db"),
            P(None, "db"),
            P(),
            P("dp", None),
            P("dp", None),
        ),
        out_specs=(
            P("dp", "db"),
            P("dp", "db"),
            P("dp", "db", None),
            P(None, "db"),
            P(None, "db"),
            P(),
        ),
        check_vma=False,
    )
```

```python
import functools
import math

import jax
import jax.numpy as jnp
from jax import lax
from jax.experimental import pallas as pl
from jax.experimental.pallas import tpu as pltpu
from jax.sharding import PartitionSpec as P

HD = 128
ENC = 896
SPAN = 64
NBR = 2
NLEN = 128
KW = 3
LANES = 128
CHUNKS = ENC // LANES
F32 = jnp.float32
BF16 = jnp.bfloat16
NT = (((1,), (1,)), ((), ()))


def shifted(block):
    rows = block.shape[0]
    at = lax.broadcasted_iota(jnp.int32, block.shape, 0)
    down = jnp.where(at == 0, 0.0, pltpu.roll(block, 1, 0))
    up = jnp.where(at == rows - 1, 0.0, pltpu.roll(block, rows - 1, 0))
    return down, up


def core_kernel(
    heads,
    q_ref,
    g_ref,
    raw_ref,
    kw_ref,
    vw_ref,
    taps_ref,
    att_ref,
    gq_ref,
    grads_ref,
    mixed_ref,
    mixed_s,
    kv_s,
    both_s,
    stacked_s,
):
    scale = 1.0 / math.sqrt(HD)
    for c in range(CHUNKS):
        cols = slice(c * LANES, (c + 1) * LANES)
        for n in range(NBR):
            raw = raw_ref[c, :, n].reshape(NLEN, LANES).astype(F32)
            down, up = shifted(raw)
            mixed = taps_ref[0:1, cols] * down
            mixed = mixed + taps_ref[1:2, cols] * raw
            mixed = mixed + taps_ref[2:3, cols] * up
            mixed_s[n * NLEN : (n + 1) * NLEN, cols] = mixed.astype(BF16)
    mixed = mixed_s[...]
    mixed_ref[...] = mixed.T

    zeros = jnp.zeros((SPAN, HD), BF16)
    for place, weight in enumerate((kw_ref, vw_ref)):
        states = jnp.dot(mixed, weight[...], preferred_element_type=F32).astype(BF16)
        for h in range(heads):
            at = (2 * h + place) * HD
            kv_s[:, at : at + HD] = states[:, h * HD : (h + 1) * HD]

    def diag(h):
        q = q_ref[:, h * HD : (h + 1) * HD]
        g = g_ref[:, h * HD : (h + 1) * HD]
        return jnp.concatenate(
            [jnp.concatenate([q, zeros], axis=1), jnp.concatenate([zeros, g], axis=1)], axis=0
        )

    for h in range(heads):
        wide = slice(2 * h * HD, (2 * h + 2) * HD)
        both_s[h] = lax.dot_general(diag(h), kv_s[:, wide], NT, preferred_element_type=F32)
    for h in range(heads):
        scores = both_s[h, :SPAN] * scale
        grad_probs = both_s[h, SPAN:]
        expo = jnp.exp(scores - jnp.max(scores, axis=-1, keepdims=True))
        probs = expo / jnp.sum(expo, axis=-1, keepdims=True)
        inner = jnp.sum(grad_probs * probs, axis=-1, keepdims=True)
        grad_scores = scale * probs * (grad_probs - inner)
        stacked_s[h, :SPAN] = grad_scores.astype(BF16)
        stacked_s[h, SPAN:] = probs.astype(BF16)
    for h in range(heads):
        wide = slice(2 * h * HD, (2 * h + 2) * HD)
        cols = slice(h * HD, (h + 1) * HD)
        out = jnp.dot(stacked_s[h], kv_s[:, wide], preferred_element_type=F32)
        gq_ref[:, cols] = out[:SPAN, :HD].astype(BF16)
        att_ref[:, cols] = out[SPAN:, HD:].astype(BF16)
    for h in range(heads):
        cols = slice(h * HD, (h + 1) * HD)
        pair = lax.dot_general(
            stacked_s[h], diag(h), (((0,), (0,)), ((), ())), preferred_element_type=F32
        ).astype(BF16)
        grads_ref[0, :, cols] = pair[:, :HD]
        grads_ref[1, :, cols] = pair[:, HD:]


def core(queries, cotangent, raw, key_weight, value_weight, conv_kernel):
    tokens, width = queries.shape
    heads = width // HD
    spans = tokens // SPAN
    keys_here = NBR * NLEN
    keys_all = spans * keys_here
    whole = lambda shape: pl.BlockSpec(
        shape, lambda i: (0,) * len(shape), pipeline_mode=pl.Buffered(1)
    )
    span_rows = pl.BlockSpec((SPAN, width), lambda i: (i, 0))
    parts, quarter = raw.shape[1], raw.shape[3]
    blocks = pl.BlockSpec((CHUNKS, parts, NBR, quarter, LANES), lambda i: (0, 0, i, 0, 0))
    return pl.pallas_call(
        functools.partial(core_kernel, heads),
        grid=(spans,),
        in_specs=[
            span_rows,
            span_rows,
            blocks,
            whole((ENC, width)),
            whole((ENC, width)),
            whole((KW, ENC)),
        ],
        out_specs=[
            span_rows,
            span_rows,
            pl.BlockSpec((2, keys_here, width), lambda i: (0, i, 0)),
            pl.BlockSpec((ENC, keys_here), lambda i: (0, i)),
        ],
        out_shape=[
            jax.ShapeDtypeStruct((tokens, width), BF16),
            jax.ShapeDtypeStruct((tokens, width), BF16),
            jax.ShapeDtypeStruct((2, keys_all, width), BF16),
            jax.ShapeDtypeStruct((ENC, keys_all), BF16),
        ],
        scratch_shapes=[
            pltpu.VMEM((keys_here, ENC), BF16),
            pltpu.VMEM((keys_here, 2 * width), BF16),
            pltpu.VMEM((heads, 2 * SPAN, keys_here), F32),
            pltpu.VMEM((heads, 2 * SPAN, keys_here), BF16),
        ],
        compiler_params=pltpu.CompilerParams(
            dimension_semantics=("arbitrary",), vmem_limit_bytes=60 * 1024 * 1024
        ),
        cost_estimate=pl.CostEstimate(
            flops=10_000_000_000, bytes_accessed=30_000_000, transcendentals=1_200_000
        ),
    )(queries, cotangent, raw, key_weight, value_weight, conv_kernel)


def dp_peer(step):
    me = lax.axis_index("dp")
    z = lax.rem(me // 8 + step // 8, 4)
    x = lax.rem(lax.rem(me // 2, 4) + lax.rem(step // 2, 4), 4)
    return z * 8 + x * 2 + lax.rem(me + step, 2)


def fetch_kernel(
    owners,
    parts,
    slot_ref,
    table_ref,
    states_ref,
    raw_ref,
    asked_ref,
    asked_s,
    send,
    ask_sem,
    local_sem,
    send_sem,
    recv_sem,
    y_send,
    y_recv,
    *recv,
):
    me = lax.axis_index("dp")
    y = lax.axis_index("db")
    right = lax.rem(y + 1, parts)
    left = lax.rem(y + parts - 1, parts)
    requests = raw_ref.shape[2]
    half = requests // 2
    capacity = 2
    others = owners - 1

    barrier = pltpu.get_barrier_semaphore()

    def greet(step, carry):
        pl.semaphore_signal(barrier, inc=1, device_id={"dp": dp_peer(step)})
        return carry

    lax.fori_loop(1, owners, greet, 0)
    for side in (left, right):
        pl.semaphore_signal(barrier, inc=1, device_id={"db": side})
    pl.semaphore_wait(barrier, others + 2)

    def ask(step, carry):
        peer = dp_peer(step)
        pltpu.make_async_remote_copy(
            src_ref=table_ref.at[peer],
            dst_ref=asked_ref.at[me],
            send_sem=ask_sem.at[0],
            recv_sem=ask_sem.at[1],
            device_id={"dp": peer},
        ).start()
        return carry

    lax.fori_loop(1, owners, ask, 0)
    asked_ref[me] = table_ref[me]
    most = asked_ref.at[pl.ds(0, others)]
    pltpu.make_async_copy(most, most, ask_sem.at[1]).wait()
    pltpu.make_async_copy(asked_ref, asked_s, local_sem).start()
    pltpu.make_async_copy(asked_ref, asked_s, local_sem).wait()

    def replies(c):
        cols = slice(c * LANES, (c + 1) * LANES)

        def reply(step, carry):
            peer = dp_peer(step)
            for k in range(capacity):
                row = jnp.maximum(asked_s[peer, 0, k], 0)
                send[c, capacity * peer + k] = states_ref[row, :, cols]
            pltpu.make_async_remote_copy(
                src_ref=send.at[c, pl.ds(capacity * peer, capacity)],
                dst_ref=recv[c].at[pl.ds(capacity * me, capacity)],
                send_sem=send_sem.at[c],
                recv_sem=recv_sem.at[c],
                device_id={"dp": peer},
            ).start()
            return carry

        lax.fori_loop(1, owners, reply, 0)
        for k in range(capacity):
            row = jnp.maximum(asked_s[me, 0, k], 0)
            recv[c][capacity * me + k] = states_ref[row, :, cols]

    ahead = 2
    for c in range(ahead):
        replies(c)

    def along_y(kind, c, part, rows, side):
        block = raw_ref.at[c, part, rows]
        return pltpu.make_async_remote_copy(
            src_ref=block,
            dst_ref=block,
            send_sem=y_send.at[kind, c],
            recv_sem=y_recv.at[kind, c],
            device_id={"db": side},
        )

    everything, low, high = pl.ds(0, requests), pl.ds(0, half), pl.ds(half, requests - half)

    def arrivals(kind, c):
        far = lax.rem(y + 2, parts)
        part, rows = ((left, everything), (right, everything), (far, low), (far, high))[kind]
        return along_y(kind, c, part, rows, right)

    for c in range(CHUNKS + 1):
        if c + ahead < CHUNKS:
            replies(c + ahead)
        if c < CHUNKS:
            most = recv[c].at[pl.ds(0, capacity * others)]
            pltpu.make_async_copy(most, most, recv_sem.at[c]).wait()
            for p in range(requests):
                raw_ref[c, y, p] = recv[c][slot_ref[p]]
            along_y(0, c, y, everything, right).start()
            along_y(1, c, y, everything, left).start()
        if c >= 1:
            arrivals(0, c - 1).wait_recv()
            along_y(2, c - 1, left, low, right).start()
            arrivals(1, c - 1).wait_recv()
            along_y(3, c - 1, right, high, left).start()
    for c in range(CHUNKS):
        arrivals(2, c).wait_recv()
        arrivals(3, c).wait_recv()
        along_y(0, c, y, everything, right).wait_send()
        along_y(1, c, y, everything, left).wait_send()
        along_y(2, c, left, low, right).wait_send()
        along_y(3, c, right, high, left).wait_send()
        most = send.at[c, pl.ds(0, capacity * others)]
        pltpu.make_async_copy(most, most, send_sem.at[c]).wait()
    most = table_ref.at[pl.ds(0, others)]
    pltpu.make_async_copy(most, most, ask_sem.at[0]).wait()


def fetch(slots, table, states):
    owners = table.shape[0]
    parts = lax.axis_size("db")
    requests = slots.shape[0]
    quarter = states.shape[1]
    vmem = pl.BlockSpec(memory_space=pltpu.VMEM)
    dma = pltpu.SemaphoreType.DMA
    return pl.pallas_call(
        functools.partial(fetch_kernel, owners, parts),
        in_specs=[pl.BlockSpec(memory_space=pltpu.SMEM), vmem, vmem],
        out_specs=[vmem, vmem],
        out_shape=[
            jax.ShapeDtypeStruct((CHUNKS, parts, requests, quarter, LANES), BF16),
            jax.ShapeDtypeStruct(table.shape, jnp.int32),
        ],
        scratch_shapes=[
            pltpu.SMEM(table.shape, jnp.int32),
            pltpu.VMEM((CHUNKS, 2 * owners, quarter, LANES), BF16),
            dma((2,)),
            dma,
            dma((CHUNKS,)),
            dma((CHUNKS,)),
            dma((4, CHUNKS)),
            dma((4, CHUNKS)),
        ]
        + [pltpu.VMEM((2 * owners, quarter, LANES), BF16)] * CHUNKS,
        compiler_params=pltpu.CompilerParams(
            collective_id=0, has_side_effects=True, vmem_limit_bytes=60 * 1024 * 1024
        ),
        cost_estimate=pl.CostEstimate(flops=0, bytes_accessed=16_000_000, transcendentals=0),
    )(slots, table, states)


def tail_kernel(
    owners,
    parts,
    req_ref,
    conv_ref,
    grads_hbm,
    mixed_hbm,
    raw_hbm,
    kw_hbm,
    vw_hbm,
    back_ref,
    wsum_ref,
    tsum_ref,
    grads,
    mixed_t,
    raw_ref,
    kw_ref,
    vw_ref,
    part_ref,
    w_ref,
    taps_acc,
    load_sem,
    grads_sem,
    from_far,
    onward,
    from_near,
    send,
    sibling_w,
    pair_w,
    first_in,
    first_sum,
    second_in,
    taps_in,
    taps_now,
    far_send,
    far_recv,
    near_send,
    near_recv,
    back_send,
    back_recv,
    pair_send,
    pair_recv,
    axis_send,
    axis_recv,
    taps_send,
    taps_recv,
    *mine,
):
    me = lax.axis_index("dp")
    y = lax.axis_index("db")
    z, x, core = me // 8, lax.rem(me // 2, 4), lax.rem(me, 2)
    sibling = me + 1 - 2 * core
    right = lax.rem(y + 1, parts)
    left = lax.rem(y + parts - 1, parts)
    far = lax.rem(y + 2, parts)
    requests = part_ref.shape[2]
    keys_here = NBR * NLEN
    spans = requests // NBR

    def load(index):
        pair = ((kw_hbm, kw_ref), (vw_hbm, vw_ref), (raw_hbm, raw_ref), (mixed_hbm, mixed_t))[index]
        return pltpu.make_async_copy(*pair, load_sem.at[index])

    def load_grads(span):
        rows = pl.ds(pl.multiple_of(span * keys_here, keys_here), keys_here)
        return pltpu.make_async_copy(
            grads_hbm.at[:, rows], grads.at[:, rows], grads_sem.at[span]
        )

    load(0).start()
    load(1).start()
    for span in range(spans):
        load_grads(span).start()
    load(2).start()
    load(3).start()
    taps_acc[...] = jnp.zeros_like(taps_acc)
    half = requests // 2
    capacity = 2
    others = owners - 1
    low, high = pl.ds(0, half), pl.ds(half, requests - half)

    def x_peer(step):
        return z * 8 + lax.rem(x + step, 4) * 2 + core

    def z_peer(step):
        return lax.rem(z + step, 4) * 8 + x * 2 + core

    barrier = pltpu.get_barrier_semaphore()

    def greet(step, carry):
        pl.semaphore_signal(barrier, inc=1, device_id={"dp": dp_peer(step)})
        return carry

    lax.fori_loop(1, owners, greet, 0)
    for other in range(1, parts):
        pl.semaphore_signal(barrier, inc=1, device_id={"db": lax.rem(y + other, parts)})
    pl.semaphore_wait(barrier, others + parts - 1)

    def remote(src, dst, send_sem, recv_sem, where):
        return pltpu.make_async_remote_copy(
            src_ref=src, dst_ref=dst, send_sem=send_sem, recv_sem=recv_sem, device_id=where
        )

    def grad_columns(chunks):
        cols = slice(chunks[0] * LANES, (chunks[-1] + 1) * LANES)

        def one(span, carry):
            rows = pl.ds(pl.multiple_of(span * keys_here, keys_here), keys_here)
            whole = lax.dot_general(
                grads[0, rows], kw_ref[cols], NT, preferred_element_type=F32
            ) + lax.dot_general(grads[1, rows], vw_ref[cols], NT, preferred_element_type=F32)
            for i, c in enumerate(chunks):
                lanes = slice(c * LANES, (c + 1) * LANES)
                for n in range(NBR):
                    gm = whole[n * NLEN : (n + 1) * NLEN, i * LANES : (i + 1) * LANES]
                    gm_down, gm_up = shifted(gm)
                    grad = conv_ref[0:1, lanes] * gm_up
                    grad = grad + conv_ref[1:2, lanes] * gm
                    grad = grad + conv_ref[2:3, lanes] * gm_down
                    part_ref[c, :, span * NBR + n] = grad.astype(BF16).reshape(parts, -1, LANES)
                    raw = raw_ref[c, :, span * NBR + n].reshape(NLEN, LANES).astype(F32)
                    for w, other in enumerate((gm_up, gm, gm_down)):
                        taps_acc[w, :, lanes] += jnp.sum(
                            (raw * other).reshape(NLEN // 8, 8, LANES), axis=0
                        )
            return carry

        lax.fori_loop(0, spans, one, 0)

    def far_copy(side, c):
        rows, to = ((low, right), (high, left))[side]
        return remote(
            part_ref.at[c, far, rows],
            from_far.at[side, c],
            far_send.at[side, c],
            far_recv.at[side, c],
            {"db": to},
        )

    def near_copy(side, c):
        return remote(
            onward.at[side, c],
            from_near.at[side, c],
            near_send.at[side, c],
            near_recv.at[side, c],
            {"db": (right, left)[side]},
        )

    def forward(c):
        far_copy(0, c).wait_recv()
        added = part_ref[c, right, 0:half].astype(F32) + from_far[0, c].astype(F32)
        onward[0, c, 0:half] = added.astype(BF16)
        onward[0, c, half:requests] = part_ref[c, right, half:requests]
        near_copy(0, c).start()
        far_copy(1, c).wait_recv()
        added = part_ref[c, left, half:requests].astype(F32) + from_far[1, c].astype(F32)
        onward[1, c, half:requests] = added.astype(BF16)
        onward[1, c, 0:half] = part_ref[c, left, 0:half]
        near_copy(1, c).start()

    def give_back(c):
        near_copy(0, c).wait_recv()
        near_copy(1, c).wait_recv()
        total = part_ref[c, y].astype(F32) + from_near[0, c].astype(F32)
        mine[c][...] = (total + from_near[1, c].astype(F32)).astype(BF16)

        def one(step, carry):
            peer = dp_peer(step)
            for k in range(capacity):
                send[c, capacity * peer + k] = mine[c][req_ref[capacity * peer + k]]
            remote(
                send.at[c, pl.ds(capacity * peer, capacity)],
                back_ref.at[c, pl.ds(capacity * me, capacity)],
                back_send.at[c],
                back_recv.at[c],
                {"dp": peer},
            ).start()
            return carry

        lax.fori_loop(1, owners, one, 0)
        for k in range(capacity):
            back_ref[c, capacity * me + k] = mine[c][req_ref[capacity * me + k]]

    first_at, second_at = (x, z), (z, x)
    first_peer, second_peer = (x_peer, z_peer), (z_peer, x_peer)
    order = [(d, h) for d in (1, 2, 3, 0) for h in (0, 1)]

    def group(h, step):
        return h * 4 + lax.rem(first_at[h] + step, 4)

    def pair_copy(d, h):
        g = group(h, d)
        return remote(
            w_ref.at[1 - core, g],
            sibling_w.at[g],
            pair_send.at[0, h * 4 + d],
            pair_recv.at[0, h * 4 + d],
            {"dp": sibling},
        )

    def weight_terms(which, d):
        def columns(h):
            return grads[which, :, pl.ds(pl.multiple_of(group(h, d) * HD, HD), HD)]

        both = jnp.concatenate([columns(0), columns(1)], axis=1)
        term = jnp.dot(mixed_t[...], both, preferred_element_type=F32)
        for h in (0, 1):
            block = term[:, h * HD : (h + 1) * HD].astype(BF16)
            w_ref[which, group(h, d)] = block.reshape(4, -1, HD)

    def first_copy(d, h):
        return remote(
            pair_w.at[group(h, d)],
            first_in.at[h, d - 1],
            axis_send.at[0, h * 3 + d - 1],
            axis_recv.at[0, h * 3 + d - 1],
            {"dp": first_peer[h](d)},
        )

    def second_copy(d, h):
        return remote(
            first_sum.at[h, lax.rem(second_at[h] + d, 4)],
            second_in.at[h, d - 1],
            axis_send.at[1, h * 3 + d - 1],
            axis_recv.at[1, h * 3 + d - 1],
            {"dp": second_peer[h](d)},
        )

    def second_gather(d, h, back):
        block = wsum_ref.at[core, group(h, 0), lax.rem(second_at[h] + back, 4)]
        return remote(
            block,
            block,
            axis_send.at[2, h * 3 + d - 1],
            axis_recv.at[2, h * 3 + d - 1],
            {"dp": second_peer[h](d)},
        )

    def first_gather(d, h, back):
        block = wsum_ref.at[core, group(h, back)]
        return remote(
            block,
            block,
            axis_send.at[3, h * 3 + d - 1],
            axis_recv.at[3, h * 3 + d - 1],
            {"dp": first_peer[h](d)},
        )

    def pair_gather(d, h, which):
        block = wsum_ref.at[which, group(h, 4 - d)]
        return remote(
            block,
            block,
            pair_send.at[1, h * 4 + d],
            pair_recv.at[1, h * 4 + d],
            {"dp": sibling},
        )

    def pair_sum(d, h):
        pair_copy(d, h).wait_recv()
        g = group(h, d)
        pair_w[g] = (w_ref[core, g].astype(F32) + sibling_w[g].astype(F32)).astype(BF16)
        if d:
            first_copy(d, h).start()

    def sum_first(h):
        for d in (1, 2, 3):
            first_copy(d, h).wait_recv()
        total = pair_w[group(h, 0)].astype(F32)
        for d in (1, 2, 3):
            total = total + first_in[h, d - 1].astype(F32)
        first_sum[h] = total.astype(BF16)
        for d in (1, 2, 3):
            second_copy(d, h).start()

    def sum_second(h):
        for d in (1, 2, 3):
            second_copy(d, h).wait_recv()
        total = first_sum[h, second_at[h]].astype(F32)
        for d in (1, 2, 3):
            total = total + second_in[h, d - 1].astype(F32)
        wsum_ref[core, group(h, 0), second_at[h]] = total.astype(BF16)
        for d in (1, 2, 3):
            second_gather(d, h, 0).start()

    def gather_first(h):
        for d in (1, 2, 3):
            second_gather(d, h, 4 - d).wait_recv()
        for d in (1, 2, 3):
            first_gather(d, h, 0).start()
        pair_gather(0, h, core).start()

    def gather_pair(h):
        for d in (1, 2, 3):
            first_gather(d, h, 4 - d).wait_recv()
            pair_gather(d, h, core).start()

    stages = (
        (2, core, lambda step: {"dp": sibling}),
        (4, x, lambda step: {"dp": x_peer(step)}),
        (4, z, lambda step: {"dp": z_peer(step)}),
        (parts, y, lambda step: {"db": lax.rem(y + step, parts)}),
    )

    def taps_copy(stage, d):
        count, at, peer = stages[stage]
        return remote(
            taps_now.at[stage],
            taps_in.at[stage, at],
            taps_send.at[stage, d - 1],
            taps_recv.at[stage, d - 1],
            peer(d),
        )

    def taps_start(stage, value):
        count, at, peer = stages[stage]
        taps_now[stage] = value
        taps_in[stage, at] = value
        for d in range(1, count):
            taps_copy(stage, d).start()

    def taps_end(stage):
        count = stages[stage][0]
        for d in range(1, count):
            taps_copy(stage, d).wait_recv()
        total = taps_in[stage, 0]
        for other in range(1, count):
            total = total + taps_in[stage, other]
        return total

    def start_far(chunks):
        for c in chunks:
            far_copy(0, c).start()
            far_copy(1, c).start()

    def weight_step(d):
        weight_terms(1 - core, d)
        pair_copy(d, 0).start()
        pair_copy(d, 1).start()
        weight_terms(core, d)

    def pair_sums(d):
        pair_sum(d, 0)
        pair_sum(d, 1)

    for span in range(spans):
        load_grads(span).wait()
    for index in (0, 1, 2):
        load(index).wait()
    grad_columns((0, 1))
    start_far((0, 1))
    load(3).wait()
    weight_step(1)
    forward(0)
    forward(1)
    weight_step(2)
    pair_sums(1)
    give_back(0)
    weight_step(3)
    pair_sums(2)
    give_back(1)
    weight_step(0)
    pair_sums(3)
    pair_sums(0)
    grad_columns((2, 3))
    start_far((2, 3))
    grad_columns((4, 5))
    start_far((4, 5))
    forward(2)
    forward(3)
    sum_first(0)
    sum_first(1)
    grad_columns((6,))
    start_far((6,))
    give_back(2)
    forward(4)
    forward(5)
    sum_second(0)
    sum_second(1)
    taps_start(0, jnp.sum(taps_acc[...], axis=1))
    give_back(3)
    forward(6)
    gather_first(0)
    gather_first(1)
    taps_start(1, taps_end(0))
    give_back(4)
    taps_start(2, taps_end(1))
    give_back(5)
    taps_start(3, taps_end(2))
    give_back(6)
    gather_pair(0)
    gather_pair(1)
    tsum_ref[...] = taps_end(3)

    for d, h in order:
        pair_gather(d, h, 1 - core).wait_recv()
        pair_gather(d, h, core).wait_send()
        pair_copy(d, h).wait_send()
        if d:
            first_copy(d, h).wait_send()
            second_copy(d, h).wait_send()
            second_gather(d, h, 0).wait_send()
            first_gather(d, h, 0).wait_send()
    for stage in range(4):
        for d in range(1, stages[stage][0]):
            taps_copy(stage, d).wait_send()
    for c in range(CHUNKS):
        for side in (0, 1):
            far_copy(side, c).wait_send()
            near_copy(side, c).wait_send()
        most = send.at[c, pl.ds(0, capacity * others)]
        pltpu.make_async_copy(most, most, back_send.at[c]).wait()
        most = back_ref.at[c, pl.ds(0, capacity * others)]
        pltpu.make_async_copy(most, most, back_recv.at[c]).wait()


def tail(wanted, conv_kernel, grads, mixed, raw, key_weight, value_weight):
    owners = lax.axis_size("dp")
    parts = lax.axis_size("db")
    requests, quarter = raw.shape[2], raw.shape[3]
    slots = wanted.shape[0]
    vmem = pl.BlockSpec(memory_space=pltpu.VMEM)
    anywhere = pl.BlockSpec(memory_space=pl.ANY)
    dma = pltpu.SemaphoreType.DMA
    heads = key_weight.shape[1] // HD
    rows = ENC // 4
    weights = (2, heads, 4, rows, HD)
    taps = (8, ENC)
    both = (2, CHUNKS, requests, quarter, LANES)
    return pl.pallas_call(
        functools.partial(tail_kernel, owners, parts),
        in_specs=[pl.BlockSpec(memory_space=pltpu.SMEM), vmem] + [anywhere] * 5,
        out_specs=[vmem, vmem, vmem],
        out_shape=[
            jax.ShapeDtypeStruct((CHUNKS, slots, quarter, LANES), BF16),
            jax.ShapeDtypeStruct(weights, BF16),
            jax.ShapeDtypeStruct(taps, F32),
        ],
        scratch_shapes=[
            pltpu.VMEM(grads.shape, BF16),
            pltpu.VMEM(mixed.shape, BF16),
            pltpu.VMEM(raw.shape, BF16),
            pltpu.VMEM(key_weight.shape, BF16),
            pltpu.VMEM(value_weight.shape, BF16),
            pltpu.VMEM(raw.shape, BF16),
            pltpu.VMEM(weights, BF16),
            pltpu.VMEM((8, 8, ENC), F32),
            dma((4,)),
            dma((requests // NBR,)),
            pltpu.VMEM((2, CHUNKS, requests // 2, quarter, LANES), BF16),
            pltpu.VMEM(both, BF16),
            pltpu.VMEM(both, BF16),
            pltpu.VMEM((CHUNKS, slots, quarter, LANES), BF16),
            pltpu.VMEM((heads, 4, rows, HD), BF16),
            pltpu.VMEM((heads, 4, rows, HD), BF16),
            pltpu.VMEM((2, 3, 4, rows, HD), BF16),
            pltpu.VMEM((2, 4, rows, HD), BF16),
            pltpu.VMEM((2, 3, rows, HD), BF16),
            pltpu.VMEM((4, 4) + taps, F32),
            pltpu.VMEM((4,) + taps, F32),
            dma((2, CHUNKS)),
            dma((2, CHUNKS)),
            dma((2, CHUNKS)),
            dma((2, CHUNKS)),
            dma((CHUNKS,)),
            dma((CHUNKS,)),
            dma((2, 8)),
            dma((2, 8)),
            dma((4, 6)),
            dma((4, 6)),
            dma((4, 3)),
            dma((4, 3)),
        ]
        + [pltpu.VMEM((requests, quarter, LANES), BF16)] * CHUNKS,
        compiler_params=pltpu.CompilerParams(
            collective_id=1, has_side_effects=True, vmem_limit_bytes=60 * 1024 * 1024
        ),
        cost_estimate=pl.CostEstimate(
            flops=17_000_000_000, bytes_accessed=30_000_000, transcendentals=0
        ),
    )(wanted, conv_kernel, grads, mixed, raw, key_weight, value_weight)


def spread_kernel(
    asked_ref, back_ref, w_ref, taps_ref, states_ref, gkw_ref, gvw_ref, gt_ref, used, count
):
    gkw_ref[...] = w_ref[0, 0].astype(F32)
    gvw_ref[...] = w_ref[1, 0].astype(F32)
    step = pl.program_id(0)

    @pl.when(step == 0)
    def _():
        gt_ref[...] = taps_ref[0:KW]
        count[0] = 0

        def note(owner, carry):
            for k in (0, 1):
                row = asked_ref[owner, 0, k]

                @pl.when(row >= 0)
                def _():
                    at = count[0]
                    used[0, at] = 2 * owner + k
                    used[1, at] = row
                    count[0] = at + 1

            return carry

        lax.fori_loop(0, asked_ref.shape[0], note, 0)

    @pl.when(step < CHUNKS)
    def _():
        states_ref[...] = jnp.zeros_like(states_ref)

        def add(index, carry):
            states_ref[used[1, index]] += back_ref[0, used[0, index]].astype(F32)
            return carry

        lax.fori_loop(0, count[0], add, 0)


def spread(asked, back, weights, taps, blocks):
    heads = weights.shape[1]
    slots, quarter = back.shape[1], back.shape[2]
    last = CHUNKS - 1
    head_cols = pl.BlockSpec((ENC, HD), lambda i: (0, i))
    return pl.pallas_call(
        spread_kernel,
        grid=(max(heads, CHUNKS),),
        in_specs=[
            pl.BlockSpec(memory_space=pltpu.SMEM),
            pl.BlockSpec((1, slots, quarter, LANES), lambda i: (jnp.minimum(i, last), 0, 0, 0)),
            pl.BlockSpec((2, 1, ENC, HD), lambda i: (0, i, 0, 0)),
            pl.BlockSpec((8, ENC), lambda i: (0, 0)),
        ],
        out_specs=[
            pl.BlockSpec((blocks, quarter, LANES), lambda i: (0, 0, jnp.minimum(i, last))),
            head_cols,
            head_cols,
            pl.BlockSpec((KW, ENC), lambda i: (0, 0)),
        ],
        out_shape=[
            jax.ShapeDtypeStruct((blocks, quarter, ENC), F32),
            jax.ShapeDtypeStruct((ENC, heads * HD), F32),
            jax.ShapeDtypeStruct((ENC, heads * HD), F32),
            jax.ShapeDtypeStruct((KW, ENC), F32),
        ],
        scratch_shapes=[pltpu.SMEM((2, slots), jnp.int32), pltpu.SMEM((1,), jnp.int32)],
        compiler_params=pltpu.CompilerParams(
            dimension_semantics=("arbitrary",), vmem_limit_bytes=60 * 1024 * 1024
        ),
        cost_estimate=pl.CostEstimate(flops=0, bytes_accessed=19_000_000, transcendentals=0),
    )(asked, back, weights.reshape(2, heads, ENC, HD), taps)


def tables_kernel(owner_ref, row_ref, slot_ref, wanted_ref, table_ref, rows, taken):
    owners = table_ref.shape[0]
    requests = slot_ref.shape[0]

    def clear(owner, carry):
        taken[owner] = 0
        for k in (0, 1):
            rows[2 * owner + k] = -1
            wanted_ref[2 * owner + k] = 0
        return carry

    lax.fori_loop(0, owners, clear, 0)
    for p in range(requests):
        owner = owner_ref[p % NBR, p // NBR]
        slot = 2 * owner + jnp.minimum(taken[owner], 1)
        taken[owner] = taken[owner] + 1
        slot_ref[p] = slot
        rows[slot] = row_ref[p % NBR, p // NBR]
        wanted_ref[slot] = p
    lane = lax.broadcasted_iota(jnp.int32, (1, LANES), 1)
    for owner in range(owners):
        table_ref[owner] = jnp.where(lane == 0, rows[2 * owner], rows[2 * owner + 1])


def tables(nbr_owner, nbr_row, owners):
    requests = nbr_owner.shape[0] * NBR
    smem = pl.BlockSpec(memory_space=pltpu.SMEM)
    return pl.pallas_call(
        tables_kernel,
        in_specs=[smem, smem],
        out_specs=[smem, smem, pl.BlockSpec(memory_space=pltpu.VMEM)],
        out_shape=[
            jax.ShapeDtypeStruct((requests,), jnp.int32),
            jax.ShapeDtypeStruct((2 * owners,), jnp.int32),
            jax.ShapeDtypeStruct((owners, 1, LANES), jnp.int32),
        ],
        scratch_shapes=[pltpu.SMEM((2 * owners,), jnp.int32), pltpu.SMEM((owners,), jnp.int32)],
        compiler_params=pltpu.CompilerParams(vmem_limit_bytes=60 * 1024 * 1024),
    )(nbr_owner.T, nbr_row.T)


def shards(
    queries, cotangent, db_states, key_weight, value_weight, conv_kernel, nbr_owner, nbr_row
):
    slots, wanted, table = tables(nbr_owner, nbr_row, lax.axis_size("dp"))
    raw, asked = fetch(slots, table, db_states)
    attended, grad_query, grads, mixed = core(
        queries, cotangent, raw, key_weight, value_weight, conv_kernel
    )
    back, weight_sums, taps_sum = tail(
        wanted, conv_kernel, grads, mixed, raw, key_weight, value_weight
    )
    grad_states, grad_key_weight, grad_value_weight, grad_kernel = spread(
        asked, back, weight_sums, taps_sum, db_states.shape[0]
    )
    return (
        attended,
        grad_query,
        grad_states,
        grad_key_weight,
        grad_value_weight,
        grad_kernel,
    )


def solution(mesh):
    return jax.shard_map(
        shards,
        mesh=mesh,
        in_specs=(
            P("dp", "db"),
            P("dp", "db"),
            P("dp", "db", None),
            P(None, "db"),
            P(None, "db"),
            P(),
            P("dp", None),
            P("dp", None),
        ),
        out_specs=(
            P("dp", "db"),
            P("dp", "db"),
            P("dp", "db", None),
            P(None, "db"),
            P(None, "db"),
            P(),
        ),
        check_vma=False,
    )
```

```python
import functools
import math

import jax
import jax.numpy as jnp
from jax import lax
from jax.experimental import pallas as pl
from jax.experimental.pallas import tpu as pltpu
from jax.sharding import PartitionSpec as P

HD = 128
ENC = 896
SPAN = 64
NBR = 2
NLEN = 128
KW = 3
LANES = 128
CHUNKS = ENC // LANES
F32 = jnp.float32
BF16 = jnp.bfloat16
NT = (((1,), (1,)), ((), ()))


def shifted(block):
    rows = block.shape[0]
    at = lax.broadcasted_iota(jnp.int32, block.shape, 0)
    down = jnp.where(at == 0, 0.0, pltpu.roll(block, 1, 0))
    up = jnp.where(at == rows - 1, 0.0, pltpu.roll(block, rows - 1, 0))
    return down, up


def core_kernel(
    heads,
    q_ref,
    g_ref,
    raw_ref,
    kw_ref,
    vw_ref,
    taps_ref,
    att_ref,
    gq_ref,
    grads_ref,
    mixed_ref,
    mixed_s,
    kv_s,
    both_s,
    stacked_s,
):
    scale = 1.0 / math.sqrt(HD)
    for c in range(CHUNKS):
        cols = slice(c * LANES, (c + 1) * LANES)
        for n in range(NBR):
            raw = raw_ref[c, :, n].reshape(NLEN, LANES).astype(F32)
            down, up = shifted(raw)
            mixed = taps_ref[0:1, cols] * down
            mixed = mixed + taps_ref[1:2, cols] * raw
            mixed = mixed + taps_ref[2:3, cols] * up
            mixed_s[n * NLEN : (n + 1) * NLEN, cols] = mixed.astype(BF16)
    mixed = mixed_s[...]
    mixed_ref[...] = mixed.T

    zeros = jnp.zeros((SPAN, HD), BF16)
    for place, weight in enumerate((kw_ref, vw_ref)):
        states = jnp.dot(mixed, weight[...], preferred_element_type=F32).astype(BF16)
        for h in range(heads):
            at = (2 * h + place) * HD
            kv_s[:, at : at + HD] = states[:, h * HD : (h + 1) * HD]

    def diag(h):
        q = q_ref[:, h * HD : (h + 1) * HD]
        g = g_ref[:, h * HD : (h + 1) * HD]
        return jnp.concatenate(
            [jnp.concatenate([q, zeros], axis=1), jnp.concatenate([zeros, g], axis=1)], axis=0
        )

    for h in range(heads):
        wide = slice(2 * h * HD, (2 * h + 2) * HD)
        both_s[h] = lax.dot_general(diag(h), kv_s[:, wide], NT, preferred_element_type=F32)
    for h in range(heads):
        scores = both_s[h, :SPAN] * scale
        grad_probs = both_s[h, SPAN:]
        expo = jnp.exp(scores - jnp.max(scores, axis=-1, keepdims=True))
        probs = expo / jnp.sum(expo, axis=-1, keepdims=True)
        inner = jnp.sum(grad_probs * probs, axis=-1, keepdims=True)
        grad_scores = scale * probs * (grad_probs - inner)
        stacked_s[h, :SPAN] = grad_scores.astype(BF16)
        stacked_s[h, SPAN:] = probs.astype(BF16)
    for h in range(heads):
        wide = slice(2 * h * HD, (2 * h + 2) * HD)
        cols = slice(h * HD, (h + 1) * HD)
        out = jnp.dot(stacked_s[h], kv_s[:, wide], preferred_element_type=F32)
        gq_ref[:, cols] = out[:SPAN, :HD].astype(BF16)
        att_ref[:, cols] = out[SPAN:, HD:].astype(BF16)
    for h in range(heads):
        cols = slice(h * HD, (h + 1) * HD)
        pair = lax.dot_general(
            stacked_s[h], diag(h), (((0,), (0,)), ((), ())), preferred_element_type=F32
        ).astype(BF16)
        grads_ref[0, :, cols] = pair[:, :HD]
        grads_ref[1, :, cols] = pair[:, HD:]


def core(queries, cotangent, raw, key_weight, value_weight, conv_kernel):
    tokens, width = queries.shape
    heads = width // HD
    spans = tokens // SPAN
    keys_here = NBR * NLEN
    keys_all = spans * keys_here
    whole = lambda shape: pl.BlockSpec(
        shape, lambda i: (0,) * len(shape), pipeline_mode=pl.Buffered(1)
    )
    span_rows = pl.BlockSpec((SPAN, width), lambda i: (i, 0))
    parts, quarter = raw.shape[1], raw.shape[3]
    blocks = pl.BlockSpec((CHUNKS, parts, NBR, quarter, LANES), lambda i: (0, 0, i, 0, 0))
    return pl.pallas_call(
        functools.partial(core_kernel, heads),
        grid=(spans,),
        in_specs=[
            span_rows,
            span_rows,
            blocks,
            whole((ENC, width)),
            whole((ENC, width)),
            whole((KW, ENC)),
        ],
        out_specs=[
            span_rows,
            span_rows,
            pl.BlockSpec((2, keys_here, width), lambda i: (0, i, 0)),
            pl.BlockSpec((ENC, keys_here), lambda i: (0, i)),
        ],
        out_shape=[
            jax.ShapeDtypeStruct((tokens, width), BF16),
            jax.ShapeDtypeStruct((tokens, width), BF16),
            jax.ShapeDtypeStruct((2, keys_all, width), BF16),
            jax.ShapeDtypeStruct((ENC, keys_all), BF16),
        ],
        scratch_shapes=[
            pltpu.VMEM((keys_here, ENC), BF16),
            pltpu.VMEM((keys_here, 2 * width), BF16),
            pltpu.VMEM((heads, 2 * SPAN, keys_here), F32),
            pltpu.VMEM((heads, 2 * SPAN, keys_here), BF16),
        ],
        compiler_params=pltpu.CompilerParams(
            dimension_semantics=("arbitrary",), vmem_limit_bytes=60 * 1024 * 1024
        ),
        cost_estimate=pl.CostEstimate(
            flops=10_000_000_000, bytes_accessed=30_000_000, transcendentals=1_200_000
        ),
    )(queries, cotangent, raw, key_weight, value_weight, conv_kernel)


def dp_peer(step):
    me = lax.axis_index("dp")
    z = lax.rem(me // 8 + step // 8, 4)
    x = lax.rem(lax.rem(me // 2, 4) + lax.rem(step // 2, 4), 4)
    return z * 8 + x * 2 + lax.rem(me + step, 2)


def fetch_kernel(
    owners,
    parts,
    slot_ref,
    table_ref,
    states_ref,
    raw_ref,
    asked_ref,
    asked_s,
    send,
    ask_sem,
    local_sem,
    send_sem,
    recv_sem,
    y_send,
    y_recv,
    *recv,
):
    me = lax.axis_index("dp")
    y = lax.axis_index("db")
    right = lax.rem(y + 1, parts)
    left = lax.rem(y + parts - 1, parts)
    requests = raw_ref.shape[2]
    half = requests // 2
    capacity = 2
    others = owners - 1

    barrier = pltpu.get_barrier_semaphore()

    def greet(step, carry):
        pl.semaphore_signal(barrier, inc=1, device_id={"dp": dp_peer(step)})
        return carry

    lax.fori_loop(1, owners, greet, 0)
    for side in (left, right):
        pl.semaphore_signal(barrier, inc=1, device_id={"db": side})
    pl.semaphore_wait(barrier, others + 2)

    def ask(step, carry):
        peer = dp_peer(step)
        pltpu.make_async_remote_copy(
            src_ref=table_ref.at[peer],
            dst_ref=asked_ref.at[me],
            send_sem=ask_sem.at[0],
            recv_sem=ask_sem.at[1],
            device_id={"dp": peer},
        ).start()
        return carry

    lax.fori_loop(1, owners, ask, 0)
    asked_ref[me] = table_ref[me]
    most = asked_ref.at[pl.ds(0, others)]
    pltpu.make_async_copy(most, most, ask_sem.at[1]).wait()
    pltpu.make_async_copy(asked_ref, asked_s, local_sem).start()
    pltpu.make_async_copy(asked_ref, asked_s, local_sem).wait()

    def replies(c):
        cols = slice(c * LANES, (c + 1) * LANES)

        def reply(step, carry):
            peer = dp_peer(step)
            for k in range(capacity):
                row = jnp.maximum(asked_s[peer, 0, k], 0)
                send[c, capacity * peer + k] = states_ref[row, :, cols]
            pltpu.make_async_remote_copy(
                src_ref=send.at[c, pl.ds(capacity * peer, capacity)],
                dst_ref=recv[c].at[pl.ds(capacity * me, capacity)],
                send_sem=send_sem.at[c],
                recv_sem=recv_sem.at[c],
                device_id={"dp": peer},
            ).start()
            return carry

        lax.fori_loop(1, owners, reply, 0)
        for k in range(capacity):
            row = jnp.maximum(asked_s[me, 0, k], 0)
            recv[c][capacity * me + k] = states_ref[row, :, cols]

    ahead = 2
    for c in range(ahead):
        replies(c)

    def along_y(kind, c, part, rows, side):
        block = raw_ref.at[c, part, rows]
        return pltpu.make_async_remote_copy(
            src_ref=block,
            dst_ref=block,
            send_sem=y_send.at[kind, c],
            recv_sem=y_recv.at[kind, c],
            device_id={"db": side},
        )

    everything, low, high = pl.ds(0, requests), pl.ds(0, half), pl.ds(half, requests - half)

    def arrivals(kind, c):
        far = lax.rem(y + 2, parts)
        part, rows = ((left, everything), (right, everything), (far, low), (far, high))[kind]
        return along_y(kind, c, part, rows, right)

    for c in range(CHUNKS + 1):
        if c + ahead < CHUNKS:
            replies(c + ahead)
        if c < CHUNKS:
            most = recv[c].at[pl.ds(0, capacity * others)]
            pltpu.make_async_copy(most, most, recv_sem.at[c]).wait()
            for p in range(requests):
                raw_ref[c, y, p] = recv[c][slot_ref[p]]
            along_y(0, c, y, everything, right).start()
            along_y(1, c, y, everything, left).start()
        if c >= 1:
            arrivals(0, c - 1).wait_recv()
            along_y(2, c - 1, left, low, right).start()
            arrivals(1, c - 1).wait_recv()
            along_y(3, c - 1, right, high, left).start()
    for c in range(CHUNKS):
        arrivals(2, c).wait_recv()
        arrivals(3, c).wait_recv()
        along_y(0, c, y, everything, right).wait_send()
        along_y(1, c, y, everything, left).wait_send()
        along_y(2, c, left, low, right).wait_send()
        along_y(3, c, right, high, left).wait_send()
        most = send.at[c, pl.ds(0, capacity * others)]
        pltpu.make_async_copy(most, most, send_sem.at[c]).wait()
    most = table_ref.at[pl.ds(0, others)]
    pltpu.make_async_copy(most, most, ask_sem.at[0]).wait()


def fetch(slots, table, states):
    owners = table.shape[0]
    parts = lax.axis_size("db")
    requests = slots.shape[0]
    quarter = states.shape[1]
    vmem = pl.BlockSpec(memory_space=pltpu.VMEM)
    dma = pltpu.SemaphoreType.DMA
    return pl.pallas_call(
        functools.partial(fetch_kernel, owners, parts),
        in_specs=[pl.BlockSpec(memory_space=pltpu.SMEM), vmem, vmem],
        out_specs=[vmem, vmem],
        out_shape=[
            jax.ShapeDtypeStruct((CHUNKS, parts, requests, quarter, LANES), BF16),
            jax.ShapeDtypeStruct(table.shape, jnp.int32),
        ],
        scratch_shapes=[
            pltpu.SMEM(table.shape, jnp.int32),
            pltpu.VMEM((CHUNKS, 2 * owners, quarter, LANES), BF16),
            dma((2,)),
            dma,
            dma((CHUNKS,)),
            dma((CHUNKS,)),
            dma((4, CHUNKS)),
            dma((4, CHUNKS)),
        ]
        + [pltpu.VMEM((2 * owners, quarter, LANES), BF16)] * CHUNKS,
        compiler_params=pltpu.CompilerParams(
            collective_id=0, has_side_effects=True, vmem_limit_bytes=60 * 1024 * 1024
        ),
        cost_estimate=pl.CostEstimate(flops=0, bytes_accessed=16_000_000, transcendentals=0),
    )(slots, table, states)


def tail_kernel(
    owners,
    parts,
    req_ref,
    conv_ref,
    grads_hbm,
    mixed_hbm,
    raw_hbm,
    kw_hbm,
    vw_hbm,
    back_ref,
    wsum_ref,
    tsum_ref,
    grads,
    mixed_t,
    raw_ref,
    kw_ref,
    vw_ref,
    part_ref,
    w_ref,
    taps_acc,
    load_sem,
    grads_sem,
    from_far,
    onward,
    from_near,
    send,
    sibling_w,
    pair_w,
    first_in,
    first_sum,
    second_in,
    taps_in,
    taps_now,
    far_send,
    far_recv,
    near_send,
    near_recv,
    back_send,
    back_recv,
    pair_send,
    pair_recv,
    axis_send,
    axis_recv,
    taps_send,
    taps_recv,
    *mine,
):
    me = lax.axis_index("dp")
    y = lax.axis_index("db")
    z, x, core = me // 8, lax.rem(me // 2, 4), lax.rem(me, 2)
    sibling = me + 1 - 2 * core
    right = lax.rem(y + 1, parts)
    left = lax.rem(y + parts - 1, parts)
    far = lax.rem(y + 2, parts)
    requests = part_ref.shape[2]
    keys_here = NBR * NLEN
    spans = requests // NBR

    def load(index):
        pair = ((kw_hbm, kw_ref), (vw_hbm, vw_ref), (raw_hbm, raw_ref), (mixed_hbm, mixed_t))[index]
        return pltpu.make_async_copy(*pair, load_sem.at[index])

    def load_grads(span):
        rows = pl.ds(pl.multiple_of(span * keys_here, keys_here), keys_here)
        return pltpu.make_async_copy(
            grads_hbm.at[:, rows], grads.at[:, rows], grads_sem.at[span]
        )

    load(0).start()
    load(1).start()
    for span in range(spans):
        load_grads(span).start()
    load(2).start()
    load(3).start()
    taps_acc[...] = jnp.zeros_like(taps_acc)
    half = requests // 2
    capacity = 2
    others = owners - 1
    low, high = pl.ds(0, half), pl.ds(half, requests - half)

    def x_peer(step):
        return z * 8 + lax.rem(x + step, 4) * 2 + core

    def z_peer(step):
        return lax.rem(z + step, 4) * 8 + x * 2 + core

    barrier = pltpu.get_barrier_semaphore()

    def greet(step, carry):
        pl.semaphore_signal(barrier, inc=1, device_id={"dp": dp_peer(step)})
        return carry

    lax.fori_loop(1, owners, greet, 0)
    for other in range(1, parts):
        pl.semaphore_signal(barrier, inc=1, device_id={"db": lax.rem(y + other, parts)})
    pl.semaphore_wait(barrier, others + parts - 1)

    def remote(src, dst, send_sem, recv_sem, where):
        return pltpu.make_async_remote_copy(
            src_ref=src, dst_ref=dst, send_sem=send_sem, recv_sem=recv_sem, device_id=where
        )

    def grad_columns(chunks):
        cols = slice(chunks[0] * LANES, (chunks[-1] + 1) * LANES)

        def one(span, carry):
            rows = pl.ds(pl.multiple_of(span * keys_here, keys_here), keys_here)
            whole = lax.dot_general(
                grads[0, rows], kw_ref[cols], NT, preferred_element_type=F32
            ) + lax.dot_general(grads[1, rows], vw_ref[cols], NT, preferred_element_type=F32)
            for i, c in enumerate(chunks):
                lanes = slice(c * LANES, (c + 1) * LANES)
                for n in range(NBR):
                    gm = whole[n * NLEN : (n + 1) * NLEN, i * LANES : (i + 1) * LANES]
                    gm_down, gm_up = shifted(gm)
                    grad = conv_ref[0:1, lanes] * gm_up
                    grad = grad + conv_ref[1:2, lanes] * gm
                    grad = grad + conv_ref[2:3, lanes] * gm_down
                    part_ref[c, :, span * NBR + n] = grad.astype(BF16).reshape(parts, -1, LANES)
                    raw = raw_ref[c, :, span * NBR + n].reshape(NLEN, LANES).astype(F32)
                    for w, other in enumerate((gm_up, gm, gm_down)):
                        taps_acc[w, :, lanes] += jnp.sum(
                            (raw * other).reshape(NLEN // 8, 8, LANES), axis=0
                        )
            return carry

        lax.fori_loop(0, spans, one, 0)

    def far_copy(side, c):
        rows, to = ((low, right), (high, left))[side]
        return remote(
            part_ref.at[c, far, rows],
            from_far.at[side, c],
            far_send.at[side, c],
            far_recv.at[side, c],
            {"db": to},
        )

    def near_copy(side, c):
        return remote(
            onward.at[side, c],
            from_near.at[side, c],
            near_send.at[side, c],
            near_recv.at[side, c],
            {"db": (right, left)[side]},
        )

    def forward(c):
        far_copy(0, c).wait_recv()
        added = part_ref[c, right, 0:half].astype(F32) + from_far[0, c].astype(F32)
        onward[0, c, 0:half] = added.astype(BF16)
        onward[0, c, half:requests] = part_ref[c, right, half:requests]
        near_copy(0, c).start()
        far_copy(1, c).wait_recv()
        added = part_ref[c, left, half:requests].astype(F32) + from_far[1, c].astype(F32)
        onward[1, c, half:requests] = added.astype(BF16)
        onward[1, c, 0:half] = part_ref[c, left, 0:half]
        near_copy(1, c).start()

    def give_back(c):
        near_copy(0, c).wait_recv()
        near_copy(1, c).wait_recv()
        total = part_ref[c, y].astype(F32) + from_near[0, c].astype(F32)
        mine[c][...] = (total + from_near[1, c].astype(F32)).astype(BF16)

        def one(step, carry):
            peer = dp_peer(step)
            for k in range(capacity):
                send[c, capacity * peer + k] = mine[c][req_ref[capacity * peer + k]]
            remote(
                send.at[c, pl.ds(capacity * peer, capacity)],
                back_ref.at[c, pl.ds(capacity * me, capacity)],
                back_send.at[c],
                back_recv.at[c],
                {"dp": peer},
            ).start()
            return carry

        lax.fori_loop(1, owners, one, 0)
        for k in range(capacity):
            back_ref[c, capacity * me + k] = mine[c][req_ref[capacity * me + k]]

    first_at, second_at = (x, z), (z, x)
    first_peer, second_peer = (x_peer, z_peer), (z_peer, x_peer)
    order = [(d, h) for d in (1, 2, 3, 0) for h in (0, 1)]

    def group(h, step):
        return h * 4 + lax.rem(first_at[h] + step, 4)

    def pair_copy(d, h):
        g = group(h, d)
        return remote(
            w_ref.at[1 - core, g],
            sibling_w.at[g],
            pair_send.at[0, h * 4 + d],
            pair_recv.at[0, h * 4 + d],
            {"dp": sibling},
        )

    def weight_terms(which, d):
        def columns(h):
            return grads[which, :, pl.ds(pl.multiple_of(group(h, d) * HD, HD), HD)]

        both = jnp.concatenate([columns(0), columns(1)], axis=1)
        term = jnp.dot(mixed_t[...], both, preferred_element_type=F32)
        for h in (0, 1):
            block = term[:, h * HD : (h + 1) * HD].astype(BF16)
            w_ref[which, group(h, d)] = block.reshape(4, -1, HD)

    def first_copy(d, h):
        return remote(
            pair_w.at[group(h, d)],
            first_in.at[h, d - 1],
            axis_send.at[0, h * 3 + d - 1],
            axis_recv.at[0, h * 3 + d - 1],
            {"dp": first_peer[h](d)},
        )

    def far_half(side, h):
        at = (0, h * 3 + 1) if side == 0 else (4, h * 3)
        return remote(
            pair_w.at[group(h, 2), pl.ds(2 * side, 2)],
            first_in.at[h, 1, pl.ds(2 * side, 2)],
            axis_send.at[at],
            axis_recv.at[at],
            {"dp": first_peer[h](1 + 2 * side)},
        )

    def relay(side, h, back):
        at = (3, h * 3 + 1) if side == 0 else (4, h * 3 + 1)
        block = wsum_ref.at[core, group(h, back), pl.ds(2 * side, 2)]
        return remote(
            block,
            block,
            axis_send.at[at],
            axis_recv.at[at],
            {"dp": first_peer[h](1 + 2 * side)},
        )

    def second_copy(d, h):
        return remote(
            first_sum.at[h, lax.rem(second_at[h] + d, 4)],
            second_in.at[h, d - 1],
            axis_send.at[1, h * 3 + d - 1],
            axis_recv.at[1, h * 3 + d - 1],
            {"dp": second_peer[h](d)},
        )

    def second_gather(d, h, back):
        block = wsum_ref.at[core, group(h, 0), lax.rem(second_at[h] + back, 4)]
        return remote(
            block,
            block,
            axis_send.at[2, h * 3 + d - 1],
            axis_recv.at[2, h * 3 + d - 1],
            {"dp": second_peer[h](d)},
        )

    def first_gather(d, h, back):
        block = wsum_ref.at[core, group(h, back)]
        return remote(
            block,
            block,
            axis_send.at[3, h * 3 + d - 1],
            axis_recv.at[3, h * 3 + d - 1],
            {"dp": first_peer[h](d)},
        )

    def pair_gather(d, h, which):
        block = wsum_ref.at[which, group(h, 4 - d)]
        return remote(
            block,
            block,
            pair_send.at[1, h * 4 + d],
            pair_recv.at[1, h * 4 + d],
            {"dp": sibling},
        )

    def pair_sum(d, h):
        pair_copy(d, h).wait_recv()
        g = group(h, d)
        total = w_ref[core, g].astype(F32) + sibling_w[g].astype(F32)
        if d in (1, 3):
            side = d // 2
            far_half(side, h).wait_recv()
            added = total[2 * side : 2 * side + 2]
            added = added + first_in[h, 1, 2 * side : 2 * side + 2].astype(F32)
            pair_w[g, 2 * side : 2 * side + 2] = added.astype(BF16)
            pair_w[g, 2 - 2 * side : 4 - 2 * side] = total[2 - 2 * side : 4 - 2 * side].astype(BF16)
            first_copy(d, h).start()
        else:
            pair_w[g] = total.astype(BF16)
            if d:
                far_half(0, h).start()
                far_half(1, h).start()

    def sum_first(h):
        for d in (1, 3):
            first_copy(d, h).wait_recv()
        total = pair_w[group(h, 0)].astype(F32)
        for d in (1, 3):
            total = total + first_in[h, d - 1].astype(F32)
        first_sum[h] = total.astype(BF16)
        for d in (1, 2, 3):
            second_copy(d, h).start()

    def sum_second(h):
        for d in (1, 2, 3):
            second_copy(d, h).wait_recv()
        total = first_sum[h, second_at[h]].astype(F32)
        for d in (1, 2, 3):
            total = total + second_in[h, d - 1].astype(F32)
        wsum_ref[core, group(h, 0), second_at[h]] = total.astype(BF16)
        for d in (1, 2, 3):
            second_gather(d, h, 0).start()

    def gather_first(h):
        for d in (1, 2, 3):
            second_gather(d, h, 4 - d).wait_recv()
        for d in (1, 3):
            first_gather(d, h, 0).start()
        pair_gather(0, h, core).start()

    def gather_relay(h):
        for side, d in ((0, 1), (1, 3)):
            first_gather(d, h, 4 - d).wait_recv()
            relay(side, h, 4 - d).start()
            pair_gather(d, h, core).start()

    def gather_far(h):
        relay(0, h, 2).wait_recv()
        relay(1, h, 2).wait_recv()
        pair_gather(2, h, core).start()

    stages = (
        (2, core, lambda step: {"dp": sibling}),
        (4, x, lambda step: {"dp": x_peer(step)}),
        (4, z, lambda step: {"dp": z_peer(step)}),
        (parts, y, lambda step: {"db": lax.rem(y + step, parts)}),
    )

    def taps_copy(stage, d):
        count, at, peer = stages[stage]
        return remote(
            taps_now.at[stage],
            taps_in.at[stage, at],
            taps_send.at[stage, d - 1],
            taps_recv.at[stage, d - 1],
            peer(d),
        )

    def taps_start(stage, value):
        count, at, peer = stages[stage]
        taps_now[stage] = value
        taps_in[stage, at] = value
        for d in range(1, count):
            taps_copy(stage, d).start()

    def taps_end(stage):
        count = stages[stage][0]
        for d in range(1, count):
            taps_copy(stage, d).wait_recv()
        total = taps_in[stage, 0]
        for other in range(1, count):
            total = total + taps_in[stage, other]
        return total

    def start_far(chunks):
        for c in chunks:
            far_copy(0, c).start()
            far_copy(1, c).start()

    def weight_step(d):
        weight_terms(1 - core, d)
        pair_copy(d, 0).start()
        pair_copy(d, 1).start()
        weight_terms(core, d)

    def pair_sums(d):
        pair_sum(d, 0)
        pair_sum(d, 1)

    for span in range(spans):
        load_grads(span).wait()
    for index in (0, 1, 2):
        load(index).wait()
    grad_columns((0, 1))
    start_far((0, 1))
    load(3).wait()
    weight_step(2)
    forward(0)
    forward(1)
    weight_step(1)
    pair_sums(2)
    give_back(0)
    weight_step(3)
    pair_sums(1)
    give_back(1)
    weight_step(0)
    pair_sums(3)
    pair_sums(0)
    grad_columns((2, 3))
    start_far((2, 3))
    grad_columns((4, 5))
    start_far((4, 5))
    forward(2)
    forward(3)
    sum_first(0)
    sum_first(1)
    grad_columns((6,))
    start_far((6,))
    give_back(2)
    forward(4)
    forward(5)
    sum_second(0)
    sum_second(1)
    taps_start(0, jnp.sum(taps_acc[...], axis=1))
    give_back(3)
    forward(6)
    gather_first(0)
    gather_first(1)
    taps_start(1, taps_end(0))
    give_back(4)
    taps_start(2, taps_end(1))
    give_back(5)
    gather_relay(0)
    gather_relay(1)
    taps_start(3, taps_end(2))
    give_back(6)
    gather_far(0)
    gather_far(1)
    tsum_ref[...] = taps_end(3)

    for d, h in order:
        pair_gather(d, h, 1 - core).wait_recv()
        pair_gather(d, h, core).wait_send()
        pair_copy(d, h).wait_send()
        if d:
            second_copy(d, h).wait_send()
            second_gather(d, h, 0).wait_send()
        if d in (1, 3):
            first_copy(d, h).wait_send()
            first_gather(d, h, 0).wait_send()
            far_half(d // 2, h).wait_send()
            relay(d // 2, h, 4 - d).wait_send()
    for stage in range(4):
        for d in range(1, stages[stage][0]):
            taps_copy(stage, d).wait_send()
    for c in range(CHUNKS):
        for side in (0, 1):
            far_copy(side, c).wait_send()
            near_copy(side, c).wait_send()
        most = send.at[c, pl.ds(0, capacity * others)]
        pltpu.make_async_copy(most, most, back_send.at[c]).wait()
        most = back_ref.at[c, pl.ds(0, capacity * others)]
        pltpu.make_async_copy(most, most, back_recv.at[c]).wait()


def tail(wanted, conv_kernel, grads, mixed, raw, key_weight, value_weight):
    owners = lax.axis_size("dp")
    parts = lax.axis_size("db")
    requests, quarter = raw.shape[2], raw.shape[3]
    slots = wanted.shape[0]
    vmem = pl.BlockSpec(memory_space=pltpu.VMEM)
    anywhere = pl.BlockSpec(memory_space=pl.ANY)
    dma = pltpu.SemaphoreType.DMA
    heads = key_weight.shape[1] // HD
    rows = ENC // 4
    weights = (2, heads, 4, rows, HD)
    taps = (8, ENC)
    both = (2, CHUNKS, requests, quarter, LANES)
    return pl.pallas_call(
        functools.partial(tail_kernel, owners, parts),
        in_specs=[pl.BlockSpec(memory_space=pltpu.SMEM), vmem] + [anywhere] * 5,
        out_specs=[vmem, vmem, vmem],
        out_shape=[
            jax.ShapeDtypeStruct((CHUNKS, slots, quarter, LANES), BF16),
            jax.ShapeDtypeStruct(weights, BF16),
            jax.ShapeDtypeStruct(taps, F32),
        ],
        scratch_shapes=[
            pltpu.VMEM(grads.shape, BF16),
            pltpu.VMEM(mixed.shape, BF16),
            pltpu.VMEM(raw.shape, BF16),
            pltpu.VMEM(key_weight.shape, BF16),
            pltpu.VMEM(value_weight.shape, BF16),
            pltpu.VMEM(raw.shape, BF16),
            pltpu.VMEM(weights, BF16),
            pltpu.VMEM((8, 8, ENC), F32),
            dma((4,)),
            dma((requests // NBR,)),
            pltpu.VMEM((2, CHUNKS, requests // 2, quarter, LANES), BF16),
            pltpu.VMEM(both, BF16),
            pltpu.VMEM(both, BF16),
            pltpu.VMEM((CHUNKS, slots, quarter, LANES), BF16),
            pltpu.VMEM((heads, 4, rows, HD), BF16),
            pltpu.VMEM((heads, 4, rows, HD), BF16),
            pltpu.VMEM((2, 3, 4, rows, HD), BF16),
            pltpu.VMEM((2, 4, rows, HD), BF16),
            pltpu.VMEM((2, 3, rows, HD), BF16),
            pltpu.VMEM((4, 4) + taps, F32),
            pltpu.VMEM((4,) + taps, F32),
            dma((2, CHUNKS)),
            dma((2, CHUNKS)),
            dma((2, CHUNKS)),
            dma((2, CHUNKS)),
            dma((CHUNKS,)),
            dma((CHUNKS,)),
            dma((2, 8)),
            dma((2, 8)),
            dma((5, 6)),
            dma((5, 6)),
            dma((4, 3)),
            dma((4, 3)),
        ]
        + [pltpu.VMEM((requests, quarter, LANES), BF16)] * CHUNKS,
        compiler_params=pltpu.CompilerParams(
            collective_id=1, has_side_effects=True, vmem_limit_bytes=60 * 1024 * 1024
        ),
        cost_estimate=pl.CostEstimate(
            flops=17_000_000_000, bytes_accessed=30_000_000, transcendentals=0
        ),
    )(wanted, conv_kernel, grads, mixed, raw, key_weight, value_weight)


def spread_kernel(
    asked_ref, back_ref, w_ref, taps_ref, states_ref, gkw_ref, gvw_ref, gt_ref, used, count
):
    gkw_ref[...] = w_ref[0, 0].astype(F32)
    gvw_ref[...] = w_ref[1, 0].astype(F32)
    step = pl.program_id(0)

    @pl.when(step == 0)
    def _():
        gt_ref[...] = taps_ref[0:KW]
        count[0] = 0

        def note(owner, carry):
            for k in (0, 1):
                row = asked_ref[owner, 0, k]

                @pl.when(row >= 0)
                def _():
                    at = count[0]
                    used[0, at] = 2 * owner + k
                    used[1, at] = row
                    count[0] = at + 1

            return carry

        lax.fori_loop(0, asked_ref.shape[0], note, 0)

    @pl.when(step < CHUNKS)
    def _():
        states_ref[...] = jnp.zeros_like(states_ref)

        def add(index, carry):
            states_ref[used[1, index]] += back_ref[0, used[0, index]].astype(F32)
            return carry

        lax.fori_loop(0, count[0], add, 0)


def spread(asked, back, weights, taps, blocks):
    heads = weights.shape[1]
    slots, quarter = back.shape[1], back.shape[2]
    last = CHUNKS - 1
    head_cols = pl.BlockSpec((ENC, HD), lambda i: (0, i))
    return pl.pallas_call(
        spread_kernel,
        grid=(max(heads, CHUNKS),),
        in_specs=[
            pl.BlockSpec(memory_space=pltpu.SMEM),
            pl.BlockSpec((1, slots, quarter, LANES), lambda i: (jnp.minimum(i, last), 0, 0, 0)),
            pl.BlockSpec((2, 1, ENC, HD), lambda i: (0, i, 0, 0)),
            pl.BlockSpec((8, ENC), lambda i: (0, 0)),
        ],
        out_specs=[
            pl.BlockSpec((blocks, quarter, LANES), lambda i: (0, 0, jnp.minimum(i, last))),
            head_cols,
            head_cols,
            pl.BlockSpec((KW, ENC), lambda i: (0, 0)),
        ],
        out_shape=[
            jax.ShapeDtypeStruct((blocks, quarter, ENC), F32),
            jax.ShapeDtypeStruct((ENC, heads * HD), F32),
            jax.ShapeDtypeStruct((ENC, heads * HD), F32),
            jax.ShapeDtypeStruct((KW, ENC), F32),
        ],
        scratch_shapes=[pltpu.SMEM((2, slots), jnp.int32), pltpu.SMEM((1,), jnp.int32)],
        compiler_params=pltpu.CompilerParams(
            dimension_semantics=("arbitrary",), vmem_limit_bytes=60 * 1024 * 1024
        ),
        cost_estimate=pl.CostEstimate(flops=0, bytes_accessed=19_000_000, transcendentals=0),
    )(asked, back, weights.reshape(2, heads, ENC, HD), taps)


def tables_kernel(owner_ref, row_ref, slot_ref, wanted_ref, table_ref, rows, taken):
    owners = table_ref.shape[0]
    requests = slot_ref.shape[0]

    def clear(owner, carry):
        taken[owner] = 0
        for k in (0, 1):
            rows[2 * owner + k] = -1
            wanted_ref[2 * owner + k] = 0
        return carry

    lax.fori_loop(0, owners, clear, 0)
    for p in range(requests):
        owner = owner_ref[p % NBR, p // NBR]
        slot = 2 * owner + jnp.minimum(taken[owner], 1)
        taken[owner] = taken[owner] + 1
        slot_ref[p] = slot
        rows[slot] = row_ref[p % NBR, p // NBR]
        wanted_ref[slot] = p
    lane = lax.broadcasted_iota(jnp.int32, (1, LANES), 1)
    for owner in range(owners):
        table_ref[owner] = jnp.where(lane == 0, rows[2 * owner], rows[2 * owner + 1])


def tables(nbr_owner, nbr_row, owners):
    requests = nbr_owner.shape[0] * NBR
    smem = pl.BlockSpec(memory_space=pltpu.SMEM)
    return pl.pallas_call(
        tables_kernel,
        in_specs=[smem, smem],
        out_specs=[smem, smem, pl.BlockSpec(memory_space=pltpu.VMEM)],
        out_shape=[
            jax.ShapeDtypeStruct((requests,), jnp.int32),
            jax.ShapeDtypeStruct((2 * owners,), jnp.int32),
            jax.ShapeDtypeStruct((owners, 1, LANES), jnp.int32),
        ],
        scratch_shapes=[pltpu.SMEM((2 * owners,), jnp.int32), pltpu.SMEM((owners,), jnp.int32)],
        compiler_params=pltpu.CompilerParams(vmem_limit_bytes=60 * 1024 * 1024),
    )(nbr_owner.T, nbr_row.T)


def shards(
    queries, cotangent, db_states, key_weight, value_weight, conv_kernel, nbr_owner, nbr_row
):
    slots, wanted, table = tables(nbr_owner, nbr_row, lax.axis_size("dp"))
    raw, asked = fetch(slots, table, db_states)
    attended, grad_query, grads, mixed = core(
        queries, cotangent, raw, key_weight, value_weight, conv_kernel
    )
    back, weight_sums, taps_sum = tail(
        wanted, conv_kernel, grads, mixed, raw, key_weight, value_weight
    )
    grad_states, grad_key_weight, grad_value_weight, grad_kernel = spread(
        asked, back, weight_sums, taps_sum, db_states.shape[0]
    )
    return (
        attended,
        grad_query,
        grad_states,
        grad_key_weight,
        grad_value_weight,
        grad_kernel,
    )


def solution(mesh):
    return jax.shard_map(
        shards,
        mesh=mesh,
        in_specs=(
            P("dp", "db"),
            P("dp", "db"),
            P("dp", "db", None),
            P(None, "db"),
            P(None, "db"),
            P(),
            P("dp", None),
            P("dp", None),
        ),
        out_specs=(
            P("dp", "db"),
            P("dp", "db"),
            P("dp", "db", None),
            P(None, "db"),
            P(None, "db"),
            P(),
        ),
        check_vma=False,
    )
```

```python
import functools
import math

import jax
import jax.numpy as jnp
from jax import lax
from jax.experimental import pallas as pl
from jax.experimental.pallas import tpu as pltpu
from jax.sharding import PartitionSpec as P

HD = 128
ENC = 896
SPAN = 64
NBR = 2
NLEN = 128
KW = 3
LANES = 128
CHUNKS = ENC // LANES
F32 = jnp.float32
BF16 = jnp.bfloat16
NT = (((1,), (1,)), ((), ()))


def shifted(block):
    rows = block.shape[0]
    at = lax.broadcasted_iota(jnp.int32, block.shape, 0)
    down = jnp.where(at == 0, 0.0, pltpu.roll(block, 1, 0))
    up = jnp.where(at == rows - 1, 0.0, pltpu.roll(block, rows - 1, 0))
    return down, up


def core_kernel(
    heads,
    q_ref,
    g_ref,
    raw_ref,
    kw_ref,
    vw_ref,
    taps_ref,
    att_ref,
    gq_ref,
    grads_ref,
    mixed_ref,
    mixed_s,
    kv_s,
    both_s,
    stacked_s,
):
    scale = 1.0 / math.sqrt(HD)
    for c in range(CHUNKS):
        cols = slice(c * LANES, (c + 1) * LANES)
        for n in range(NBR):
            raw = raw_ref[c, :, n].reshape(NLEN, LANES).astype(F32)
            down, up = shifted(raw)
            mixed = taps_ref[0:1, cols] * down
            mixed = mixed + taps_ref[1:2, cols] * raw
            mixed = mixed + taps_ref[2:3, cols] * up
            mixed_s[n * NLEN : (n + 1) * NLEN, cols] = mixed.astype(BF16)
    mixed = mixed_s[...]
    mixed_ref[...] = mixed.T

    zeros = jnp.zeros((SPAN, HD), BF16)
    for place, weight in enumerate((kw_ref, vw_ref)):
        states = jnp.dot(mixed, weight[...], preferred_element_type=F32).astype(BF16)
        for h in range(heads):
            at = (2 * h + place) * HD
            kv_s[:, at : at + HD] = states[:, h * HD : (h + 1) * HD]

    def diag(h):
        q = q_ref[:, h * HD : (h + 1) * HD]
        g = g_ref[:, h * HD : (h + 1) * HD]
        return jnp.concatenate(
            [jnp.concatenate([q, zeros], axis=1), jnp.concatenate([zeros, g], axis=1)], axis=0
        )

    for h in range(heads):
        wide = slice(2 * h * HD, (2 * h + 2) * HD)
        both_s[h] = lax.dot_general(diag(h), kv_s[:, wide], NT, preferred_element_type=F32)
    for h in range(heads):
        scores = both_s[h, :SPAN] * scale
        grad_probs = both_s[h, SPAN:]
        expo = jnp.exp(scores - jnp.max(scores, axis=-1, keepdims=True))
        probs = expo / jnp.sum(expo, axis=-1, keepdims=True)
        inner = jnp.sum(grad_probs * probs, axis=-1, keepdims=True)
        grad_scores = scale * probs * (grad_probs - inner)
        stacked_s[h, :SPAN] = grad_scores.astype(BF16)
        stacked_s[h, SPAN:] = probs.astype(BF16)
    for h in range(heads):
        wide = slice(2 * h * HD, (2 * h + 2) * HD)
        cols = slice(h * HD, (h + 1) * HD)
        out = jnp.dot(stacked_s[h], kv_s[:, wide], preferred_element_type=F32)
        gq_ref[:, cols] = out[:SPAN, :HD].astype(BF16)
        att_ref[:, cols] = out[SPAN:, HD:].astype(BF16)
    for h in range(heads):
        cols = slice(h * HD, (h + 1) * HD)
        pair = lax.dot_general(
            stacked_s[h], diag(h), (((0,), (0,)), ((), ())), preferred_element_type=F32
        ).astype(BF16)
        grads_ref[0, :, cols] = pair[:, :HD]
        grads_ref[1, :, cols] = pair[:, HD:]


def core(queries, cotangent, raw, key_weight, value_weight, conv_kernel):
    tokens, width = queries.shape
    heads = width // HD
    spans = tokens // SPAN
    keys_here = NBR * NLEN
    keys_all = spans * keys_here
    whole = lambda shape: pl.BlockSpec(
        shape, lambda i: (0,) * len(shape), pipeline_mode=pl.Buffered(1)
    )
    span_rows = pl.BlockSpec((SPAN, width), lambda i: (i, 0))
    parts, quarter = raw.shape[1], raw.shape[3]
    blocks = pl.BlockSpec((CHUNKS, parts, NBR, quarter, LANES), lambda i: (0, 0, i, 0, 0))
    return pl.pallas_call(
        functools.partial(core_kernel, heads),
        grid=(spans,),
        in_specs=[
            span_rows,
            span_rows,
            blocks,
            whole((ENC, width)),
            whole((ENC, width)),
            whole((KW, ENC)),
        ],
        out_specs=[
            span_rows,
            span_rows,
            pl.BlockSpec((2, keys_here, width), lambda i: (0, i, 0)),
            pl.BlockSpec((ENC, keys_here), lambda i: (0, i)),
        ],
        out_shape=[
            jax.ShapeDtypeStruct((tokens, width), BF16),
            jax.ShapeDtypeStruct((tokens, width), BF16),
            jax.ShapeDtypeStruct((2, keys_all, width), BF16),
            jax.ShapeDtypeStruct((ENC, keys_all), BF16),
        ],
        scratch_shapes=[
            pltpu.VMEM((keys_here, ENC), BF16),
            pltpu.VMEM((keys_here, 2 * width), BF16),
            pltpu.VMEM((heads, 2 * SPAN, keys_here), F32),
            pltpu.VMEM((heads, 2 * SPAN, keys_here), BF16),
        ],
        compiler_params=pltpu.CompilerParams(
            dimension_semantics=("arbitrary",), vmem_limit_bytes=60 * 1024 * 1024
        ),
        cost_estimate=pl.CostEstimate(
            flops=10_000_000_000, bytes_accessed=30_000_000, transcendentals=1_200_000
        ),
    )(queries, cotangent, raw, key_weight, value_weight, conv_kernel)


def dp_peer(step):
    me = lax.axis_index("dp")
    index = step - 1

    def distance(i):
        return (2 + 3 * i + 3 * (i * (i - 1) // 2)) % 4

    z = (me // 8 + distance(index % 16 // 4)) % 4
    x = (me // 2 + distance(index % 4)) % 4
    core = (me + 1 + index // 16) % 2
    return z * 8 + x * 2 + core


def fetch_kernel(
    owners,
    parts,
    slot_ref,
    table_ref,
    states_ref,
    raw_ref,
    asked_ref,
    asked_s,
    send,
    ask_sem,
    local_sem,
    send_sem,
    recv_sem,
    y_send,
    y_recv,
    *recv,
):
    me = lax.axis_index("dp")
    y = lax.axis_index("db")
    right = lax.rem(y + 1, parts)
    left = lax.rem(y + parts - 1, parts)
    requests = raw_ref.shape[2]
    half = requests // 2
    capacity = 2
    others = owners - 1

    barrier = pltpu.get_barrier_semaphore()

    def greet(step, carry):
        pl.semaphore_signal(barrier, inc=1, device_id={"dp": dp_peer(step)})
        return carry

    lax.fori_loop(1, owners, greet, 0)
    for side in (left, right):
        pl.semaphore_signal(barrier, inc=1, device_id={"db": side})
    pl.semaphore_wait(barrier, others + 2)

    def ask(step, carry):
        peer = dp_peer(step)
        pltpu.make_async_remote_copy(
            src_ref=table_ref.at[peer],
            dst_ref=asked_ref.at[me],
            send_sem=ask_sem.at[0],
            recv_sem=ask_sem.at[1],
            device_id={"dp": peer},
        ).start()
        return carry

    lax.fori_loop(1, owners, ask, 0)
    asked_ref[me] = table_ref[me]
    most = asked_ref.at[pl.ds(0, others)]
    pltpu.make_async_copy(most, most, ask_sem.at[1]).wait()
    pltpu.make_async_copy(asked_ref, asked_s, local_sem).start()
    pltpu.make_async_copy(asked_ref, asked_s, local_sem).wait()

    def replies(c):
        cols = slice(c * LANES, (c + 1) * LANES)

        def reply(step, carry):
            peer = dp_peer(step)
            for k in range(capacity):
                row = jnp.maximum(asked_s[peer, 0, k], 0)
                send[c, capacity * peer + k] = states_ref[row, :, cols]
            pltpu.make_async_remote_copy(
                src_ref=send.at[c, pl.ds(capacity * peer, capacity)],
                dst_ref=recv[c].at[pl.ds(capacity * me, capacity)],
                send_sem=send_sem.at[c],
                recv_sem=recv_sem.at[c],
                device_id={"dp": peer},
            ).start()
            return carry

        lax.fori_loop(1, owners, reply, 0)
        for k in range(capacity):
            row = jnp.maximum(asked_s[me, 0, k], 0)
            recv[c][capacity * me + k] = states_ref[row, :, cols]

    ahead = 3
    for c in range(ahead):
        replies(c)

    def along_y(kind, c, part, rows, side):
        block = raw_ref.at[c, part, rows]
        return pltpu.make_async_remote_copy(
            src_ref=block,
            dst_ref=block,
            send_sem=y_send.at[kind, c],
            recv_sem=y_recv.at[kind, c],
            device_id={"db": side},
        )

    everything, low, high = pl.ds(0, requests), pl.ds(0, half), pl.ds(half, requests - half)

    def arrivals(kind, c):
        far = lax.rem(y + 2, parts)
        part, rows = ((left, everything), (right, everything), (far, low), (far, high))[kind]
        return along_y(kind, c, part, rows, right)

    for c in range(CHUNKS + 1):
        if c + ahead < CHUNKS:
            replies(c + ahead)
        if c < CHUNKS:
            most = recv[c].at[pl.ds(0, capacity * others)]
            pltpu.make_async_copy(most, most, recv_sem.at[c]).wait()
            for p in range(requests):
                raw_ref[c, y, p] = recv[c][slot_ref[p]]
            along_y(0, c, y, everything, right).start()
            along_y(1, c, y, everything, left).start()
        if c >= 1:
            arrivals(0, c - 1).wait_recv()
            along_y(2, c - 1, left, low, right).start()
            arrivals(1, c - 1).wait_recv()
            along_y(3, c - 1, right, high, left).start()
    for c in range(CHUNKS):
        arrivals(2, c).wait_recv()
        arrivals(3, c).wait_recv()
        along_y(0, c, y, everything, right).wait_send()
        along_y(1, c, y, everything, left).wait_send()
        along_y(2, c, left, low, right).wait_send()
        along_y(3, c, right, high, left).wait_send()
        most = send.at[c, pl.ds(0, capacity * others)]
        pltpu.make_async_copy(most, most, send_sem.at[c]).wait()
    most = table_ref.at[pl.ds(0, others)]
    pltpu.make_async_copy(most, most, ask_sem.at[0]).wait()


def fetch(slots, table, states):
    owners = table.shape[0]
    parts = lax.axis_size("db")
    requests = slots.shape[0]
    quarter = states.shape[1]
    vmem = pl.BlockSpec(memory_space=pltpu.VMEM)
    dma = pltpu.SemaphoreType.DMA
    return pl.pallas_call(
        functools.partial(fetch_kernel, owners, parts),
        in_specs=[pl.BlockSpec(memory_space=pltpu.SMEM), vmem, vmem],
        out_specs=[vmem, vmem],
        out_shape=[
            jax.ShapeDtypeStruct((CHUNKS, parts, requests, quarter, LANES), BF16),
            jax.ShapeDtypeStruct(table.shape, jnp.int32),
        ],
        scratch_shapes=[
            pltpu.SMEM(table.shape, jnp.int32),
            pltpu.VMEM((CHUNKS, 2 * owners, quarter, LANES), BF16),
            dma((2,)),
            dma,
            dma((CHUNKS,)),
            dma((CHUNKS,)),
            dma((4, CHUNKS)),
            dma((4, CHUNKS)),
        ]
        + [pltpu.VMEM((2 * owners, quarter, LANES), BF16)] * CHUNKS,
        compiler_params=pltpu.CompilerParams(
            collective_id=0, has_side_effects=True, vmem_limit_bytes=60 * 1024 * 1024
        ),
        cost_estimate=pl.CostEstimate(flops=0, bytes_accessed=16_000_000, transcendentals=0),
    )(slots, table, states)


def tail_kernel(
    owners,
    parts,
    req_ref,
    conv_ref,
    grads_hbm,
    mixed_hbm,
    raw_hbm,
    kw_hbm,
    vw_hbm,
    back_ref,
    wsum_ref,
    tsum_ref,
    grads,
    mixed_t,
    raw_ref,
    kw_ref,
    vw_ref,
    part_ref,
    w_ref,
    taps_acc,
    load_sem,
    grads_sem,
    from_far,
    onward,
    from_near,
    send,
    sibling_w,
    pair_w,
    first_in,
    first_sum,
    second_in,
    taps_in,
    taps_now,
    far_send,
    far_recv,
    near_send,
    near_recv,
    back_send,
    back_recv,
    pair_send,
    pair_recv,
    axis_send,
    axis_recv,
    taps_send,
    taps_recv,
    *mine,
):
    me = lax.axis_index("dp")
    y = lax.axis_index("db")
    z, x, core = me // 8, lax.rem(me // 2, 4), lax.rem(me, 2)
    sibling = me + 1 - 2 * core
    right = lax.rem(y + 1, parts)
    left = lax.rem(y + parts - 1, parts)
    far = lax.rem(y + 2, parts)
    requests = part_ref.shape[2]
    keys_here = NBR * NLEN
    spans = requests // NBR

    def load(index):
        pair = ((kw_hbm, kw_ref), (vw_hbm, vw_ref), (raw_hbm, raw_ref), (mixed_hbm, mixed_t))[index]
        return pltpu.make_async_copy(*pair, load_sem.at[index])

    def load_grads(span):
        rows = pl.ds(pl.multiple_of(span * keys_here, keys_here), keys_here)
        return pltpu.make_async_copy(
            grads_hbm.at[:, rows], grads.at[:, rows], grads_sem.at[span]
        )

    load(0).start()
    load(1).start()
    for span in range(spans):
        load_grads(span).start()
    load(2).start()
    load(3).start()
    taps_acc[...] = jnp.zeros_like(taps_acc)
    half = requests // 2
    capacity = 2
    others = owners - 1
    low, high = pl.ds(0, half), pl.ds(half, requests - half)

    def x_peer(step):
        return z * 8 + lax.rem(x + step, 4) * 2 + core

    def z_peer(step):
        return lax.rem(z + step, 4) * 8 + x * 2 + core

    barrier = pltpu.get_barrier_semaphore()

    def greet(step, carry):
        pl.semaphore_signal(barrier, inc=1, device_id={"dp": dp_peer(step)})
        return carry

    lax.fori_loop(1, owners, greet, 0)
    for other in range(1, parts):
        pl.semaphore_signal(barrier, inc=1, device_id={"db": lax.rem(y + other, parts)})
    pl.semaphore_wait(barrier, others + parts - 1)

    def remote(src, dst, send_sem, recv_sem, where):
        return pltpu.make_async_remote_copy(
            src_ref=src, dst_ref=dst, send_sem=send_sem, recv_sem=recv_sem, device_id=where
        )

    def grad_columns(chunks):
        cols = slice(chunks[0] * LANES, (chunks[-1] + 1) * LANES)

        def one(span, carry):
            rows = pl.ds(pl.multiple_of(span * keys_here, keys_here), keys_here)
            whole = lax.dot_general(
                grads[0, rows], kw_ref[cols], NT, preferred_element_type=F32
            ) + lax.dot_general(grads[1, rows], vw_ref[cols], NT, preferred_element_type=F32)
            for i, c in enumerate(chunks):
                lanes = slice(c * LANES, (c + 1) * LANES)
                for n in range(NBR):
                    gm = whole[n * NLEN : (n + 1) * NLEN, i * LANES : (i + 1) * LANES]
                    gm_down, gm_up = shifted(gm)
                    grad = conv_ref[0:1, lanes] * gm_up
                    grad = grad + conv_ref[1:2, lanes] * gm
                    grad = grad + conv_ref[2:3, lanes] * gm_down
                    part_ref[c, :, span * NBR + n] = grad.astype(BF16).reshape(parts, -1, LANES)
                    raw = raw_ref[c, :, span * NBR + n].reshape(NLEN, LANES).astype(F32)
                    for w, other in enumerate((gm_up, gm, gm_down)):
                        taps_acc[w, :, lanes] += jnp.sum(
                            (raw * other).reshape(NLEN // 8, 8, LANES), axis=0
                        )
            return carry

        lax.fori_loop(0, spans, one, 0)

    def far_copy(side, c):
        rows, to = ((low, right), (high, left))[side]
        return remote(
            part_ref.at[c, far, rows],
            from_far.at[side, c],
            far_send.at[side, c],
            far_recv.at[side, c],
            {"db": to},
        )

    def near_copy(side, c):
        return remote(
            onward.at[side, c],
            from_near.at[side, c],
            near_send.at[side, c],
            near_recv.at[side, c],
            {"db": (right, left)[side]},
        )

    def forward(c):
        far_copy(0, c).wait_recv()
        added = part_ref[c, right, 0:half].astype(F32) + from_far[0, c].astype(F32)
        onward[0, c, 0:half] = added.astype(BF16)
        onward[0, c, half:requests] = part_ref[c, right, half:requests]
        near_copy(0, c).start()
        far_copy(1, c).wait_recv()
        added = part_ref[c, left, half:requests].astype(F32) + from_far[1, c].astype(F32)
        onward[1, c, half:requests] = added.astype(BF16)
        onward[1, c, 0:half] = part_ref[c, left, 0:half]
        near_copy(1, c).start()

    def give_back(c):
        near_copy(0, c).wait_recv()
        near_copy(1, c).wait_recv()
        total = part_ref[c, y].astype(F32) + from_near[0, c].astype(F32)
        mine[c][...] = (total + from_near[1, c].astype(F32)).astype(BF16)

        def one(step, carry):
            peer = dp_peer(step)
            for k in range(capacity):
                send[c, capacity * peer + k] = mine[c][req_ref[capacity * peer + k]]
            remote(
                send.at[c, pl.ds(capacity * peer, capacity)],
                back_ref.at[c, pl.ds(capacity * me, capacity)],
                back_send.at[c],
                back_recv.at[c],
                {"dp": peer},
            ).start()
            return carry

        lax.fori_loop(1, owners, one, 0)
        for k in range(capacity):
            back_ref[c, capacity * me + k] = mine[c][req_ref[capacity * me + k]]

    first_at, second_at = (x, z), (z, x)
    first_peer, second_peer = (x_peer, z_peer), (z_peer, x_peer)
    order = [(d, h) for d in (1, 2, 3, 0) for h in (0, 1)]

    def group(h, step):
        return h * 4 + lax.rem(first_at[h] + step, 4)

    def pair_copy(d, h):
        g = group(h, d)
        return remote(
            w_ref.at[1 - core, g],
            sibling_w.at[g],
            pair_send.at[0, h * 4 + d],
            pair_recv.at[0, h * 4 + d],
            {"dp": sibling},
        )

    def weight_terms(which, d):
        def columns(h):
            return grads[which, :, pl.ds(pl.multiple_of(group(h, d) * HD, HD), HD)]

        both = jnp.concatenate([columns(0), columns(1)], axis=1)
        term = jnp.dot(mixed_t[...], both, preferred_element_type=F32)
        for h in (0, 1):
            block = term[:, h * HD : (h + 1) * HD].astype(BF16)
            w_ref[which, group(h, d)] = block.reshape(4, -1, HD)

    def first_copy(d, h):
        return remote(
            pair_w.at[group(h, d)],
            first_in.at[h, d - 1],
            axis_send.at[0, h * 3 + d - 1],
            axis_recv.at[0, h * 3 + d - 1],
            {"dp": first_peer[h](d)},
        )

    def far_half(side, h):
        at = (0, h * 3 + 1) if side == 0 else (4, h * 3)
        return remote(
            pair_w.at[group(h, 2), pl.ds(2 * side, 2)],
            first_in.at[h, 1, pl.ds(2 * side, 2)],
            axis_send.at[at],
            axis_recv.at[at],
            {"dp": first_peer[h](1 + 2 * side)},
        )

    def relay(side, h, back):
        at = (3, h * 3 + 1) if side == 0 else (4, h * 3 + 1)
        block = wsum_ref.at[core, group(h, back), pl.ds(2 * side, 2)]
        return remote(
            block,
            block,
            axis_send.at[at],
            axis_recv.at[at],
            {"dp": first_peer[h](1 + 2 * side)},
        )

    def second_copy(d, h):
        return remote(
            first_sum.at[h, lax.rem(second_at[h] + d, 4)],
            second_in.at[h, d - 1],
            axis_send.at[1, h * 3 + d - 1],
            axis_recv.at[1, h * 3 + d - 1],
            {"dp": second_peer[h](d)},
        )

    def second_gather(d, h, back):
        block = wsum_ref.at[core, group(h, 0), lax.rem(second_at[h] + back, 4)]
        return remote(
            block,
            block,
            axis_send.at[2, h * 3 + d - 1],
            axis_recv.at[2, h * 3 + d - 1],
            {"dp": second_peer[h](d)},
        )

    def first_gather(d, h, back):
        block = wsum_ref.at[core, group(h, back)]
        return remote(
            block,
            block,
            axis_send.at[3, h * 3 + d - 1],
            axis_recv.at[3, h * 3 + d - 1],
            {"dp": first_peer[h](d)},
        )

    def pair_gather(d, h, which):
        block = wsum_ref.at[which, group(h, 4 - d)]
        return remote(
            block,
            block,
            pair_send.at[1, h * 4 + d],
            pair_recv.at[1, h * 4 + d],
            {"dp": sibling},
        )

    def pair_sum(d, h):
        pair_copy(d, h).wait_recv()
        g = group(h, d)
        total = w_ref[core, g].astype(F32) + sibling_w[g].astype(F32)
        if d in (1, 3):
            side = d // 2
            far_half(side, h).wait_recv()
            added = total[2 * side : 2 * side + 2]
            added = added + first_in[h, 1, 2 * side : 2 * side + 2].astype(F32)
            pair_w[g, 2 * side : 2 * side + 2] = added.astype(BF16)
            pair_w[g, 2 - 2 * side : 4 - 2 * side] = total[2 - 2 * side : 4 - 2 * side].astype(BF16)
            first_copy(d, h).start()
        else:
            pair_w[g] = total.astype(BF16)
            if d:
                far_half(0, h).start()
                far_half(1, h).start()

    def sum_first(h):
        for d in (1, 3):
            first_copy(d, h).wait_recv()
        total = pair_w[group(h, 0)].astype(F32)
        for d in (1, 3):
            total = total + first_in[h, d - 1].astype(F32)
        first_sum[h] = total.astype(BF16)
        for d in (1, 2, 3):
            second_copy(d, h).start()

    def sum_second(h):
        for d in (1, 2, 3):
            second_copy(d, h).wait_recv()
        total = first_sum[h, second_at[h]].astype(F32)
        for d in (1, 2, 3):
            total = total + second_in[h, d - 1].astype(F32)
        wsum_ref[core, group(h, 0), second_at[h]] = total.astype(BF16)
        for d in (1, 2, 3):
            second_gather(d, h, 0).start()

    def gather_first(h):
        for d in (1, 2, 3):
            second_gather(d, h, 4 - d).wait_recv()
        for d in (1, 3):
            first_gather(d, h, 0).start()
        pair_gather(0, h, core).start()

    def gather_relay(h):
        for side, d in ((0, 1), (1, 3)):
            first_gather(d, h, 4 - d).wait_recv()
            relay(side, h, 4 - d).start()
            pair_gather(d, h, core).start()

    def gather_far(h):
        relay(0, h, 2).wait_recv()
        relay(1, h, 2).wait_recv()
        pair_gather(2, h, core).start()

    stages = (
        (2, core, lambda step: {"dp": sibling}),
        (4, x, lambda step: {"dp": x_peer(step)}),
        (4, z, lambda step: {"dp": z_peer(step)}),
        (parts, y, lambda step: {"db": lax.rem(y + step, parts)}),
    )

    def taps_copy(stage, d):
        count, at, peer = stages[stage]
        return remote(
            taps_now.at[stage],
            taps_in.at[stage, at],
            taps_send.at[stage, d - 1],
            taps_recv.at[stage, d - 1],
            peer(d),
        )

    def taps_start(stage, value):
        count, at, peer = stages[stage]
        taps_now[stage] = value
        taps_in[stage, at] = value
        for d in range(1, count):
            taps_copy(stage, d).start()

    def taps_end(stage):
        count = stages[stage][0]
        for d in range(1, count):
            taps_copy(stage, d).wait_recv()
        total = taps_in[stage, 0]
        for other in range(1, count):
            total = total + taps_in[stage, other]
        return total

    def start_far(chunks):
        for c in chunks:
            far_copy(0, c).start()
            far_copy(1, c).start()

    def weight_step(d):
        weight_terms(1 - core, d)
        pair_copy(d, 0).start()
        pair_copy(d, 1).start()
        weight_terms(core, d)

    def pair_sums(d):
        pair_sum(d, 0)
        pair_sum(d, 1)

    for span in range(spans):
        load_grads(span).wait()
    for index in (0, 1, 2):
        load(index).wait()
    grad_columns((0, 1))
    start_far((0, 1))
    load(3).wait()
    weight_step(2)
    forward(0)
    forward(1)
    weight_step(1)
    pair_sums(2)
    give_back(0)
    weight_step(3)
    pair_sums(1)
    give_back(1)
    weight_step(0)
    pair_sums(3)
    pair_sums(0)
    grad_columns((2, 3))
    start_far((2, 3))
    grad_columns((4, 5))
    start_far((4, 5))
    forward(2)
    forward(3)
    sum_first(0)
    sum_first(1)
    grad_columns((6,))
    start_far((6,))
    give_back(2)
    forward(4)
    forward(5)
    sum_second(0)
    sum_second(1)
    taps_start(0, jnp.sum(taps_acc[...], axis=1))
    give_back(3)
    forward(6)
    gather_first(0)
    gather_first(1)
    taps_start(1, taps_end(0))
    give_back(4)
    taps_start(2, taps_end(1))
    give_back(5)
    gather_relay(0)
    gather_relay(1)
    taps_start(3, taps_end(2))
    give_back(6)
    gather_far(0)
    gather_far(1)
    tsum_ref[...] = taps_end(3)

    for d, h in order:
        pair_gather(d, h, 1 - core).wait_recv()
        pair_gather(d, h, core).wait_send()
        pair_copy(d, h).wait_send()
        if d:
            second_copy(d, h).wait_send()
            second_gather(d, h, 0).wait_send()
        if d in (1, 3):
            first_copy(d, h).wait_send()
            first_gather(d, h, 0).wait_send()
            far_half(d // 2, h).wait_send()
            relay(d // 2, h, 4 - d).wait_send()
    for stage in range(4):
        for d in range(1, stages[stage][0]):
            taps_copy(stage, d).wait_send()
    for c in range(CHUNKS):
        for side in (0, 1):
            far_copy(side, c).wait_send()
            near_copy(side, c).wait_send()
        most = send.at[c, pl.ds(0, capacity * others)]
        pltpu.make_async_copy(most, most, back_send.at[c]).wait()
        most = back_ref.at[c, pl.ds(0, capacity * others)]
        pltpu.make_async_copy(most, most, back_recv.at[c]).wait()


def tail(wanted, conv_kernel, grads, mixed, raw, key_weight, value_weight):
    owners = lax.axis_size("dp")
    parts = lax.axis_size("db")
    requests, quarter = raw.shape[2], raw.shape[3]
    slots = wanted.shape[0]
    vmem = pl.BlockSpec(memory_space=pltpu.VMEM)
    anywhere = pl.BlockSpec(memory_space=pl.ANY)
    dma = pltpu.SemaphoreType.DMA
    heads = key_weight.shape[1] // HD
    rows = ENC // 4
    weights = (2, heads, 4, rows, HD)
    taps = (8, ENC)
    both = (2, CHUNKS, requests, quarter, LANES)
    return pl.pallas_call(
        functools.partial(tail_kernel, owners, parts),
        in_specs=[pl.BlockSpec(memory_space=pltpu.SMEM), vmem] + [anywhere] * 5,
        out_specs=[vmem, vmem, vmem],
        out_shape=[
            jax.ShapeDtypeStruct((CHUNKS, slots, quarter, LANES), BF16),
            jax.ShapeDtypeStruct(weights, BF16),
            jax.ShapeDtypeStruct(taps, F32),
        ],
        scratch_shapes=[
            pltpu.VMEM(grads.shape, BF16),
            pltpu.VMEM(mixed.shape, BF16),
            pltpu.VMEM(raw.shape, BF16),
            pltpu.VMEM(key_weight.shape, BF16),
            pltpu.VMEM(value_weight.shape, BF16),
            pltpu.VMEM(raw.shape, BF16),
            pltpu.VMEM(weights, BF16),
            pltpu.VMEM((8, 8, ENC), F32),
            dma((4,)),
            dma((requests // NBR,)),
            pltpu.VMEM((2, CHUNKS, requests // 2, quarter, LANES), BF16),
            pltpu.VMEM(both, BF16),
            pltpu.VMEM(both, BF16),
            pltpu.VMEM((CHUNKS, slots, quarter, LANES), BF16),
            pltpu.VMEM((heads, 4, rows, HD), BF16),
            pltpu.VMEM((heads, 4, rows, HD), BF16),
            pltpu.VMEM((2, 3, 4, rows, HD), BF16),
            pltpu.VMEM((2, 4, rows, HD), BF16),
            pltpu.VMEM((2, 3, rows, HD), BF16),
            pltpu.VMEM((4, 4) + taps, F32),
            pltpu.VMEM((4,) + taps, F32),
            dma((2, CHUNKS)),
            dma((2, CHUNKS)),
            dma((2, CHUNKS)),
            dma((2, CHUNKS)),
            dma((CHUNKS,)),
            dma((CHUNKS,)),
            dma((2, 8)),
            dma((2, 8)),
            dma((5, 6)),
            dma((5, 6)),
            dma((4, 3)),
            dma((4, 3)),
        ]
        + [pltpu.VMEM((requests, quarter, LANES), BF16)] * CHUNKS,
        compiler_params=pltpu.CompilerParams(
            collective_id=1, has_side_effects=True, vmem_limit_bytes=60 * 1024 * 1024
        ),
        cost_estimate=pl.CostEstimate(
            flops=17_000_000_000, bytes_accessed=30_000_000, transcendentals=0
        ),
    )(wanted, conv_kernel, grads, mixed, raw, key_weight, value_weight)


def spread_kernel(
    asked_ref, back_ref, w_ref, taps_ref, states_ref, gkw_ref, gvw_ref, gt_ref, used, count
):
    gkw_ref[...] = w_ref[0, 0].astype(F32)
    gvw_ref[...] = w_ref[1, 0].astype(F32)
    step = pl.program_id(0)

    @pl.when(step == 0)
    def _():
        gt_ref[...] = taps_ref[0:KW]
        count[0] = 0

        def note(owner, carry):
            for k in (0, 1):
                row = asked_ref[owner, 0, k]

                @pl.when(row >= 0)
                def _():
                    at = count[0]
                    used[0, at] = 2 * owner + k
                    used[1, at] = row
                    count[0] = at + 1

            return carry

        lax.fori_loop(0, asked_ref.shape[0], note, 0)

    @pl.when(step < CHUNKS)
    def _():
        states_ref[...] = jnp.zeros_like(states_ref)

        def add(index, carry):
            states_ref[used[1, index]] += back_ref[0, used[0, index]].astype(F32)
            return carry

        lax.fori_loop(0, count[0], add, 0)


def spread(asked, back, weights, taps, blocks):
    heads = weights.shape[1]
    slots, quarter = back.shape[1], back.shape[2]
    last = CHUNKS - 1
    head_cols = pl.BlockSpec((ENC, HD), lambda i: (0, i))
    return pl.pallas_call(
        spread_kernel,
        grid=(max(heads, CHUNKS),),
        in_specs=[
            pl.BlockSpec(memory_space=pltpu.SMEM),
            pl.BlockSpec((1, slots, quarter, LANES), lambda i: (jnp.minimum(i, last), 0, 0, 0)),
            pl.BlockSpec((2, 1, ENC, HD), lambda i: (0, i, 0, 0)),
            pl.BlockSpec((8, ENC), lambda i: (0, 0)),
        ],
        out_specs=[
            pl.BlockSpec((blocks, quarter, LANES), lambda i: (0, 0, jnp.minimum(i, last))),
            head_cols,
            head_cols,
            pl.BlockSpec((KW, ENC), lambda i: (0, 0)),
        ],
        out_shape=[
            jax.ShapeDtypeStruct((blocks, quarter, ENC), F32),
            jax.ShapeDtypeStruct((ENC, heads * HD), F32),
            jax.ShapeDtypeStruct((ENC, heads * HD), F32),
            jax.ShapeDtypeStruct((KW, ENC), F32),
        ],
        scratch_shapes=[pltpu.SMEM((2, slots), jnp.int32), pltpu.SMEM((1,), jnp.int32)],
        compiler_params=pltpu.CompilerParams(
            dimension_semantics=("arbitrary",), vmem_limit_bytes=60 * 1024 * 1024
        ),
        cost_estimate=pl.CostEstimate(flops=0, bytes_accessed=19_000_000, transcendentals=0),
    )(asked, back, weights.reshape(2, heads, ENC, HD), taps)


def tables_kernel(owner_ref, row_ref, slot_ref, wanted_ref, table_ref, rows, taken):
    owners = table_ref.shape[0]
    requests = slot_ref.shape[0]

    def clear(owner, carry):
        taken[owner] = 0
        for k in (0, 1):
            rows[2 * owner + k] = -1
            wanted_ref[2 * owner + k] = 0
        return carry

    lax.fori_loop(0, owners, clear, 0)
    for p in range(requests):
        owner = owner_ref[p % NBR, p // NBR]
        slot = 2 * owner + jnp.minimum(taken[owner], 1)
        taken[owner] = taken[owner] + 1
        slot_ref[p] = slot
        rows[slot] = row_ref[p % NBR, p // NBR]
        wanted_ref[slot] = p
    lane = lax.broadcasted_iota(jnp.int32, (1, LANES), 1)
    for owner in range(owners):
        table_ref[owner] = jnp.where(lane == 0, rows[2 * owner], rows[2 * owner + 1])


def tables(nbr_owner, nbr_row, owners):
    requests = nbr_owner.shape[0] * NBR
    smem = pl.BlockSpec(memory_space=pltpu.SMEM)
    return pl.pallas_call(
        tables_kernel,
        in_specs=[smem, smem],
        out_specs=[smem, smem, pl.BlockSpec(memory_space=pltpu.VMEM)],
        out_shape=[
            jax.ShapeDtypeStruct((requests,), jnp.int32),
            jax.ShapeDtypeStruct((2 * owners,), jnp.int32),
            jax.ShapeDtypeStruct((owners, 1, LANES), jnp.int32),
        ],
        scratch_shapes=[pltpu.SMEM((2 * owners,), jnp.int32), pltpu.SMEM((owners,), jnp.int32)],
        compiler_params=pltpu.CompilerParams(vmem_limit_bytes=60 * 1024 * 1024),
    )(nbr_owner.T, nbr_row.T)


def shards(
    queries, cotangent, db_states, key_weight, value_weight, conv_kernel, nbr_owner, nbr_row
):
    slots, wanted, table = tables(nbr_owner, nbr_row, lax.axis_size("dp"))
    raw, asked = fetch(slots, table, db_states)
    attended, grad_query, grads, mixed = core(
        queries, cotangent, raw, key_weight, value_weight, conv_kernel
    )
    back, weight_sums, taps_sum = tail(
        wanted, conv_kernel, grads, mixed, raw, key_weight, value_weight
    )
    grad_states, grad_key_weight, grad_value_weight, grad_kernel = spread(
        asked, back, weight_sums, taps_sum, db_states.shape[0]
    )
    return (
        attended,
        grad_query,
        grad_states,
        grad_key_weight,
        grad_value_weight,
        grad_kernel,
    )


def solution(mesh):
    return jax.shard_map(
        shards,
        mesh=mesh,
        in_specs=(
            P("dp", "db"),
            P("dp", "db"),
            P("dp", "db", None),
            P(None, "db"),
            P(None, "db"),
            P(),
            P("dp", None),
            P("dp", None),
        ),
        out_specs=(
            P("dp", "db"),
            P("dp", "db"),
            P("dp", "db", None),
            P(None, "db"),
            P(None, "db"),
            P(),
        ),
        check_vma=False,
    )
```
